256 devices in a mesh: row: 8 (over x, z_hi), col: 32 (over y, z_lo, core).
Axes of the slice: x: 4, y: 4, z: 8 (z_hi: 2, z_lo: 4; z = z_hi * 4 + z_lo), core: 2. Of those that a mesh axis runs over, the one named last changes fastest.
Arguments:
- query_single: bfloat16 [1024, 384], P(('row', 'col')), may hold values from -6 to 6
- query_frames: float32 [12, 1024], P(None, 'row'), may hold values from -30 to 30, as said below
- query_chain: int32 [1024], P('row'), may hold values from 0 to 3, never falling along the last dimension, each value on 1 to 512 neighbouring positions
- key_single: bfloat16 [8192, 384], P('col', 'row'), may hold values from -32 to 32
- key_frames: float32 [12, 8192], P(None, 'col'), may hold values from -30 to 30, as said below
- key_chain: int32 [8192], P('col'), may hold values from 0 to 7, never falling along the last dimension, each value on 1 to 2048 neighbouring positions
- key_mask: int32 [8192], P('col'), may hold values 0 or 1
- pair: bfloat16 [1024, 8192, 128], P('row', 'col'), may hold values from -1000 to 1000
- w_query: bfloat16 [384, 336], replicated, may hold values from -0.3125 to 0.3125
- w_key: bfloat16 [384, 816], replicated, may hold values from -0.3125 to 0.3125
- pair_weight: bfloat16 [128, 12], replicated, may hold values from -1 to 1
- point_raw: float32 [12], replicated, may hold values from -1.5 to 1
- chain_bias: float32 [12], replicated, may hold values from -2 to 2
- out_weight: bfloat16 [2112, 384], replicated, may hold values from -0.125 to 0.125
- out_bias: float32 [384], replicated, may hold values from -2 to 2
Outputs:
- update: bfloat16 [1024, 384], P(('row', 'col'))
The draws below stay inside these ranges and needn't reach their ends.
Inputs may be any that keep to these rules, and one draw needn't show every extreme that they name: `query_frames`: rows 0 to 8 of each column are a rotation matrix in row-major order, rows 9 to 11 a translation. `key_frames`: rows 0 to 8 of each column are a rotation matrix in row-major order, rows 9 to 11 a translation.
All inputs are finite; a program needn't handle non-finite values. No bound on the sum of `key_mask` on one device may be relied on, other than what follows from the above.
Results may differ from the reference program's by a relative error of at most 0.0095.
Values may be sent and summed in bfloat16 or wider, within the bound.
No kernel may reach another device: no remote copies, remote signals or barrier semaphores. Data moves between devices by JAX's collectives and lax.ppermute only.
A program may use at most 64 MiB of HBM per device.

```python
import math
import jax
import jax.numpy as jnp
import numpy as np
from jax import lax

D = 384
H = 12
C = 16
PQ = 4
PV = 8
CZ = 128
QD = 128
QROWS = 1024
N = 8192
FEAT = 2112


def frame_table(key, count, spread):
    quat = jax.random.normal(key, (4, count), jnp.float32)
    quat = quat / jnp.sqrt(jnp.sum(quat * quat, 0, keepdims=True) + 1e-06)
    first, second, third, fourth = (quat[0], quat[1], quat[2], quat[3])
    rotation = [first * first + second * second - third * third - fourth * fourth, 2.0 * (second * third - first * fourth), 2.0 * (second * fourth + first * third), 2.0 * (second * third + first * fourth), first * first - second * second + third * third - fourth * fourth, 2.0 * (third * fourth - first * second), 2.0 * (second * fourth - first * third), 2.0 * (third * fourth + first * second), first * first - second * second - third * third + fourth * fourth]
    shift = spread * jax.random.normal(jax.random.fold_in(key, 1), (3, count), jnp.float32)
    return jnp.concatenate([jnp.stack(rotation), shift], 0)


def bias_columns(key):
    return jax.random.normal(jax.random.fold_in(key, 71), (CZ, H), jnp.float32) / math.sqrt(CZ)


def ramped_rows(noise, key):
    position = jnp.arange(D, dtype=jnp.float32) / float(D - 1)
    jitter = jax.random.uniform(jax.random.fold_in(key, 3), (D,), jnp.float32, 0.7, 1.3)
    column_scale = 0.2 * jnp.exp(3.0 * position) * jitter
    return noise * column_scale[None, :]


def draw_key_single(key, part):
    key = jax.random.fold_in(key, 17)
    noise = jnp.clip(jax.random.normal(key, (N, D), jnp.float32), -6.0, 6.0)
    return ramped_rows(noise, key).astype(jnp.bfloat16)


def draw_query_frames(key, part):
    key = jax.random.fold_in(key, 11)
    return frame_table(key, QROWS, 3.0)


def draw_key_frames(key, part):
    key = jax.random.fold_in(key, 13)
    return frame_table(key, N, 3.0)


def draw_pair_weight(key, part):
    columns = bias_columns(key)
    return columns.astype(jnp.bfloat16)


def draw_pair(key, part):
    key = jax.random.fold_in(key, 5)
    tile = jax.random.normal(key, (QROWS, N, CZ), jnp.float32)
    return tile.astype(jnp.bfloat16)


def set_ends(drawn, stream_key, smallest, top_value):
    longest = drawn.shape.index(max(drawn.shape))
    spots = []
    for shift in (0, 1):
        where = [jax.random.randint(jax.random.fold_in(stream_key, axis), (), 0, length) for axis, length in enumerate(drawn.shape)]
        where[longest] = (where[longest] + shift) % drawn.shape[longest]
        spots.append(tuple(where))
    return drawn.at[spots[0]].set(smallest).at[spots[1]].set(top_value)


def block_levels(stream_key, extent, shards, smallest, largest):
    def one(dim, shards_of):
        draws = jax.random.uniform(jax.random.fold_in(jax.random.fold_in(stream_key, 6), dim), (shards_of,), jnp.float32, smallest / len(shards), largest / len(shards))
        return jnp.repeat(jnp.exp(draws), extent[dim] // shards_of).reshape((-1,) + (1,) * (len(extent) - dim - 1))

    gain = one(*shards[0])
    for cut in shards[1:]:
        gain = gain * one(*cut)
    return gain


def length_profile(number_of, total, reach, lean):
    portions = [(1 << 20) // math.isqrt(rank ** lean) + 1 for rank in range(2, number_of + 1)]
    surplus, given = total - reach - (number_of - 1), [1] * (number_of - 1)
    while surplus > 0:
        movable = [i for i in range(number_of - 1) if given[i] < reach]
        mass, left = sum([portions[i] for i in movable]), surplus
        for i in movable:
            extra = min(reach - given[i], max(1, left * portions[i] // mass), surplus)
            given[i] = given[i] + extra
            surplus = surplus - extra
    return np.array([reach] + given)


def uneven(rng, count, total, bound, slope):
    if count == 2:
        one = jax.random.randint(rng, (), max(1, total - bound), min(bound, total - 1) + 1)
        return jnp.stack([one, total - one])
    tallies = jnp.asarray(length_profile(count, total, bound, slope), jnp.int32)
    couples = (count - 1) // 2
    source_of, taker = tallies[1:1 + 2 * couples:2], tallies[2:2 + 2 * couples:2]
    margin = jnp.minimum(source_of - 1, bound - taker)
    moved = jax.random.randint(jax.random.fold_in(rng, 1), (couples,), 0, 1 << 20) % (margin + 1)
    tallies = tallies.at[1:1 + 2 * couples:2].set(source_of - moved).at[2:2 + 2 * couples:2].set(taker + moved)
    return tallies[jax.random.permutation(jax.random.fold_in(rng, 2), count)]


def normal_values(stream_key, extent, scale, most, cuts=(), kind=jnp.bfloat16):
    drawn = jax.random.normal(stream_key, extent, jnp.float32) * scale
    if len(cuts) > 0:
        drawn = block_levels(stream_key, extent, cuts, -0.22, 0.18) * drawn
    return jnp.clip(drawn, min=-most, max=most).astype(kind)


def setup_inputs(seed: int = 0) -> dict:
    arg_keys = jax.random.split(jax.random.key(seed), 16)
    query_single = normal_values(arg_keys[0], (QROWS, D), 1.0, 6.0, ((0, 256),))
    query_frames = draw_query_frames(jax.random.fold_in(arg_keys[15], 71), 0)
    query_chain = jnp.searchsorted(jnp.cumsum(uneven(arg_keys[2], 4, QROWS, QROWS // 2, 2)), jnp.arange(QROWS), side="right").astype(jnp.int32)
    key_single = draw_key_single(jax.random.fold_in(arg_keys[15], 71), 0)
    key_frames = draw_key_frames(jax.random.fold_in(arg_keys[15], 71), 0)
    key_chain = jnp.searchsorted(jnp.cumsum(uneven(arg_keys[5], 8, N, N // 4, 2)), jnp.arange(N), side="right").astype(jnp.int32)
    key_mask = set_ends((jax.random.randint(arg_keys[6], (N,), 0, 8) < 7).astype(jnp.int32), jax.random.fold_in(arg_keys[6], 1), 0, 1)
    pair = draw_pair(jax.random.fold_in(arg_keys[15], 71), 0)
    w_query = normal_values(arg_keys[8], (D, H * C + 3 * H * PQ), D ** -0.5, 0.3125)
    w_key = normal_values(arg_keys[9], (D, 2 * H * C + 3 * H * PQ + 3 * H * PV), D ** -0.5, 0.3125)
    pair_weight = draw_pair_weight(jax.random.fold_in(arg_keys[15], 71), 0)
    point_raw = jnp.clip(jax.random.uniform(arg_keys[11], (H,), jnp.float32, -1.5, 1.0), -1.5, 1.0)
    chain_bias = jnp.clip(jax.random.uniform(arg_keys[12], (H,), jnp.float32, -2.0, 2.0), -2.0, 2.0)
    out_weight = normal_values(arg_keys[13], (FEAT, D), FEAT ** -0.5, 0.125)
    out_bias = normal_values(arg_keys[14], (D,), 0.3, 2.0, (), jnp.float32)
    return dict(query_single=query_single, query_frames=query_frames, query_chain=query_chain, key_single=key_single, key_frames=key_frames, key_chain=key_chain, key_mask=key_mask, pair=pair, w_query=w_query, w_key=w_key, pair_weight=pair_weight, point_raw=point_raw, chain_bias=chain_bias, out_weight=out_weight, out_bias=out_bias)


HIGH = lax.Precision.HIGHEST

def to_global(local, frames):
    count = local.shape[0]
    points = local.reshape(count, -1, 3)
    rotation = frames[:9].T.reshape(count, 3, 3)
    moved = jnp.einsum('nxy,nay->nax', rotation, points, precision=HIGH)
    return (moved + frames[9:].T[:, None, :]).reshape(count, -1)

def logits_of(queries, query_points, query_chain, keys, key_points, key_chain, pair_tile, pair_weight, point_raw, chain_bias):
    rows = queries.shape[0]
    cols = keys.shape[0]
    dots = jnp.einsum('mhc,nhc->hmn', queries.astype(jnp.float32).reshape(rows, H, C), keys.astype(jnp.float32).reshape(cols, H, C), precision=HIGH)
    qpts = query_points.reshape(rows, H, 3 * PQ)
    kpts = key_points.reshape(cols, H, 3 * PQ)
    cross = jnp.einsum('mhe,nhe->hmn', qpts, kpts, precision=HIGH)
    dist = lax.optimization_barrier(jnp.sum(qpts * qpts, 2)).T[:, :, None] + lax.optimization_barrier(jnp.sum(kpts * kpts, 2)).T[:, None, :] - 2.0 * cross
    bias = jnp.einsum('mnc,ch->hmn', pair_tile.astype(jnp.float32), pair_weight.astype(jnp.float32), precision=HIGH)
    same = (query_chain[:, None] == key_chain[None, :]).astype(jnp.float32)
    gamma = jax.nn.softplus(point_raw)
    total = dots * (1.0 / math.sqrt(C)) + bias + chain_bias[:, None, None] * same[None] - 0.5 * math.sqrt(2.0 / (9.0 * PQ)) * gamma[:, None, None] * dist
    return math.sqrt(1.0 / 3.0) * total

def weigh(logits, peak, keep, values, value_points, pair_tile):
    rows = logits.shape[1]
    cols = logits.shape[2]
    expd = jnp.where(keep[None, None, :], jnp.exp(logits - peak.T[:, :, None]), 0.0)
    total = lax.optimization_barrier(jnp.sum(expd, 2)).T
    weights = expd.astype(jnp.bfloat16).astype(jnp.float32)
    mixed = jnp.einsum('hmn,nhc->mhc', weights, values.astype(jnp.float32).reshape(cols, H, C), precision=HIGH).reshape(rows, -1)
    points = jnp.einsum('hmn,nhe->mhe', weights, value_points.astype(jnp.float32).reshape(cols, H, 3 * PV), precision=HIGH).reshape(rows, -1)
    paired = jnp.einsum('hmn,mnc->mhc', weights, pair_tile.astype(jnp.float32), precision=HIGH).reshape(rows, -1)
    return (total, mixed, points, paired)

def finish(total, mixed, points, paired, frames, out_weight, out_bias):
    rows = total.shape[0]
    scale = 1.0 / total
    mixed = (mixed.reshape(rows, H, C) * scale[:, :, None]).reshape(rows, -1)
    spots = points.reshape(rows, H, 3 * PV) * scale[:, :, None]
    spots = spots.reshape(rows, H * PV, 3) - frames[9:].T[:, None, :]
    rotation = frames[:9].T.reshape(rows, 3, 3)
    local = jnp.einsum('nyx,nay->nax', rotation, spots, precision=HIGH)
    lengths = jnp.sqrt(lax.optimization_barrier(jnp.sum(local * local, 2)) + 1.0)
    paired = (paired.reshape(rows, H, CZ) * scale[:, :, None]).reshape(rows, -1)
    features = jnp.concatenate([mixed, local.reshape(rows, -1), lengths, paired], 1).astype(jnp.bfloat16)
    return (jnp.dot(features, out_weight, preferred_element_type=jnp.float32) + out_bias).astype(jnp.bfloat16)

def reference(query_single, query_frames, query_chain, key_single, key_frames, key_chain, key_mask, pair, w_query, w_key, pair_weight, point_raw, chain_bias, out_weight, out_bias):
    key_proj = jnp.dot(key_single, w_key, preferred_element_type=jnp.float32)
    keys = key_proj[:, :H * C].astype(jnp.bfloat16)
    values = key_proj[:, H * C:2 * H * C].astype(jnp.bfloat16)
    key_points = to_global(key_proj[:, 2 * H * C:2 * H * C + 3 * H * PQ], key_frames)
    value_points = to_global(key_proj[:, 2 * H * C + 3 * H * PQ:], key_frames).astype(jnp.bfloat16)
    query_proj = jnp.dot(query_single, w_query, preferred_element_type=jnp.float32)
    queries = query_proj[:, :H * C].astype(jnp.bfloat16)
    query_points = to_global(query_proj[:, H * C:], query_frames)
    keep = key_mask == 1

    def one_block(block):
        start = (block * QD).astype(jnp.int32)
        q_rows = lax.dynamic_slice_in_dim(queries, start, QD, 0)
        q_pts = lax.dynamic_slice_in_dim(query_points, start, QD, 0)
        q_chain = lax.dynamic_slice_in_dim(query_chain, start, QD, 0)
        q_frames = lax.dynamic_slice_in_dim(query_frames, start, QD, 1)
        tile = lax.dynamic_slice_in_dim(pair, start, QD, 0)
        logits = logits_of(q_rows, q_pts, q_chain, keys, key_points, key_chain, tile, pair_weight, point_raw, chain_bias)
        peak = lax.optimization_barrier(jnp.max(jnp.where(keep[None, None, :], logits, -1e+30), 2)).T
        total, mixed, points, paired = weigh(logits, peak, keep, values, value_points, tile)
        return finish(total, mixed, points, paired, q_frames, out_weight, out_bias)
    blocks = lax.map(one_block, jnp.arange(QROWS // QD, dtype=jnp.int32))
    return blocks.reshape(QROWS, D)
```

```python
import math

import jax
import jax.numpy as jnp
import numpy as np
from jax import lax
from jax.experimental import pallas as pl
from jax.experimental.pallas import tpu as pltpu
from jax.sharding import PartitionSpec as P

H = 12
C = 16
PQ = 4
PV = 8
CZ = 128
HP = 16
KD = 768
GL = 512
QB = 16
FAR = -1e30
F32 = jnp.float32
BF16 = jnp.bfloat16
NT = (((1,), (1,)), ((), ()))
NN = (((1,), (0,)), ((), ()))


def lane_heads():
    head = np.full((GL,), -1)
    for row in range(3):
        head[128 * row : 128 * row + 96] = np.arange(96) // PV
        head[128 * row + 96 : 128 * row + 128] = (np.arange(32) + 32 * row) // C
    head[384:480] = (np.arange(96) + 96) // C
    plain = head.copy()
    head[480:492] = np.arange(H)
    head[492:504] = np.arange(H)
    return plain, head


def depth_mask():
    column = np.arange(KD)
    head = np.full((KD,), -1)
    head[:192] = column[:192] // C
    head[192:624] = ((column[192:624] - 192) % 48) // PQ
    head[624:720] = (column[624:720] - 624) % HP
    mask = (head[None, :] == np.arange(HP)[:, None]).astype(np.float32)
    mask[:, 744] = 1.0
    mask[H:] = 0.0
    return mask


def split(x):
    hi = x.astype(BF16).astype(F32)
    return hi, x - hi


def split3(x):
    hi, rest = split(x)
    mid, rest = split(rest)
    return hi, mid, rest.astype(BF16).astype(F32)


def column_of(row, rows, per):
    shape = (rows, H)
    index = lax.broadcasted_iota(jnp.int32, shape, 0)
    lane = lax.broadcasted_iota(jnp.int32, shape, 1)
    hit = (index >= lane * per) & (index < lane * per + per)
    return jnp.sum(jnp.where(hit, row, 0.0), 1, keepdims=True)


def rotate(points, frames):
    return [
        frames[3 * x : 3 * x + 1] * points[0]
        + frames[3 * x + 1 : 3 * x + 2] * points[1]
        + frames[3 * x + 2 : 3 * x + 3] * points[2]
        + frames[9 + x : 10 + x]
        for x in range(3)
    ]


def take(ref, start, count, stride):
    return jnp.concatenate(
        [ref.at[tile][pl.ds(start, count, stride=stride), :] for tile in range(ref.shape[0])], 1
    )


def put(ref, start, value):
    for tile in range(ref.shape[0]):
        ref[tile, start : start + value.shape[0], :] = value[:, 128 * tile : 128 * tile + 128]


def prepare(
    ks_ref, wk_ref, kf_ref, kc_ref, km_ref, qs_ref, wq_ref, qf_ref, qc_ref, pw_ref, raw_ref, cb_ref,
    dm_ref, kp_s, kpt_s, qp_s, qpt_s, nk_s, nq_s, pw_s, kt_s, vt_s, qft_s, qf_s, m_s, w_s,
):
    raw = raw_ref[...]
    soft = jnp.maximum(raw, 0.0) + jnp.log1p(jnp.exp(-jnp.abs(raw)))
    gamma = (0.5 * math.sqrt(2.0 / (9.0 * PQ))) * soft
    gamma16 = column_of(gamma, HP, 1)
    gamma48 = column_of(gamma, H * PQ, PQ)

    kp_s[:, :816] = jnp.dot(ks_ref[...].T, wk_ref[...], preferred_element_type=F32)
    put(kpt_s, 0, kp_s[...].T)
    frames = kf_ref[...]
    kt_s[0:192] = take(kpt_s, 0, 192, 1).astype(BF16)
    points = rotate([take(kpt_s, 384 + x, 48, 3) for x in range(3)], frames)
    for x in range(3):
        hi, lo = split(points[x])
        kt_s[192 + 48 * x : 240 + 48 * x] = hi.astype(BF16)
        kt_s[336 + 48 * x : 384 + 48 * x] = lo.astype(BF16)
        kt_s[480 + 48 * x : 528 + 48 * x] = hi.astype(BF16)
    put(kpt_s, 832, points[0] * points[0] + points[1] * points[1] + points[2] * points[2])
    nk_s[...] = jnp.zeros_like(nk_s)
    nk_s[0:H] = sum(take(kpt_s, 832 + p, H, PQ) for p in range(PQ))
    for t, part in enumerate(split3(-gamma16 * nk_s[...])):
        kt_s[624 + HP * t : 640 + HP * t] = part.astype(BF16)
    kt_s[672:720] = jnp.ones((48, kt_s.shape[1]), BF16)
    shape = (48, kt_s.shape[1])
    index = lax.broadcasted_iota(jnp.int32, shape, 0)
    same = (jnp.bitwise_and(index, 7) == kc_ref[...]) & (index < 24)
    away = jnp.where((index == 24) & (km_ref[...] != 1), FAR, 0.0)
    kt_s[720:768] = (same.astype(F32) + away).astype(BF16)
    points = rotate([take(kpt_s, 528 + x, 96, 3) for x in range(3)], frames)
    for x in range(3):
        vt_s[128 * x : 128 * x + 96] = points[x].astype(BF16)
        vt_s[128 * x + 96 : 128 * x + 128] = take(kpt_s, 192 + 32 * x, 32, 1).astype(BF16)
    vt_s[384:480] = take(kpt_s, 288, 96, 1).astype(BF16)
    vt_s[480:512] = jnp.zeros((32, vt_s.shape[1]), BF16)

    qp_s[:, :336] = jnp.dot(qs_ref[...], wq_ref[...], preferred_element_type=F32)
    put(qpt_s, 0, qp_s[...].T)
    frames = qf_ref[...]
    qft_s[0:192] = take(qpt_s, 0, 192, 1).astype(BF16).astype(F32) * (1.0 / math.sqrt(C))
    points = rotate([take(qpt_s, 192 + x, 48, 3) for x in range(3)], frames)
    for x in range(3):
        hi, lo = split(2.0 * gamma48 * points[x])
        qft_s[192 + 48 * x : 240 + 48 * x] = hi
        qft_s[336 + 48 * x : 384 + 48 * x] = hi
        qft_s[480 + 48 * x : 528 + 48 * x] = lo
    put(qpt_s, 336, points[0] * points[0] + points[1] * points[1] + points[2] * points[2])
    nq_s[...] = jnp.zeros_like(nq_s)
    nq_s[0:H] = sum(take(qpt_s, 336 + p, H, PQ) for p in range(PQ))
    qft_s[624:672] = jnp.ones((48, qft_s.shape[1]), F32)
    for t, part in enumerate(split3(-gamma16 * nq_s[...])):
        qft_s[672 + HP * t : 688 + HP * t] = part
    shape = (48, qft_s.shape[1])
    index = lax.broadcasted_iota(jnp.int32, shape, 0)
    same = (jnp.bitwise_and(index, 7) == qc_ref[...]) & (index < 24)
    qft_s[720:768] = (same | (index == 24)).astype(F32)
    qf_s[...] = qft_s[...].T

    m_s[...] = dm_ref[...]
    lane = lax.broadcasted_iota(jnp.int32, (HP, 128), 1)
    tail = dm_ref[:, 640:768]
    for t, part in enumerate(split3(column_of(cb_ref[...], HP, 1))):
        tail = jnp.where((lane >= 80 + 8 * t) & (lane < 88 + 8 * t), part, tail)
    m_s[:, 640:768] = tail
    pw_s[...] = jnp.zeros_like(pw_s)
    pw_s[:, :H] = pw_ref[...].astype(F32)
    w_s[...] = pw_s[...].T[:HP].astype(BF16)


def attend_kernel(
    ks_ref, wk_ref, kf_ref, kc_ref, km_ref, qs_ref, wq_ref, qf_ref, qc_ref, pw_ref, raw_ref, cb_ref,
    dm_ref, lm_ref, pair_ref, out_ref,
    kp_s, kpt_s, qp_s, qpt_s, nk_s, nq_s, pw_s, kt_s, vt_s, qft_s, qf_s, m_s, w_s, o_s,
):
    step = pl.program_id(0)

    @pl.when(step == 0)
    def _():
        prepare(
            ks_ref, wk_ref, kf_ref, kc_ref, km_ref, qs_ref, wq_ref, qf_ref, qc_ref, pw_ref, raw_ref,
            cb_ref, dm_ref, kp_s, kpt_s, qp_s, qpt_s, nk_s, nq_s, pw_s, kt_s, vt_s, qft_s, qf_s,
            m_s, w_s,
        )

    rows = QB * HP
    first = pl.multiple_of(step * QB, QB)
    mine = qf_s[pl.ds(first, QB), :]
    spread = (mine[:, None, :] * m_s[...][None]).reshape(rows, KD).astype(BF16)
    logits = jnp.dot(spread, kt_s[...], preferred_element_type=F32)
    weight = w_s[...]
    bias = jnp.concatenate(
        [lax.dot_general(weight, pair_ref[i], NT, preferred_element_type=F32) for i in range(QB)], 0
    )
    logits = math.sqrt(1.0 / 3.0) * (logits + bias)
    peak = jnp.maximum(jnp.max(logits, 1, keepdims=True), 0.1 * FAR)
    expd = jnp.exp(logits - peak)
    total = jnp.maximum(jnp.sum(expd, 1, keepdims=True), 1e-30)
    weights = expd.astype(BF16)
    scale = 1.0 / total
    level = peak + jnp.log(total)
    hi, lo = split(level)
    paired = jnp.concatenate(
        [
            jnp.dot(weights[HP * i : HP * i + HP], pair_ref[i], preferred_element_type=F32)
            for i in range(QB)
        ],
        0,
    )
    o_s[...] = paired * scale
    spots = lax.dot_general(weights, vt_s[...], NT, preferred_element_type=F32) * scale
    lane = lax.broadcasted_iota(jnp.int32, (rows, 128), 1)
    for row in range(4):
        part = spots[:, 128 * row : 128 * row + 128]
        if row == 3:
            part = jnp.where(lane < 96, part, jnp.where(lane < 108, hi, lo))
        part = part.reshape(QB, HP, 128) * lm_ref[:, 128 * row : 128 * row + 128][None]
        o_s[pl.ds(H + row, QB, stride=HP), :] = jnp.sum(part, 1)
    out_ref[...] = o_s[...].astype(BF16)


def whole(shape):
    return pl.BlockSpec(shape, lambda i: (0,) * len(shape))


def attend(ks, wk, kf, kc, km, qs, wq, qf, qc, pw, raw, cb, pair):
    queries, keys = pair.shape[:2]
    operands = [
        ks, wk, kf, kc.reshape(1, -1), km.reshape(1, -1), qs, wq, qf, qc.reshape(1, -1), pw,
        raw.reshape(1, -1), cb.reshape(1, -1), jnp.asarray(depth_mask()),
        jnp.asarray((lane_heads()[1][None, :] == np.arange(HP)[:, None]).astype(np.float32)),
    ]
    return pl.pallas_call(
        attend_kernel,
        grid=(queries // QB,),
        out_shape=jax.ShapeDtypeStruct((queries * HP, CZ), BF16),
        in_specs=[whole(x.shape) for x in operands]
        + [pl.BlockSpec((QB, keys, CZ), lambda i: (i, 0, 0))],
        out_specs=pl.BlockSpec((QB * HP, CZ), lambda i: (i, 0)),
        scratch_shapes=[
            pltpu.VMEM((keys, 896), F32),
            pltpu.VMEM((keys // 128, 896, 128), F32),
            pltpu.VMEM((queries, 384), F32),
            pltpu.VMEM((queries // 128, 384, 128), F32),
            pltpu.VMEM((HP, keys), F32),
            pltpu.VMEM((HP, queries), F32),
            pltpu.VMEM((CZ, 128), F32),
            pltpu.VMEM((KD, keys), BF16),
            pltpu.VMEM((GL, keys), BF16),
            pltpu.VMEM((KD, queries), F32),
            pltpu.VMEM((queries, KD), F32),
            pltpu.VMEM((HP, KD), F32),
            pltpu.VMEM((HP, CZ), BF16),
            pltpu.VMEM((QB * HP, CZ), F32),
        ],
        compiler_params=pltpu.CompilerParams(vmem_limit_bytes=32 * 2**20),
    )(*operands, pair)


def finish_kernel(x_ref, qf_ref, em_ref, ow_ref, ob_ref, out_ref, x_s, p_s, g_s, w_s, f_s):
    share = out_ref.shape[0]
    sources = x_ref.shape[0]
    first = lax.axis_index("col") * share
    lane = lax.broadcasted_iota(jnp.int32, (sources, 128), 1)
    stat = (lane >= 96) & (lane < 108)
    for q in range(share):
        block = x_ref[:, HP * q : HP * q + HP, :].reshape(sources * HP, 128)
        x_s[...] = block.astype(F32)
        rows = [x_s[pl.ds(H + r, sources, stride=HP), :] for r in range(4)]
        level = jnp.where(stat, rows[3] + pltpu.roll(rows[3], 128 - H, 1), 0.0)
        part = jnp.exp(level - jnp.max(level, 0, keepdims=True))
        part = jnp.where(stat, part / jnp.sum(part, 0, keepdims=True), 0.0)
        hi, lo = split(part)
        spread = jnp.dot(hi.astype(BF16), em_ref[...], preferred_element_type=F32) + jnp.dot(
            lo.astype(BF16), em_ref[...], preferred_element_type=F32
        )
        for r in range(4):
            g_s[pl.ds(8 * r + q, 1), :] = jnp.sum(
                spread[:, 128 * r : 128 * r + 128] * rows[r], 0, keepdims=True
            )
        w_s[...] = jnp.zeros_like(w_s)
        w_s[0:sources] = part
        turned = w_s[...].T[96:112]
        source = lax.broadcasted_iota(jnp.int32, (128, sources * HP), 0)
        column = lax.broadcasted_iota(jnp.int32, (128, sources * HP), 1)
        repeat = (lax.shift_right_logical(column, 4) == source).astype(BF16)
        own = lax.broadcasted_iota(jnp.int32, (HP, sources * HP), 0) == jnp.bitwise_and(
            lax.broadcasted_iota(jnp.int32, (HP, sources * HP), 1), HP - 1
        )
        paired = jnp.zeros((HP, 128), F32)
        for piece in split(turned):
            wide = jnp.dot(piece.astype(BF16), repeat, preferred_element_type=F32)
            wide = jnp.where(own, wide, 0.0).astype(BF16)
            paired += jnp.dot(wide, block, preferred_element_type=F32)
        p_s[HP * q : HP * q + HP] = paired

    slot = lax.broadcasted_iota(jnp.int32, (share, 128), 1) == first + lax.broadcasted_iota(
        jnp.int32, (share, 128), 0
    )
    frame = [
        jnp.sum(jnp.where(slot, qf_ref[j : j + 1, :], 0.0), 1, keepdims=True) for j in range(12)
    ]
    g = [g_s[8 * r : 8 * r + share, :] for r in range(4)]
    moved = [g[x] - frame[9 + x] for x in range(3)]
    local = [
        frame[x] * moved[0] + frame[3 + x] * moved[1] + frame[6 + x] * moved[2] for x in range(3)
    ]
    lengths = jnp.sqrt(local[0] * local[0] + local[1] * local[1] + local[2] * local[2] + 1.0)
    spot = lax.broadcasted_iota(jnp.int32, (128, 384), 0)
    column = lax.broadcasted_iota(jnp.int32, (128, 384), 1)
    woven = sum(
        jnp.dot(
            local[x].astype(BF16),
            ((column == 3 * spot + x) & (spot < 96)).astype(BF16),
            preferred_element_type=F32,
        )
        for x in range(3)
    )
    f_s[:, 0:384] = woven
    f_s[:, 384:512] = lengths
    for r in range(3):
        f_s[:, 512 + 128 * r : 640 + 128 * r] = pltpu.roll(g[r], 32, 1)
    total = ob_ref[...] + jnp.zeros((share, ob_ref.shape[1]), F32)

    def add(value, low, high):
        return jnp.dot(value.astype(BF16), ow_ref[low:high, :], preferred_element_type=F32)

    total += add(f_s[:, 0:288], 192, 480)
    total += add(f_s[:, 384:480], 480, 576)
    for r in range(3):
        total += add(f_s[:, 512 + 128 * r : 544 + 128 * r], 32 * r, 32 * r + 32)
    total += add(g[3][:, 0:96], 96, 192)
    for h in range(H):
        value = p_s[pl.ds(h, share, stride=HP), :]
        total += add(value, 576 + CZ * h, 576 + CZ * h + CZ)
    out_ref[...] = total.astype(BF16)


def finish(parts, qf, out_weight, out_bias):
    share = parts.shape[1] // HP
    expand = np.zeros((128, GL), np.float32)
    for index, head in enumerate(lane_heads()[0]):
        if head >= 0:
            expand[96 + head, index] = 1.0
    sources = parts.shape[0]
    return pl.pallas_call(
        finish_kernel,
        out_shape=jax.ShapeDtypeStruct((share, out_bias.shape[0]), BF16),
        scratch_shapes=[
            pltpu.VMEM((sources * HP, 128), F32),
            pltpu.VMEM((share * HP, 128), F32),
            pltpu.VMEM((32, 128), F32),
            pltpu.VMEM((128, 128), F32),
            pltpu.VMEM((share, 896), F32),
        ],
        compiler_params=pltpu.CompilerParams(vmem_limit_bytes=24 * 2**20),
    )(parts, qf, jnp.asarray(expand, BF16), out_weight, out_bias.reshape(1, -1))


def body(
    query_single,
    query_frames,
    query_chain,
    key_single,
    key_frames,
    key_chain,
    key_mask,
    pair,
    w_query,
    w_key,
    pair_weight,
    point_raw,
    chain_bias,
    out_weight,
    out_bias,
):
    rows, cols = lax.axis_size("row"), lax.axis_size("col")
    turned = key_single.T
    keys = lax.all_to_all(
        jnp.broadcast_to(turned[None], (rows, *turned.shape)), "row", 0, 0, tiled=True
    ).reshape(-1, turned.shape[1])
    queries = lax.all_to_all(
        jnp.broadcast_to(query_single[None], (cols, *query_single.shape)), "col", 0, 0, tiled=True
    ).reshape(-1, query_single.shape[1])
    sums = attend(
        keys, w_key, key_frames, key_chain, key_mask, queries, w_query, query_frames, query_chain,
        pair_weight, point_raw, chain_bias, pair,
    )
    parts = lax.all_to_all(sums.reshape(cols, -1, CZ), "col", 0, 0, tiled=True)
    return finish(parts, query_frames, out_weight, out_bias)


def solution(mesh):
    return jax.shard_map(
        body,
        mesh=mesh,
        in_specs=(
            P(("row", "col"), None),
            P(None, "row"),
            P("row"),
            P("col", "row"),
            P(None, "col"),
            P("col"),
            P("col"),
            P("row", "col", None),
            P(),
            P(),
            P(),
            P(),
            P(),
            P(),
            P(),
        ),
        out_specs=P(("row", "col"), None),
        check_vma=False,
    )
```

```python
import functools
import math

import jax
import jax.numpy as jnp
import numpy as np
from jax import lax
from jax.experimental import pallas as pl
from jax.experimental.pallas import tpu as pltpu
from jax.sharding import PartitionSpec as P

H = 12
C = 16
PQ = 4
PV = 8
CZ = 128
HP = 16
KD = 768
GL = 512
QB = 16
FAR = -1e30
F32 = jnp.float32
BF16 = jnp.bfloat16
NT = (((1,), (1,)), ((), ()))
NN = (((1,), (0,)), ((), ()))


def lane_heads():
    head = np.full((GL,), -1)
    for row in range(3):
        head[128 * row : 128 * row + 96] = np.arange(96) // PV
        head[128 * row + 96 : 128 * row + 128] = (np.arange(32) + 32 * row) // C
    head[384:480] = (np.arange(96) + 96) // C
    plain = head.copy()
    head[480:492] = np.arange(H)
    head[492:504] = np.arange(H)
    return plain, head


def depth_mask():
    column = np.arange(KD)
    head = np.full((KD,), -1)
    head[:192] = column[:192] // C
    head[192:624] = ((column[192:624] - 192) % 48) // PQ
    head[624:720] = (column[624:720] - 624) % HP
    mask = (head[None, :] == np.arange(HP)[:, None]).astype(np.float32)
    mask[:, 744] = 1.0
    mask[H:] = 0.0
    return mask


def split(x):
    hi = x.astype(BF16).astype(F32)
    return hi, x - hi


def split3(x):
    hi, rest = split(x)
    mid, rest = split(rest)
    return hi, mid, rest.astype(BF16).astype(F32)


def column_of(row, rows, per):
    shape = (rows, H)
    index = lax.broadcasted_iota(jnp.int32, shape, 0)
    lane = lax.broadcasted_iota(jnp.int32, shape, 1)
    hit = (index >= lane * per) & (index < lane * per + per)
    return jnp.sum(jnp.where(hit, row, 0.0), 1, keepdims=True)


def rotate(points, frames):
    return [
        frames[3 * x : 3 * x + 1] * points[0]
        + frames[3 * x + 1 : 3 * x + 2] * points[1]
        + frames[3 * x + 2 : 3 * x + 3] * points[2]
        + frames[9 + x : 10 + x]
        for x in range(3)
    ]


def take(ref, start, count, stride):
    return jnp.concatenate(
        [ref.at[tile][pl.ds(start, count, stride=stride), :] for tile in range(ref.shape[0])], 1
    )


def put(ref, start, value):
    for tile in range(ref.shape[0]):
        ref[tile, start : start + value.shape[0], :] = value[:, 128 * tile : 128 * tile + 128]


def gamma_of(raw):
    soft = jnp.maximum(raw, 0.0) + jnp.log1p(jnp.exp(-jnp.abs(raw)))
    return (0.5 * math.sqrt(2.0 / (9.0 * PQ))) * soft


def spread_kernel(q_ref, k_ref, q_out, k_out):
    q_out[...] = jnp.broadcast_to(q_ref[...][None], q_out.shape)
    k_out[...] = jnp.broadcast_to(k_ref[...][None], k_out.shape)


def shadow_kernel(
    qs_ref, wq_hbm, qf_hbm, qc_hbm, raw_hbm, cb_hbm, dm_hbm, kf_hbm, kc_hbm, km_hbm, pw_hbm, wk_hbm,
    pair_ref, feat_ref, mask_ref, wk_ref, bias_ref,
    wq_v, qf_v, qc_v, raw_v, cb_v, dm_v, kf_v, kc_v, km_v, pw_v,
    qpt_s, nq_s, qft_s, pw_s, pair_v, sem, pair_sem,
):
    moves = [
        (pw_hbm, pw_v), (wq_hbm, wq_v), (qf_hbm, qf_v), (qc_hbm, qc_v), (raw_hbm, raw_v),
        (cb_hbm, cb_v), (dm_hbm, dm_v), (kf_hbm, kf_v), (kc_hbm, kc_v), (km_hbm, km_v),
        (wk_hbm, wk_ref),
    ]
    small = [pltpu.make_async_copy(*move, sem.at[i]) for i, move in enumerate(moves)]
    copies = [
        pltpu.make_async_copy(
            pair_ref.at[pl.ds(QB * i, QB)], pair_v.at[pl.ds(QB * i, QB)], pair_sem.at[i]
        )
        for i in range(pair_ref.shape[0] // QB)
    ]
    for copy in small[:1] + copies[:4] + small[1:] + copies[4:]:
        copy.start()
    small[0].wait()
    pw_s[...] = jnp.zeros_like(pw_s)
    pw_s[0:H] = pw_v[...].astype(F32)
    weight = pw_s[...].astype(BF16)
    for i, copy in enumerate(copies):
        if i == 4:
            for other in small[1:]:
                other.wait()
            prepare_queries(
                qs_ref, wq_v, qf_v, qc_v, raw_v, cb_v, dm_v, feat_ref, mask_ref, qpt_s, nq_s, qft_s
            )
            mask_ref[0:H, KD + GL : KD + GL + 256] = kf_v[...]
            mask_ref[H : H + 1, KD + GL : KD + GL + 256] = kc_v[...].astype(F32)
            mask_ref[H + 1 : H + 2, KD + GL : KD + GL + 256] = km_v[...].astype(F32)
        copy.wait()
        for q in range(QB * i, QB * i + QB):
            bias_ref[HP * q : HP * q + HP] = lax.dot_general(
                weight, pair_v[q], NT, preferred_element_type=F32
            )


def prepare_keys(info, gamma16, kt_ref, vt_ref, kpt_s, nk_s):
    frames, chain, kept = info[0:H], info[H : H + 1], info[H + 1 : H + 2]
    kt_ref[0:192] = take(kpt_s, 0, 192, 1).astype(BF16)
    points = rotate([take(kpt_s, 384 + x, 48, 3) for x in range(3)], frames)
    for x in range(3):
        hi, lo = split(points[x])
        kt_ref[192 + 48 * x : 240 + 48 * x] = hi.astype(BF16)
        kt_ref[336 + 48 * x : 384 + 48 * x] = lo.astype(BF16)
        kt_ref[480 + 48 * x : 528 + 48 * x] = hi.astype(BF16)
    put(kpt_s, 816, points[0] * points[0] + points[1] * points[1] + points[2] * points[2])
    nk_s[...] = jnp.zeros_like(nk_s)
    nk_s[0:H] = sum(take(kpt_s, 816 + p, H, PQ) for p in range(PQ))
    for t, part in enumerate(split3(-gamma16 * nk_s[...])):
        kt_ref[624 + HP * t : 640 + HP * t] = part.astype(BF16)
    kt_ref[672:720] = jnp.ones((48, kt_ref.shape[1]), BF16)
    shape = (48, kt_ref.shape[1])
    index = lax.broadcasted_iota(jnp.int32, shape, 0)
    same = (jnp.bitwise_and(index, 7).astype(F32) == chain) & (index < 24)
    away = jnp.where((index == 24) & (kept != 1.0), FAR, 0.0)
    kt_ref[720:768] = (same.astype(F32) + away).astype(BF16)
    points = rotate([take(kpt_s, 528 + x, 96, 3) for x in range(3)], frames)
    for x in range(3):
        vt_ref[128 * x : 128 * x + 96] = points[x].astype(BF16)
        vt_ref[128 * x + 96 : 128 * x + 128] = take(kpt_s, 192 + 32 * x, 32, 1).astype(BF16)
    vt_ref[384:480] = take(kpt_s, 288, 96, 1).astype(BF16)
    vt_ref[480:512] = jnp.zeros((32, vt_ref.shape[1]), BF16)


def prepare_queries(
    qs_ref, wq_ref, qf_ref, qc_ref, raw_ref, cb_ref, dm_ref, qf_s, m_s, qpt_s, nq_s, qft_s
):
    gamma = gamma_of(raw_ref[...])
    gamma16 = column_of(gamma, HP, 1)
    gamma48 = column_of(gamma, H * PQ, PQ)
    put(qpt_s, 0, lax.dot_general(wq_ref[...], qs_ref[...], NT, preferred_element_type=F32))
    frames = qf_ref[...]
    qft_s[0:192] = take(qpt_s, 0, 192, 1).astype(BF16).astype(F32) * (1.0 / math.sqrt(C))
    points = rotate([take(qpt_s, 192 + x, 48, 3) for x in range(3)], frames)
    for x in range(3):
        hi, lo = split(2.0 * gamma48 * points[x])
        qft_s[192 + 48 * x : 240 + 48 * x] = hi
        qft_s[336 + 48 * x : 384 + 48 * x] = hi
        qft_s[480 + 48 * x : 528 + 48 * x] = lo
    put(qpt_s, 336, points[0] * points[0] + points[1] * points[1] + points[2] * points[2])
    nq_s[...] = jnp.zeros_like(nq_s)
    nq_s[0:H] = sum(take(qpt_s, 336 + p, H, PQ) for p in range(PQ))
    qft_s[624:672] = jnp.ones((48, qft_s.shape[1]), F32)
    for t, part in enumerate(split3(-gamma16 * nq_s[...])):
        qft_s[672 + HP * t : 688 + HP * t] = part
    shape = (48, qft_s.shape[1])
    index = lax.broadcasted_iota(jnp.int32, shape, 0)
    same = (jnp.bitwise_and(index, 7) == qc_ref[...]) & (index < 24)
    qft_s[720:768] = (same | (index == 24)).astype(F32)
    qf_s[...] = qft_s[...].T

    m_s[:, 0 : KD + GL] = dm_ref[...]
    m_s[:, KD + GL + 256 :] = jnp.broadcast_to(gamma16, (HP, 128))
    lane = lax.broadcasted_iota(jnp.int32, (HP, 128), 1)
    tail = dm_ref[:, 640:768]
    for t, part in enumerate(split3(column_of(cb_ref[...], HP, 1))):
        tail = jnp.where((lane >= 80 + 8 * t) & (lane < 88 + 8 * t), part, tail)
    m_s[:, 640:768] = tail


def attend_kernel(
    ks_ref, wk_ref, feat_ref, mask_ref, bias_ref, pair_ref,
    out_ref, kpt_s, nk_s, kt_s, vt_s, v_s, w_s, z_s, o_s, pair_v, pair_sem,
):
    queries = pair_ref.shape[0]
    copies = [
        pltpu.make_async_copy(
            pair_ref.at[pl.ds(QB * i, QB)], pair_v.at[pl.ds(QB * i, QB)], pair_sem.at[i]
        )
        for i in range(queries // QB)
    ]
    for copy in copies:
        copy.start()
    put(kpt_s, 0, jnp.dot(wk_ref[...], ks_ref[...], preferred_element_type=F32))
    info = mask_ref[:, KD + GL : KD + GL + 256]
    gamma16 = mask_ref[:, KD + GL + 256 : KD + GL + 257]
    prepare_keys(info, gamma16, kt_s, vt_s, kpt_s, nk_s)
    v_s[...] = vt_s[...].T
    rows = QB * HP
    lane = lax.broadcasted_iota(jnp.int32, (rows, 128), 1)
    gather = (
        lax.shift_right_logical(lax.broadcasted_iota(jnp.int32, (QB, rows), 1), 4)
        == lax.broadcasted_iota(jnp.int32, (QB, rows), 0)
    ).astype(BF16)

    for step in range(queries // QB):
        first, start = step * QB, step * rows
        mine = feat_ref[first : first + QB, :]
        spread = (mine[:, None, :] * mask_ref[:, 0:KD][None]).reshape(rows, KD).astype(BF16)
        logits = jnp.dot(spread, kt_s[...], preferred_element_type=F32)
        logits = math.sqrt(1.0 / 3.0) * (logits + bias_ref[start : start + rows, :])
        peak = jnp.maximum(jnp.max(logits, 1, keepdims=True), 0.1 * FAR)
        expd = jnp.exp(logits - peak)
        total = jnp.maximum(jnp.sum(expd, 1, keepdims=True), 1e-30)
        weights = (expd * (1.0 / total)).astype(BF16)
        hi, lo = split(peak + jnp.log(total))
        w_s[start : start + rows, :] = weights
        spots = jnp.dot(weights, v_s[...], preferred_element_type=F32)
        tail = jnp.where(lane < 96, spots[:, 384:512], jnp.where(lane < 108, hi, lo))
        own = [
            (part.reshape(QB, HP, 128) * mask_ref[:, KD + 128 * row : KD + 128 * row + 128][None])
            .reshape(rows, 128)
            .astype(BF16)
            for row, part in enumerate([spots[:, 128 * r : 128 * r + 128] for r in range(3)] + [tail])
        ]
        z_s[first : first + QB, :] = jnp.dot(
            gather, jnp.concatenate(own, 1), preferred_element_type=F32
        )

    for step, copy in enumerate(copies):
        first, start = step * QB, step * rows
        copy.wait()
        for i in range(QB):
            row = start + HP * i
            o_s[row : row + HP] = jnp.dot(
                w_s[row : row + HP, :], pair_v[first + i], preferred_element_type=F32
            )
        for r in range(4):
            o_s[pl.ds(start + H + r, QB, stride=HP), :] = z_s[
                first : first + QB, 128 * r : 128 * r + 128
            ]
        out_ref[start : start + rows, :] = o_s[start : start + rows, :].astype(BF16)


def inside(x):
    return pltpu.with_memory_space_constraint(x, pltpu.VMEM)


def outside(x):
    return pltpu.with_memory_space_constraint(x, pltpu.HBM)


VMEM = pl.BlockSpec(memory_space=pltpu.VMEM)


def spread_out(query_single, key_single, rows, cols):
    turned = key_single.T
    return pl.pallas_call(
        spread_kernel,
        out_shape=(
            pltpu.VMEM((cols, *query_single.shape), BF16),
            pltpu.VMEM((rows, *turned.shape), BF16),
        ),
        in_specs=[VMEM, VMEM],
        out_specs=(VMEM, VMEM),
        compiler_params=pltpu.CompilerParams(vmem_limit_bytes=4 * 2**20),
    )(outside(query_single), outside(turned))


HBM = pl.BlockSpec(memory_space=pltpu.HBM)


def shadow(qs, others, pair):
    queries, keys = pair.shape[:2]
    return pl.pallas_call(
        shadow_kernel,
        out_shape=(
            pltpu.VMEM((queries, KD), F32),
            pltpu.VMEM((HP, KD + GL + keys + 128), F32),
            pltpu.VMEM(others[10].shape, BF16),
            pltpu.VMEM((queries * HP, keys), F32),
        ),
        in_specs=[VMEM] + [HBM] * 12,
        out_specs=(VMEM,) * 4,
        scratch_shapes=[pltpu.VMEM(x.shape, x.dtype) for x in others[:10]]
        + [
            pltpu.VMEM((queries // 128, 384, 128), F32),
            pltpu.VMEM((HP, queries), F32),
            pltpu.VMEM((KD, queries), F32),
            pltpu.VMEM((HP, CZ), F32),
            pltpu.VMEM(pair.shape, BF16),
            pltpu.SemaphoreType.DMA((11,)),
            pltpu.SemaphoreType.DMA((queries // QB,)),
        ],
        cost_estimate=pl.CostEstimate(
            flops=2 * queries * keys * CZ * HP, bytes_accessed=pair.size * 2, transcendentals=0
        ),
        compiler_params=pltpu.CompilerParams(vmem_limit_bytes=16 * 2**20),
    )(qs, *[outside(x) for x in (*others, pair)])


def attend(ks, wk, feats, mask, bias, pair):
    queries, keys = pair.shape[:2]
    return pl.pallas_call(
        attend_kernel,
        out_shape=jax.ShapeDtypeStruct((queries * HP, CZ), BF16),
        in_specs=[VMEM] * 5 + [HBM],
        out_specs=VMEM,
        scratch_shapes=[
            pltpu.VMEM((keys // 128, 896, 128), F32),
            pltpu.VMEM((HP, keys), F32),
            pltpu.VMEM((KD, keys), BF16),
            pltpu.VMEM((GL, keys), BF16),
            pltpu.VMEM((keys, GL), BF16),
            pltpu.VMEM((queries * HP, keys), BF16),
            pltpu.VMEM((queries, GL), F32),
            pltpu.VMEM((queries * HP, CZ), F32),
            pltpu.VMEM(pair.shape, BF16),
            pltpu.SemaphoreType.DMA((queries // QB,)),
        ],
        cost_estimate=pl.CostEstimate(
            flops=2 * queries * HP * keys * (KD + GL + CZ),
            bytes_accessed=queries * keys * CZ * 2,
            transcendentals=queries * HP * keys,
        ),
        compiler_params=pltpu.CompilerParams(vmem_limit_bytes=24 * 2**20),
    )(ks, *[inside(x) for x in (wk, feats, mask, bias)], outside(pair))


def finish_kernel(
    x_ref, qf_hbm, em_hbm, ob_hbm, ow_hbm, out_ref,
    qf_ref, em_ref, ob_ref, ow_ref, x_s, p_s, g_s, w_s, f_s, sem,
):
    moves = [(em_hbm, em_ref), (qf_hbm, qf_ref), (ob_hbm, ob_ref), (ow_hbm, ow_ref)]
    copies = [pltpu.make_async_copy(*move, sem.at[i]) for i, move in enumerate(moves)]
    for copy in copies:
        copy.start()
    share = out_ref.shape[0]
    sources = x_ref.shape[0]
    first = lax.axis_index("col") * share
    lane = lax.broadcasted_iota(jnp.int32, (sources, 128), 1)
    stat = (lane >= 96) & (lane < 108)
    for q in range(share):
        block = x_ref[:, HP * q : HP * q + HP, :].reshape(sources * HP, 128)
        x_s[...] = block.astype(F32)
        rows = [x_s[pl.ds(H + r, sources, stride=HP), :] for r in range(4)]
        level = jnp.where(stat, rows[3] + pltpu.roll(rows[3], 128 - H, 1), 0.0)
        part = jnp.exp(level - jnp.max(level, 0, keepdims=True))
        part = jnp.where(stat, part / jnp.sum(part, 0, keepdims=True), 0.0)
        hi, lo = split(part)
        if q == 0:
            copies[0].wait()
        spread = jnp.dot(hi.astype(BF16), em_ref[...], preferred_element_type=F32) + jnp.dot(
            lo.astype(BF16), em_ref[...], preferred_element_type=F32
        )
        for r in range(4):
            g_s[pl.ds(8 * r + q, 1), :] = jnp.sum(
                spread[:, 128 * r : 128 * r + 128] * rows[r], 0, keepdims=True
            )
        w_s[...] = jnp.zeros_like(w_s)
        w_s[0:sources] = part
        turned = w_s[...].T[96:112]
        source = lax.broadcasted_iota(jnp.int32, (128, sources * HP), 0)
        column = lax.broadcasted_iota(jnp.int32, (128, sources * HP), 1)
        repeat = (lax.shift_right_logical(column, 4) == source).astype(BF16)
        own = lax.broadcasted_iota(jnp.int32, (HP, sources * HP), 0) == jnp.bitwise_and(
            lax.broadcasted_iota(jnp.int32, (HP, sources * HP), 1), HP - 1
        )
        paired = jnp.zeros((HP, 128), F32)
        for piece in split(turned):
            wide = jnp.dot(piece.astype(BF16), repeat, preferred_element_type=F32)
            wide = jnp.where(own, wide, 0.0).astype(BF16)
            paired += jnp.dot(wide, block, preferred_element_type=F32)
        p_s[HP * q : HP * q + HP] = paired

    for copy in copies[1:]:
        copy.wait()
    slot = lax.broadcasted_iota(jnp.int32, (share, 128), 1) == first + lax.broadcasted_iota(
        jnp.int32, (share, 128), 0
    )
    frame = [
        jnp.sum(jnp.where(slot, qf_ref[j : j + 1, :], 0.0), 1, keepdims=True) for j in range(12)
    ]
    g = [g_s[8 * r : 8 * r + share, :] for r in range(4)]
    moved = [g[x] - frame[9 + x] for x in range(3)]
    local = [
        frame[x] * moved[0] + frame[3 + x] * moved[1] + frame[6 + x] * moved[2] for x in range(3)
    ]
    lengths = jnp.sqrt(local[0] * local[0] + local[1] * local[1] + local[2] * local[2] + 1.0)
    spot = lax.broadcasted_iota(jnp.int32, (128, 384), 0)
    column = lax.broadcasted_iota(jnp.int32, (128, 384), 1)
    woven = sum(
        jnp.dot(
            local[x].astype(BF16),
            ((column == 3 * spot + x) & (spot < 96)).astype(BF16),
            preferred_element_type=F32,
        )
        for x in range(3)
    )
    f_s[:, 0:384] = woven
    f_s[:, 384:512] = lengths
    for r in range(3):
        f_s[:, 512 + 128 * r : 640 + 128 * r] = pltpu.roll(g[r], 32, 1)
    total = ob_ref[...] + jnp.zeros((share, ob_ref.shape[1]), F32)

    def add(value, low, high):
        return jnp.dot(value.astype(BF16), ow_ref[low:high, :], preferred_element_type=F32)

    total += add(f_s[:, 0:288], 192, 480)
    total += add(f_s[:, 384:480], 480, 576)
    for r in range(3):
        total += add(f_s[:, 512 + 128 * r : 544 + 128 * r], 32 * r, 32 * r + 32)
    total += add(g[3][:, 0:96], 96, 192)
    for h in range(H):
        value = p_s[pl.ds(h, share, stride=HP), :]
        total += add(value, 576 + CZ * h, 576 + CZ * h + CZ)
    out_ref[...] = total.astype(BF16)


def finish(parts, qf, out_weight, out_bias):
    share = parts.shape[1] // HP
    expand = np.zeros((128, GL), np.float32)
    for index, head in enumerate(lane_heads()[0]):
        if head >= 0:
            expand[96 + head, index] = 1.0
    sources = parts.shape[0]
    others = [qf, jnp.asarray(expand, BF16), out_bias.reshape(1, -1), out_weight]
    return pl.pallas_call(
        finish_kernel,
        out_shape=jax.ShapeDtypeStruct((share, out_bias.shape[0]), BF16),
        in_specs=[VMEM] + [HBM] * 4,
        out_specs=VMEM,
        scratch_shapes=[pltpu.VMEM(x.shape, x.dtype) for x in others]
        + [
            pltpu.VMEM((sources * HP, 128), F32),
            pltpu.VMEM((share * HP, 128), F32),
            pltpu.VMEM((32, 128), F32),
            pltpu.VMEM((128, 128), F32),
            pltpu.VMEM((share, 896), F32),
            pltpu.SemaphoreType.DMA((4,)),
        ],
        compiler_params=pltpu.CompilerParams(vmem_limit_bytes=12 * 2**20),
    )(parts, *[outside(x) for x in others])


def body(
    query_single,
    query_frames,
    query_chain,
    key_single,
    key_frames,
    key_chain,
    key_mask,
    pair,
    w_query,
    w_key,
    pair_weight,
    point_raw,
    chain_bias,
    out_weight,
    out_bias,
):
    rows, cols = lax.axis_size("row"), lax.axis_size("col")
    query_parts, key_parts = spread_out(query_single, key_single, rows, cols)
    queries = lax.all_to_all(query_parts, "col", 0, 0, tiled=True).reshape(
        -1, query_single.shape[1]
    )
    keys = lax.all_to_all(key_parts, "row", 0, 0, tiled=True).reshape(-1, key_single.shape[0])
    heads = (lane_heads()[1][None, :] == np.arange(HP)[:, None]).astype(np.float32)
    feats, mask, wk, bias = shadow(
        queries,
        [
            w_query.T, query_frames, query_chain.reshape(1, -1), point_raw.reshape(1, -1),
            chain_bias.reshape(1, -1), jnp.asarray(np.concatenate([depth_mask(), heads], 1)),
            key_frames, key_chain.reshape(1, -1), key_mask.reshape(1, -1), pair_weight.T, w_key.T,
        ],
        pair,
    )
    sums = attend(keys, wk, feats, mask, bias, pair)
    parts = lax.all_to_all(sums.reshape(cols, -1, CZ), "col", 0, 0, tiled=True)
    return finish(parts, query_frames, out_weight, out_bias)


def solution(mesh):
    return jax.shard_map(
        body,
        mesh=mesh,
        in_specs=(
            P(("row", "col"), None),
            P(None, "row"),
            P("row"),
            P("col", "row"),
            P(None, "col"),
            P("col"),
            P("col"),
            P("row", "col", None),
            P(),
            P(),
            P(),
            P(),
            P(),
            P(),
            P(),
        ),
        out_specs=P(("row", "col"), None),
        check_vma=False,
    )
```

```python
import functools
import math

import jax
import jax.numpy as jnp
import numpy as np
from jax import lax
from jax.experimental import pallas as pl
from jax.experimental.pallas import tpu as pltpu
from jax.sharding import PartitionSpec as P

H = 12
C = 16
PQ = 4
PV = 8
CZ = 128
HP = 16
KD = 768
GL = 512
QB = 32
SB = 16
SHARE = 4
FAR = -1e30
F32 = jnp.float32
BF16 = jnp.bfloat16
NT = (((1,), (1,)), ((), ()))
NN = (((1,), (0,)), ((), ()))


def lane_heads():
    head = np.full((GL,), -1)
    for row in range(3):
        head[128 * row : 128 * row + 96] = np.arange(96) // PV
        head[128 * row + 96 : 128 * row + 128] = (np.arange(32) + 32 * row) // C
    head[384:480] = (np.arange(96) + 96) // C
    plain = head.copy()
    head[480:492] = np.arange(H)
    head[492:504] = np.arange(H)
    return plain, head


def depth_mask():
    column = np.arange(KD)
    head = np.full((KD,), -1)
    head[:192] = column[:192] // C
    head[192:624] = ((column[192:624] - 192) % 48) // PQ
    head[624:720] = (column[624:720] - 624) % HP
    mask = (head[None, :] == np.arange(HP)[:, None]).astype(np.float32)
    mask[:, 744] = 1.0
    mask[H:] = 0.0
    return mask


def split(x):
    hi = x.astype(BF16).astype(F32)
    return hi, x - hi


def split3(x):
    hi, rest = split(x)
    mid, rest = split(rest)
    return hi, mid, rest.astype(BF16).astype(F32)


def column_of(row, rows, per):
    shape = (rows, H)
    index = lax.broadcasted_iota(jnp.int32, shape, 0)
    lane = lax.broadcasted_iota(jnp.int32, shape, 1)
    hit = (index >= lane * per) & (index < lane * per + per)
    return jnp.sum(jnp.where(hit, row, 0.0), 1, keepdims=True)


def rotate(points, frames):
    return [
        frames[3 * x : 3 * x + 1] * points[0]
        + frames[3 * x + 1 : 3 * x + 2] * points[1]
        + frames[3 * x + 2 : 3 * x + 3] * points[2]
        + frames[9 + x : 10 + x]
        for x in range(3)
    ]


def take(ref, start, count, stride):
    return jnp.concatenate(
        [ref.at[tile][pl.ds(start, count, stride=stride), :] for tile in range(ref.shape[0])], 1
    )


def put(ref, start, value):
    for tile in range(ref.shape[0]):
        ref[tile, start : start + value.shape[0], :] = value[:, 128 * tile : 128 * tile + 128]


def gamma_of(raw):
    soft = jnp.maximum(raw, 0.0) + jnp.log1p(jnp.exp(-jnp.abs(raw)))
    return (0.5 * math.sqrt(2.0 / (9.0 * PQ))) * soft


def spread_kernel(q_ref, k_ref, q_out, k_out):
    q_out[...] = jnp.broadcast_to(q_ref[...][None], q_out.shape)
    k_out[...] = jnp.broadcast_to(k_ref[...][None], k_out.shape)


def shadow_kernel(
    qs_ref, wq_hbm, qf_hbm, qc_hbm, raw_hbm, cb_hbm, dm_hbm, kf_hbm, kc_hbm, km_hbm, pw_hbm, wk_hbm,
    pair_ref, feat_ref, mask_ref, wk_ref, bias_ref,
    wq_v, qf_v, qc_v, raw_v, cb_v, dm_v, kf_v, kc_v, km_v, pw_v,
    qpt_s, nq_s, qft_s, pw_s, feat_s, pair_v, sem, pair_sem,
):
    moves = [
        (pw_hbm, pw_v), (wq_hbm, wq_v), (qf_hbm, qf_v), (qc_hbm, qc_v), (raw_hbm, raw_v),
        (cb_hbm, cb_v), (dm_hbm, dm_v), (kf_hbm, kf_v), (kc_hbm, kc_v), (km_hbm, km_v),
        (wk_hbm, wk_ref),
    ]
    small = [pltpu.make_async_copy(*move, sem.at[i]) for i, move in enumerate(moves)]
    core = lax.rem(lax.axis_index("col"), 2)
    groups = SB // SHARE
    steps = pair_ref.shape[0] // groups
    copies = [
        pltpu.make_async_copy(
            pair_ref.at[pl.ds(groups * step, groups), 1 - core if half == 0 else core],
            pair_v.at[half * steps + step],
            pair_sem.at[half * steps + step],
        )
        for half in range(2)
        for step in range(steps)
    ]
    for copy in small[:1] + copies[:4] + small[1:] + copies[4:]:
        copy.start()
    small[0].wait()
    pw_s[...] = jnp.zeros_like(pw_s)
    pw_s[0:H] = pw_v[...].astype(F32)
    weight = pw_s[...].astype(BF16)
    for i, copy in enumerate(copies):
        if i == len(copies) // 2:
            for other in small[1:]:
                other.wait()
            prepare_queries(
                qs_ref, wq_v, qf_v, qc_v, raw_v, cb_v, dm_v, feat_s, mask_ref, qpt_s, nq_s, qft_s
            )
            count = feat_ref.shape[0] // 2
            for group in range(2 * count):
                half = core if group % 2 == 0 else 1 - core
                feat_ref[(1 - half) * count + group // 2] = feat_s[
                    SHARE * group : SHARE * group + SHARE, :
                ]
            mask_ref[0:H, KD + GL : KD + GL + 256] = kf_v[...]
            mask_ref[H : H + 1, KD + GL : KD + GL + 256] = kc_v[...].astype(F32)
            mask_ref[H + 1 : H + 2, KD + GL : KD + GL + 256] = km_v[...].astype(F32)
        copy.wait()
        for q in range(SB):
            row = (SB * i + q) * HP
            bias_ref[row : row + HP] = lax.dot_general(
                weight,
                pair_v[i, q // SHARE, q % SHARE],
                NT,
                preferred_element_type=F32,
            )


def prepare_keys(info, gamma16, kt_ref, vt_ref, kpt_s, nk_s):
    frames, chain, kept = info[0:H], info[H : H + 1], info[H + 1 : H + 2]
    kt_ref[0:192] = take(kpt_s, 0, 192, 1).astype(BF16)
    points = rotate([take(kpt_s, 384 + x, 48, 3) for x in range(3)], frames)
    for x in range(3):
        hi, lo = split(points[x])
        kt_ref[192 + 48 * x : 240 + 48 * x] = hi.astype(BF16)
        kt_ref[336 + 48 * x : 384 + 48 * x] = lo.astype(BF16)
        kt_ref[480 + 48 * x : 528 + 48 * x] = hi.astype(BF16)
    put(kpt_s, 816, points[0] * points[0] + points[1] * points[1] + points[2] * points[2])
    nk_s[...] = jnp.zeros_like(nk_s)
    nk_s[0:H] = sum(take(kpt_s, 816 + p, H, PQ) for p in range(PQ))
    for t, part in enumerate(split3(-gamma16 * nk_s[...])):
        kt_ref[624 + HP * t : 640 + HP * t] = part.astype(BF16)
    kt_ref[672:720] = jnp.ones((48, kt_ref.shape[1]), BF16)
    shape = (48, kt_ref.shape[1])
    index = lax.broadcasted_iota(jnp.int32, shape, 0)
    same = (jnp.bitwise_and(index, 7).astype(F32) == chain) & (index < 24)
    away = jnp.where((index == 24) & (kept != 1.0), FAR, 0.0)
    kt_ref[720:768] = (same.astype(F32) + away).astype(BF16)
    points = rotate([take(kpt_s, 528 + x, 96, 3) for x in range(3)], frames)
    for x in range(3):
        vt_ref[128 * x : 128 * x + 96] = points[x].astype(BF16)
        vt_ref[128 * x + 96 : 128 * x + 128] = take(kpt_s, 192 + 32 * x, 32, 1).astype(BF16)
    vt_ref[384:480] = take(kpt_s, 288, 96, 1).astype(BF16)
    vt_ref[480:512] = jnp.zeros((32, vt_ref.shape[1]), BF16)


def prepare_queries(
    qs_ref, wq_ref, qf_ref, qc_ref, raw_ref, cb_ref, dm_ref, qf_s, m_s, qpt_s, nq_s, qft_s
):
    gamma = gamma_of(raw_ref[...])
    gamma16 = column_of(gamma, HP, 1)
    gamma48 = column_of(gamma, H * PQ, PQ)
    put(qpt_s, 0, lax.dot_general(wq_ref[...], qs_ref[...], NT, preferred_element_type=F32))
    frames = qf_ref[...]
    qft_s[0:192] = take(qpt_s, 0, 192, 1).astype(BF16).astype(F32) * (1.0 / math.sqrt(C))
    points = rotate([take(qpt_s, 192 + x, 48, 3) for x in range(3)], frames)
    for x in range(3):
        hi, lo = split(2.0 * gamma48 * points[x])
        qft_s[192 + 48 * x : 240 + 48 * x] = hi
        qft_s[336 + 48 * x : 384 + 48 * x] = hi
        qft_s[480 + 48 * x : 528 + 48 * x] = lo
    put(qpt_s, 336, points[0] * points[0] + points[1] * points[1] + points[2] * points[2])
    nq_s[...] = jnp.zeros_like(nq_s)
    nq_s[0:H] = sum(take(qpt_s, 336 + p, H, PQ) for p in range(PQ))
    qft_s[624:672] = jnp.ones((48, qft_s.shape[1]), F32)
    for t, part in enumerate(split3(-gamma16 * nq_s[...])):
        qft_s[672 + HP * t : 688 + HP * t] = part
    shape = (48, qft_s.shape[1])
    index = lax.broadcasted_iota(jnp.int32, shape, 0)
    same = (jnp.bitwise_and(index, 7) == qc_ref[...]) & (index < 24)
    qft_s[720:768] = (same | (index == 24)).astype(F32)
    qf_s[...] = qft_s[...].T

    m_s[:, 0 : KD + GL] = dm_ref[...]
    m_s[:, KD + GL + 256 :] = jnp.broadcast_to(gamma16, (HP, 128))
    lane = lax.broadcasted_iota(jnp.int32, (HP, 128), 1)
    tail = dm_ref[:, 640:768]
    for t, part in enumerate(split3(column_of(cb_ref[...], HP, 1))):
        tail = jnp.where((lane >= 80 + 8 * t) & (lane < 88 + 8 * t), part, tail)
    m_s[:, 640:768] = tail


def attend_kernel(
    ks_ref, wk_ref, feat_ref, mask_ref, bias_ref, pair_ref,
    send_ref, own_ref, kpt_s, nk_s, kt_s, vt_s, v_s, w_s, z_s, o_s, pair_v, pair_sem,
):
    core = lax.rem(lax.axis_index("col"), 2)
    groups = QB // SHARE
    steps = pair_ref.shape[0] // groups
    copies = {}
    for index in range(2 * steps):
        half, step = divmod(index, steps)
        copies[index] = pltpu.make_async_copy(
            pair_ref.at[pl.ds(groups * step, groups), 1 - core if half == 0 else core],
            pair_v.at[index],
            pair_sem.at[index],
        )
        copies[index].start()
    put(kpt_s, 0, jnp.dot(wk_ref[...], ks_ref[...], preferred_element_type=F32))
    info = mask_ref[:, KD + GL : KD + GL + 256]
    gamma16 = mask_ref[:, KD + GL + 256 : KD + GL + 257]
    prepare_keys(info, gamma16, kt_s, vt_s, kpt_s, nk_s)
    v_s[...] = vt_s[...].T
    rows = QB * HP
    lane = lax.broadcasted_iota(jnp.int32, (rows, 128), 1)
    gather = (
        lax.shift_right_logical(lax.broadcasted_iota(jnp.int32, (QB, rows), 1), 4)
        == lax.broadcasted_iota(jnp.int32, (QB, rows), 0)
    ).astype(BF16)

    for half in range(2):
        for step in range(steps):
            start = (half * steps + step) * rows
            group = start // (SHARE * HP)
            mine = feat_ref[group : group + groups].reshape(QB, 1, KD)
            spread = (mine * mask_ref[:, 0:KD][None]).reshape(rows, KD).astype(BF16)
            logits = jnp.dot(spread, kt_s[...], preferred_element_type=F32)
            bias = bias_ref[start : start + rows, :]
            logits = math.sqrt(1.0 / 3.0) * (logits + bias)
            peak = jnp.maximum(jnp.max(logits, 1, keepdims=True), 0.1 * FAR)
            expd = jnp.exp(logits - peak)
            total = jnp.maximum(jnp.sum(expd, 1, keepdims=True), 1e-30)
            weights = (expd * (1.0 / total)).astype(BF16)
            hi, lo = split(peak + jnp.log(total))
            w_s[start : start + rows, :] = weights
            spots = jnp.dot(weights, v_s[...], preferred_element_type=F32)
            tail = jnp.where(lane < 96, spots[:, 384:512], jnp.where(lane < 108, hi, lo))
            own = [
                (
                    tile.reshape(QB, HP, 128)
                    * mask_ref[:, KD + 128 * row : KD + 128 * row + 128][None]
                )
                .reshape(rows, 128)
                .astype(BF16)
                for row, tile in enumerate(
                    [spots[:, 128 * r : 128 * r + 128] for r in range(3)] + [tail]
                )
            ]
            z_s[start // HP : start // HP + QB, :] = jnp.dot(
                gather, jnp.concatenate(own, 1), preferred_element_type=F32
            )

    for half in range(2):
        out_ref = (send_ref, own_ref)[half]
        for step in range(steps):
            index = half * steps + step
            start = index * rows
            copies[index].wait()
            block = pair_v.at[index]
            for i in range(QB):
                row = start + HP * i
                o_s[row : row + HP] = jnp.dot(
                    w_s[row : row + HP, :],
                    block[i // SHARE, i % SHARE],
                    preferred_element_type=F32,
                )
            for r in range(4):
                o_s[pl.ds(start + H + r, QB, stride=HP), :] = z_s[
                    start // HP : start // HP + QB, 128 * r : 128 * r + 128
                ]
            out_ref[step * rows : step * rows + rows, :] = o_s[start : start + rows, :].astype(BF16)


def lane_columns(row):
    head = lax.broadcasted_iota(jnp.int32, (128, 128), 0) - 96
    lane = lax.broadcasted_iota(jnp.int32, (128, 128), 1)
    value = lax.shift_right_logical(lane + (96 if row == 3 else 0), 4)
    if row < 3:
        value = jnp.where(
            lane < 96,
            lax.shift_right_logical(lane, 3),
            lax.shift_right_logical(jnp.maximum(lane - 96, 0) + 32 * row, 4),
        )
        return (head == value).astype(BF16)
    return ((head == value) & (lane < 96)).astype(BF16)


def pair_kernel(own_ref, come_ref, out_ref, a_s, b_s):
    rows = own_ref.shape[0]
    queries = rows // HP
    a_s[...] = own_ref[...].astype(F32)
    b_s[...] = come_ref[...].astype(F32)
    lane = lax.broadcasted_iota(jnp.int32, (queries, 128), 1)
    stat = (lane >= 96) & (lane < 108)

    def level(ref):
        last = ref[pl.ds(HP - 1, queries, stride=HP), :]
        return jnp.where(stat, last + pltpu.roll(last, 128 - H, 1), 0.0)

    first, second = level(a_s), level(b_s)
    top = jnp.maximum(first, second)
    near, far = jnp.exp(first - top), jnp.exp(second - top)
    both = near + far
    share = jnp.where(stat, far / both, 0.0)
    hi, lo = split(top + jnp.log(both))
    pieces = [piece.astype(BF16) for piece in split(share)]
    mixed = []
    for r in range(4):
        columns = lane_columns(r)
        weight = sum(jnp.dot(piece, columns, preferred_element_type=F32) for piece in pieces)
        one = a_s[pl.ds(H + r, queries, stride=HP), :]
        two = b_s[pl.ds(H + r, queries, stride=HP), :]
        mixed.append(one + weight * (two - one))
    mixed[3] = jnp.where(
        stat, hi, jnp.where((lane >= 108) & (lane < 120), pltpu.roll(lo, H, 1), mixed[3])
    )
    own = (
        lax.broadcasted_iota(jnp.int32, (HP, 128), 0) + 96
        == lax.broadcasted_iota(jnp.int32, (HP, 128), 1)
    ).astype(F32)
    column = jnp.sum((share[:, None, :] * own[None]).reshape(rows, 128), 1, keepdims=True)
    one = a_s[...]
    a_s[...] = one + column * (b_s[...] - one)
    for r in range(4):
        a_s[pl.ds(H + r, queries, stride=HP), :] = mixed[r]
    out_ref[...] = a_s[...].astype(BF16)


def inside(x):
    return pltpu.with_memory_space_constraint(x, pltpu.VMEM)


def outside(x):
    return pltpu.with_memory_space_constraint(x, pltpu.HBM)


VMEM = pl.BlockSpec(memory_space=pltpu.VMEM)


def spread_out(query_single, key_single, rows, cols):
    turned = key_single.T
    return pl.pallas_call(
        spread_kernel,
        out_shape=(
            pltpu.VMEM((cols, *query_single.shape), BF16),
            pltpu.VMEM((rows, *turned.shape), BF16),
        ),
        in_specs=[VMEM, VMEM],
        out_specs=(VMEM, VMEM),
        compiler_params=pltpu.CompilerParams(vmem_limit_bytes=4 * 2**20),
    )(outside(query_single), outside(turned))


HBM = pl.BlockSpec(memory_space=pltpu.HBM)


def shadow(qs, others, pair):
    queries, keys = pair.shape[:2]
    pair = pair.reshape(queries // SHARE // 2, 2, SHARE, keys, CZ)
    return pl.pallas_call(
        shadow_kernel,
        out_shape=(
            pltpu.VMEM((queries // SHARE, SHARE, KD), F32),
            pltpu.VMEM((HP, KD + GL + keys + 128), F32),
            pltpu.VMEM(others[10].shape, BF16),
            pltpu.VMEM((queries * HP, keys), F32),
        ),
        in_specs=[VMEM] + [HBM] * 12,
        out_specs=(VMEM,) * 4,
        scratch_shapes=[pltpu.VMEM(x.shape, x.dtype) for x in others[:10]]
        + [
            pltpu.VMEM((queries // 128, 384, 128), F32),
            pltpu.VMEM((HP, queries), F32),
            pltpu.VMEM((KD, queries), F32),
            pltpu.VMEM((HP, CZ), F32),
            pltpu.VMEM((queries, KD), F32),
            pltpu.VMEM((queries // SB, SB // SHARE, SHARE, keys, CZ), BF16),
            pltpu.SemaphoreType.DMA((11,)),
            pltpu.SemaphoreType.DMA((queries // SB,)),
        ],
        cost_estimate=pl.CostEstimate(
            flops=2 * queries * keys * CZ * HP, bytes_accessed=pair.size * 2, transcendentals=0
        ),
        compiler_params=pltpu.CompilerParams(vmem_limit_bytes=16 * 2**20),
    )(qs, *[outside(x) for x in (*others, pair)])


def attend(ks, held, pair):
    queries, keys = pair.shape[:2]
    pair = pair.reshape(queries // SHARE // 2, 2, SHARE, keys, CZ)
    return pl.pallas_call(
        attend_kernel,
        out_shape=(jax.ShapeDtypeStruct((queries * HP // 2, CZ), BF16),) * 2,
        in_specs=[VMEM] * (len(held) + 1) + [HBM],
        out_specs=(VMEM,) * 2,
        scratch_shapes=[
            pltpu.VMEM((keys // 128, 896, 128), F32),
            pltpu.VMEM((HP, keys), F32),
            pltpu.VMEM((KD, keys), BF16),
            pltpu.VMEM((GL, keys), BF16),
            pltpu.VMEM((keys, GL), BF16),
            pltpu.VMEM((queries * HP, keys), BF16),
            pltpu.VMEM((queries, GL), F32),
            pltpu.VMEM((queries * HP, CZ), F32),
            pltpu.VMEM((queries // QB, QB // SHARE, SHARE, keys, CZ), BF16),
            pltpu.SemaphoreType.DMA((queries // QB,)),
        ],
        cost_estimate=pl.CostEstimate(
            flops=2 * queries * HP * keys * (KD + GL + CZ),
            bytes_accessed=queries * keys * CZ * 2,
            transcendentals=queries * HP * keys,
        ),
        compiler_params=pltpu.CompilerParams(vmem_limit_bytes=20 * 2**20),
    )(ks, *[inside(x) for x in held], outside(pair))


def join(own, come):
    return pl.pallas_call(
        pair_kernel,
        out_shape=jax.ShapeDtypeStruct(own.shape, BF16),
        in_specs=[VMEM, VMEM],
        out_specs=VMEM,
        scratch_shapes=[pltpu.VMEM(own.shape, F32)] * 2,
        compiler_params=pltpu.CompilerParams(vmem_limit_bytes=8 * 2**20),
    )(own, come)


def fetch_kernel(after, qf_hbm, em_hbm, ob_hbm, ow_hbm, fr_ref, em_ref, ob_ref, ow_ref, qf_v, sem):
    moves = [(qf_hbm, qf_v), (em_hbm, em_ref), (ob_hbm, ob_ref), (ow_hbm, ow_ref)]
    copies = [pltpu.make_async_copy(*move, sem.at[i]) for i, move in enumerate(moves)]
    for copy in copies:
        copy.start()
    copies[0].wait()
    first = lax.axis_index("col") * SHARE
    shape = (fr_ref.shape[0], 128)
    lane = lax.broadcasted_iota(jnp.int32, shape, 1)
    slot = lane == first + lax.broadcasted_iota(jnp.int32, shape, 0)
    frame = jnp.zeros(shape, F32)
    for j in range(12):
        value = jnp.sum(jnp.where(slot, qf_v[j : j + 1, :], 0.0), 1, keepdims=True)
        frame = jnp.where(lane == j, value, frame)
    fr_ref[...] = frame
    for copy in copies[1:]:
        copy.wait()


def finish_kernel(x_ref, fr_ref, em_ref, ob_ref, ow_ref, out_ref, x_s, p_s, g_s, w_s, f_s):
    share = out_ref.shape[0]
    sources = x_ref.shape[0]
    lane = lax.broadcasted_iota(jnp.int32, (sources, 128), 1)
    stat = (lane >= 96) & (lane < 108)
    for q in range(share):
        block = x_ref[:, HP * q : HP * q + HP, :].reshape(sources * HP, 128)
        x_s[...] = block.astype(F32)
        rows = [x_s[pl.ds(H + r, sources, stride=HP), :] for r in range(4)]
        level = jnp.where(stat, rows[3] + pltpu.roll(rows[3], 128 - H, 1), 0.0)
        part = jnp.exp(level - jnp.max(level, 0, keepdims=True))
        part = jnp.where(stat, part / jnp.sum(part, 0, keepdims=True), 0.0)
        hi, lo = split(part)
        spread = jnp.dot(hi.astype(BF16), em_ref[...], preferred_element_type=F32) + jnp.dot(
            lo.astype(BF16), em_ref[...], preferred_element_type=F32
        )
        for r in range(4):
            g_s[pl.ds(8 * r + q, 1), :] = jnp.sum(
                spread[:, 128 * r : 128 * r + 128] * rows[r], 0, keepdims=True
            )
        w_s[...] = jnp.zeros_like(w_s)
        w_s[0:sources] = part
        turned = w_s[...].T[96:112]
        source = lax.broadcasted_iota(jnp.int32, (128, sources * HP), 0)
        column = lax.broadcasted_iota(jnp.int32, (128, sources * HP), 1)
        repeat = (lax.shift_right_logical(column, 4) == source).astype(BF16)
        own = lax.broadcasted_iota(jnp.int32, (HP, sources * HP), 0) == jnp.bitwise_and(
            lax.broadcasted_iota(jnp.int32, (HP, sources * HP), 1), HP - 1
        )
        paired = jnp.zeros((HP, 128), F32)
        for piece in split(turned):
            wide = jnp.dot(piece.astype(BF16), repeat, preferred_element_type=F32)
            wide = jnp.where(own, wide, 0.0).astype(BF16)
            paired += jnp.dot(wide, block, preferred_element_type=F32)
        p_s[HP * q : HP * q + HP] = paired

    frame = [fr_ref[0:share, j : j + 1] for j in range(12)]
    g = [g_s[8 * r : 8 * r + share, :] for r in range(4)]
    moved = [g[x] - frame[9 + x] for x in range(3)]
    local = [
        frame[x] * moved[0] + frame[3 + x] * moved[1] + frame[6 + x] * moved[2] for x in range(3)
    ]
    lengths = jnp.sqrt(local[0] * local[0] + local[1] * local[1] + local[2] * local[2] + 1.0)
    spot = lax.broadcasted_iota(jnp.int32, (128, 384), 0)
    column = lax.broadcasted_iota(jnp.int32, (128, 384), 1)
    woven = sum(
        jnp.dot(
            local[x].astype(BF16),
            ((column == 3 * spot + x) & (spot < 96)).astype(BF16),
            preferred_element_type=F32,
        )
        for x in range(3)
    )
    f_s[:, 0:384] = woven
    f_s[:, 384:512] = lengths
    for r in range(3):
        f_s[:, 512 + 128 * r : 640 + 128 * r] = pltpu.roll(g[r], 32, 1)
    total = ob_ref[...] + jnp.zeros((share, ob_ref.shape[1]), F32)

    def add(value, low, high):
        return jnp.dot(value.astype(BF16), ow_ref[low:high, :], preferred_element_type=F32)

    total += add(f_s[:, 0:288], 192, 480)
    total += add(f_s[:, 384:480], 480, 576)
    for r in range(3):
        total += add(f_s[:, 512 + 128 * r : 544 + 128 * r], 32 * r, 32 * r + 32)
    total += add(g[3][:, 0:96], 96, 192)
    for h in range(H):
        value = p_s[pl.ds(h, share, stride=HP), :]
        total += add(value, 576 + CZ * h, 576 + CZ * h + CZ)
    out_ref[...] = total.astype(BF16)


def fetch(after, qf, out_weight, out_bias):
    expand = np.zeros((128, GL), np.float32)
    for index, head in enumerate(lane_heads()[0]):
        if head >= 0:
            expand[96 + head, index] = 1.0
    others = [qf, jnp.asarray(expand, BF16), out_bias.reshape(1, -1), out_weight]
    return pl.pallas_call(
        fetch_kernel,
        out_shape=(
            pltpu.VMEM((8, 128), F32),
            *[pltpu.VMEM(x.shape, x.dtype) for x in others[1:]],
        ),
        in_specs=[pl.BlockSpec(memory_space=pl.ANY)] + [HBM] * 4,
        out_specs=(VMEM,) * 4,
        scratch_shapes=[pltpu.VMEM(qf.shape, F32), pltpu.SemaphoreType.DMA((4,))],
        cost_estimate=pl.CostEstimate(flops=0, bytes_accessed=4 * 2**20, transcendentals=0),
        compiler_params=pltpu.CompilerParams(vmem_limit_bytes=4 * 2**20),
    )(after, *[outside(x) for x in others])


def finish(parts, others, columns):
    share = parts.shape[1] // HP
    sources = parts.shape[0]
    return pl.pallas_call(
        finish_kernel,
        out_shape=jax.ShapeDtypeStruct((share, columns), BF16),
        in_specs=[VMEM] * 5,
        out_specs=VMEM,
        scratch_shapes=[
            pltpu.VMEM((sources * HP, 128), F32),
            pltpu.VMEM((share * HP, 128), F32),
            pltpu.VMEM((32, 128), F32),
            pltpu.VMEM((128, 128), F32),
            pltpu.VMEM((share, 896), F32),
        ],
        compiler_params=pltpu.CompilerParams(vmem_limit_bytes=4 * 2**20),
    )(parts, *[inside(x) for x in others])


def body(
    query_single,
    query_frames,
    query_chain,
    key_single,
    key_frames,
    key_chain,
    key_mask,
    pair,
    w_query,
    w_key,
    pair_weight,
    point_raw,
    chain_bias,
    out_weight,
    out_bias,
):
    rows, cols = lax.axis_size("row"), lax.axis_size("col")
    query_parts, key_parts = spread_out(query_single, key_single, rows, cols)
    queries = lax.all_to_all(query_parts, "col", 0, 0, tiled=True).reshape(
        -1, query_single.shape[1]
    )
    keys = lax.all_to_all(key_parts, "row", 0, 0, tiled=True).reshape(-1, key_single.shape[0])
    heads = (lane_heads()[1][None, :] == np.arange(HP)[:, None]).astype(np.float32)
    feats, mask, wk, *held = shadow(
        queries,
        [
            w_query.T, query_frames, query_chain.reshape(1, -1), point_raw.reshape(1, -1),
            chain_bias.reshape(1, -1), jnp.asarray(np.concatenate([depth_mask(), heads], 1)),
            key_frames, key_chain.reshape(1, -1), key_mask.reshape(1, -1), pair_weight.T, w_key.T,
        ],
        pair,
    )
    send, own = attend(keys, [wk, feats, mask, *held], pair)
    come = lax.ppermute(send, "col", [(i, i ^ 1) for i in range(cols)])
    sums = join(own, come).reshape(cols // 2, -1, CZ)
    groups = [list(range(core, cols, 2)) for core in range(2)]
    parts = lax.all_to_all(sums, "col", 0, 0, axis_index_groups=groups, tiled=True)
    others = fetch(sums, query_frames, out_weight, out_bias)
    return finish(parts, others, out_weight.shape[1])


def solution(mesh):
    return jax.shard_map(
        body,
        mesh=mesh,
        in_specs=(
            P(("row", "col"), None),
            P(None, "row"),
            P("row"),
            P("col", "row"),
            P(None, "col"),
            P("col"),
            P("col"),
            P("row", "col", None),
            P(),
            P(),
            P(),
            P(),
            P(),
            P(),
            P(),
        ),
        out_specs=P(("row", "col"), None),
        check_vma=False,
    )
```

```python
import functools
import math

import jax
import jax.numpy as jnp
import numpy as np
from jax import lax
from jax.experimental import pallas as pl
from jax.experimental.pallas import tpu as pltpu
from jax.sharding import PartitionSpec as P

H = 12
C = 16
PQ = 4
PV = 8
CZ = 128
HP = 16
KD = 768
GL = 512
QB = 32
SB = 16
SHARE = 4
FAR = -1e30
F32 = jnp.float32
BF16 = jnp.bfloat16
NT = (((1,), (1,)), ((), ()))
NN = (((1,), (0,)), ((), ()))


def lane_heads():
    head = np.full((GL,), -1)
    for row in range(3):
        head[128 * row : 128 * row + 96] = np.arange(96) // PV
        head[128 * row + 96 : 128 * row + 128] = (np.arange(32) + 32 * row) // C
    head[384:480] = (np.arange(96) + 96) // C
    plain = head.copy()
    head[480:492] = np.arange(H)
    head[492:504] = np.arange(H)
    return plain, head


def depth_mask():
    column = np.arange(KD)
    head = np.full((KD,), -1)
    head[:192] = column[:192] // C
    head[192:624] = ((column[192:624] - 192) % 48) // PQ
    head[624:720] = (column[624:720] - 624) % HP
    mask = (head[None, :] == np.arange(HP)[:, None]).astype(np.float32)
    mask[:, 744] = 1.0
    mask[H:] = 0.0
    return mask


def split(x):
    hi = x.astype(BF16).astype(F32)
    return hi, x - hi


def split3(x):
    hi, rest = split(x)
    mid, rest = split(rest)
    return hi, mid, rest.astype(BF16).astype(F32)


def column_of(row, rows, per):
    shape = (rows, H)
    index = lax.broadcasted_iota(jnp.int32, shape, 0)
    lane = lax.broadcasted_iota(jnp.int32, shape, 1)
    hit = (index >= lane * per) & (index < lane * per + per)
    return jnp.sum(jnp.where(hit, row, 0.0), 1, keepdims=True)


def rotate(points, frames):
    return [
        frames[3 * x : 3 * x + 1] * points[0]
        + frames[3 * x + 1 : 3 * x + 2] * points[1]
        + frames[3 * x + 2 : 3 * x + 3] * points[2]
        + frames[9 + x : 10 + x]
        for x in range(3)
    ]


def take(ref, start, count, stride):
    return jnp.concatenate(
        [ref.at[tile][pl.ds(start, count, stride=stride), :] for tile in range(ref.shape[0])], 1
    )


def put(ref, start, value):
    for tile in range(ref.shape[0]):
        ref[tile, start : start + value.shape[0], :] = value[:, 128 * tile : 128 * tile + 128]


def gamma_of(raw):
    soft = jnp.maximum(raw, 0.0) + jnp.log1p(jnp.exp(-jnp.abs(raw)))
    return (0.5 * math.sqrt(2.0 / (9.0 * PQ))) * soft


def shadow_kernel(
    qs_ref, wq_hbm, qf_hbm, qc_hbm, raw_hbm, cb_hbm, dm_hbm, kf_hbm, kc_hbm, km_hbm, pw_hbm, wk_hbm,
    pair_ref, feat_ref, mask_ref, wk_ref, bias_ref,
    wq_v, qf_v, qc_v, raw_v, cb_v, dm_v, kf_v, kc_v, km_v, pw_v,
    qpt_s, nq_s, qft_s, pw_s, feat_s, pair_v, sem, pair_sem,
):
    moves = [
        (pw_hbm, pw_v), (wq_hbm, wq_v), (qf_hbm, qf_v), (qc_hbm, qc_v), (raw_hbm, raw_v),
        (cb_hbm, cb_v), (dm_hbm, dm_v), (kf_hbm, kf_v), (kc_hbm, kc_v), (km_hbm, km_v),
        (wk_hbm, wk_ref),
    ]
    small = [pltpu.make_async_copy(*move, sem.at[i]) for i, move in enumerate(moves)]
    core = lax.rem(lax.axis_index("col"), 2)
    groups = SB // SHARE
    steps = pair_ref.shape[0] // groups
    copies = [
        pltpu.make_async_copy(
            pair_ref.at[pl.ds(groups * step, groups), 1 - core if half == 0 else core],
            pair_v.at[half * steps + step],
            pair_sem.at[half * steps + step],
        )
        for half in range(2)
        for step in range(steps)
    ]
    for copy in small[:1] + copies[:4] + small[1:] + copies[4:]:
        copy.start()
    small[0].wait()
    pw_s[...] = jnp.zeros_like(pw_s)
    pw_s[0:H] = pw_v[...].astype(F32)
    weight = pw_s[...].astype(BF16)
    for i, copy in enumerate(copies):
        if i == len(copies) // 2:
            for other in small[1:]:
                other.wait()
            prepare_queries(
                qs_ref, wq_v, qf_v, qc_v, raw_v, cb_v, dm_v, feat_s, mask_ref, qpt_s, nq_s, qft_s
            )
            count = feat_ref.shape[0] // 2
            for group in range(2 * count):
                half = core if group % 2 == 0 else 1 - core
                feat_ref[(1 - half) * count + group // 2] = feat_s[
                    SHARE * group : SHARE * group + SHARE, :
                ]
            mask_ref[0:H, KD + GL : KD + GL + 256] = kf_v[...]
            mask_ref[H : H + 1, KD + GL : KD + GL + 256] = kc_v[...].astype(F32)
            mask_ref[H + 1 : H + 2, KD + GL : KD + GL + 256] = km_v[...].astype(F32)
        copy.wait()
        for q in range(SB):
            row = (SB * i + q) * HP
            bias_ref[row : row + HP] = lax.dot_general(
                weight,
                pair_v[i, q // SHARE, q % SHARE],
                NT,
                preferred_element_type=F32,
            )


def prepare_keys(info, gamma16, kt_ref, vt_ref, kpt_s, nk_s):
    frames, chain, kept = info[0:H], info[H : H + 1], info[H + 1 : H + 2]
    kt_ref[0:192] = take(kpt_s, 0, 192, 1).astype(BF16)
    points = rotate([take(kpt_s, 384 + x, 48, 3) for x in range(3)], frames)
    for x in range(3):
        hi, lo = split(points[x])
        kt_ref[192 + 48 * x : 240 + 48 * x] = hi.astype(BF16)
        kt_ref[336 + 48 * x : 384 + 48 * x] = lo.astype(BF16)
        kt_ref[480 + 48 * x : 528 + 48 * x] = hi.astype(BF16)
    put(kpt_s, 816, points[0] * points[0] + points[1] * points[1] + points[2] * points[2])
    nk_s[...] = jnp.zeros_like(nk_s)
    nk_s[0:H] = sum(take(kpt_s, 816 + p, H, PQ) for p in range(PQ))
    for t, part in enumerate(split3(-gamma16 * nk_s[...])):
        kt_ref[624 + HP * t : 640 + HP * t] = part.astype(BF16)
    kt_ref[672:720] = jnp.ones((48, kt_ref.shape[1]), BF16)
    shape = (48, kt_ref.shape[1])
    index = lax.broadcasted_iota(jnp.int32, shape, 0)
    same = (jnp.bitwise_and(index, 7).astype(F32) == chain) & (index < 24)
    away = jnp.where((index == 24) & (kept != 1.0), FAR, 0.0)
    kt_ref[720:768] = (same.astype(F32) + away).astype(BF16)
    points = rotate([take(kpt_s, 528 + x, 96, 3) for x in range(3)], frames)
    for x in range(3):
        vt_ref[128 * x : 128 * x + 96] = points[x].astype(BF16)
        vt_ref[128 * x + 96 : 128 * x + 128] = take(kpt_s, 192 + 32 * x, 32, 1).astype(BF16)
    vt_ref[384:480] = take(kpt_s, 288, 96, 1).astype(BF16)
    vt_ref[480:512] = jnp.zeros((32, vt_ref.shape[1]), BF16)


def prepare_queries(
    qs_ref, wq_ref, qf_ref, qc_ref, raw_ref, cb_ref, dm_ref, qf_s, m_s, qpt_s, nq_s, qft_s
):
    gamma = gamma_of(raw_ref[...])
    gamma16 = column_of(gamma, HP, 1)
    gamma48 = column_of(gamma, H * PQ, PQ)
    put(qpt_s, 0, lax.dot_general(wq_ref[...], qs_ref[...], NT, preferred_element_type=F32))
    frames = qf_ref[...]
    qft_s[0:192] = take(qpt_s, 0, 192, 1).astype(BF16).astype(F32) * (1.0 / math.sqrt(C))
    points = rotate([take(qpt_s, 192 + x, 48, 3) for x in range(3)], frames)
    for x in range(3):
        hi, lo = split(2.0 * gamma48 * points[x])
        qft_s[192 + 48 * x : 240 + 48 * x] = hi
        qft_s[336 + 48 * x : 384 + 48 * x] = hi
        qft_s[480 + 48 * x : 528 + 48 * x] = lo
    put(qpt_s, 336, points[0] * points[0] + points[1] * points[1] + points[2] * points[2])
    nq_s[...] = jnp.zeros_like(nq_s)
    nq_s[0:H] = sum(take(qpt_s, 336 + p, H, PQ) for p in range(PQ))
    qft_s[624:672] = jnp.ones((48, qft_s.shape[1]), F32)
    for t, part in enumerate(split3(-gamma16 * nq_s[...])):
        qft_s[672 + HP * t : 688 + HP * t] = part
    shape = (48, qft_s.shape[1])
    index = lax.broadcasted_iota(jnp.int32, shape, 0)
    same = (jnp.bitwise_and(index, 7) == qc_ref[...]) & (index < 24)
    qft_s[720:768] = (same | (index == 24)).astype(F32)
    qf_s[...] = qft_s[...].T

    m_s[:, 0 : KD + GL] = dm_ref[...]
    m_s[:, KD + GL + 256 :] = jnp.broadcast_to(gamma16, (HP, 128))
    lane = lax.broadcasted_iota(jnp.int32, (HP, 128), 1)
    tail = dm_ref[:, 640:768]
    for t, part in enumerate(split3(column_of(cb_ref[...], HP, 1))):
        tail = jnp.where((lane >= 80 + 8 * t) & (lane < 88 + 8 * t), part, tail)
    m_s[:, 640:768] = tail


def attend_kernel(
    near_ref, far_ref, wk_ref, feat_ref, mask_ref, bias_ref, pair_ref,
    send_ref, own_ref, kpt_s, nk_s, kt_s, vt_s, v_s, w_s, z_s, o_s, ks_s, pair_v, pair_sem,
):
    core = lax.rem(lax.axis_index("col"), 2)
    groups = QB // SHARE
    steps = pair_ref.shape[0] // groups
    copies = {}
    for index in range(2 * steps):
        half, step = divmod(index, steps)
        copies[index] = pltpu.make_async_copy(
            pair_ref.at[pl.ds(groups * step, groups), 1 - core if half == 0 else core],
            pair_v.at[index],
            pair_sem.at[index],
        )
        copies[index].start()
    row = lax.axis_index("row")
    count, part = near_ref.shape[:2]
    for k in range(count):
        x = lax.rem(lax.div(row, 2) + k, count)
        for ref, z in ((near_ref, lax.rem(row, 2)), (far_ref, 1 - lax.rem(row, 2))):
            ks_s[pl.ds(pl.multiple_of((2 * x + z) * part, part), part), :] = ref[k]
    put(kpt_s, 0, jnp.dot(wk_ref[...], ks_s[...], preferred_element_type=F32))
    info = mask_ref[:, KD + GL : KD + GL + 256]
    gamma16 = mask_ref[:, KD + GL + 256 : KD + GL + 257]
    prepare_keys(info, gamma16, kt_s, vt_s, kpt_s, nk_s)
    v_s[...] = vt_s[...].T
    rows = QB * HP
    lane = lax.broadcasted_iota(jnp.int32, (rows, 128), 1)
    gather = (
        lax.shift_right_logical(lax.broadcasted_iota(jnp.int32, (QB, rows), 1), 4)
        == lax.broadcasted_iota(jnp.int32, (QB, rows), 0)
    ).astype(BF16)

    for half in range(2):
        for step in range(steps):
            start = (half * steps + step) * rows
            group = start // (SHARE * HP)
            mine = feat_ref[group : group + groups].reshape(QB, 1, KD)
            spread = (mine * mask_ref[:, 0:KD][None]).reshape(rows, KD).astype(BF16)
            logits = jnp.dot(spread, kt_s[...], preferred_element_type=F32)
            bias = bias_ref[start : start + rows, :]
            logits = math.sqrt(1.0 / 3.0) * (logits + bias)
            peak = jnp.maximum(jnp.max(logits, 1, keepdims=True), 0.1 * FAR)
            expd = jnp.exp(logits - peak)
            total = jnp.maximum(jnp.sum(expd, 1, keepdims=True), 1e-30)
            weights = (expd * (1.0 / total)).astype(BF16)
            hi, lo = split(peak + jnp.log(total))
            w_s[start : start + rows, :] = weights
            spots = jnp.dot(weights, v_s[...], preferred_element_type=F32)
            tail = jnp.where(lane < 96, spots[:, 384:512], jnp.where(lane < 108, hi, lo))
            own = [
                (
                    tile.reshape(QB, HP, 128)
                    * mask_ref[:, KD + 128 * row : KD + 128 * row + 128][None]
                )
                .reshape(rows, 128)
                .astype(BF16)
                for row, tile in enumerate(
                    [spots[:, 128 * r : 128 * r + 128] for r in range(3)] + [tail]
                )
            ]
            z_s[start // HP : start // HP + QB, :] = jnp.dot(
                gather, jnp.concatenate(own, 1), preferred_element_type=F32
            )

    for half in range(2):
        out_ref = (send_ref, own_ref)[half]
        for step in range(steps):
            index = half * steps + step
            start = index * rows
            copies[index].wait()
            block = pair_v.at[index]
            for i in range(QB):
                row = start + HP * i
                o_s[row : row + HP] = jnp.dot(
                    w_s[row : row + HP, :],
                    block[i // SHARE, i % SHARE],
                    preferred_element_type=F32,
                )
            for r in range(4):
                o_s[pl.ds(start + H + r, QB, stride=HP), :] = z_s[
                    start // HP : start // HP + QB, 128 * r : 128 * r + 128
                ]
            out_ref[step * rows : step * rows + rows, :] = o_s[start : start + rows, :].astype(BF16)


def lane_columns(row):
    head = lax.broadcasted_iota(jnp.int32, (128, 128), 0) - 96
    lane = lax.broadcasted_iota(jnp.int32, (128, 128), 1)
    value = lax.shift_right_logical(lane + (96 if row == 3 else 0), 4)
    if row < 3:
        value = jnp.where(
            lane < 96,
            lax.shift_right_logical(lane, 3),
            lax.shift_right_logical(jnp.maximum(lane - 96, 0) + 32 * row, 4),
        )
        return (head == value).astype(BF16)
    return ((head == value) & (lane < 96)).astype(BF16)


def pair_kernel(own_ref, come_ref, out_ref, a_s, b_s):
    rows = own_ref.shape[0]
    queries = rows // HP
    a_s[...] = own_ref[...].astype(F32)
    b_s[...] = come_ref[...].astype(F32)
    lane = lax.broadcasted_iota(jnp.int32, (queries, 128), 1)
    stat = (lane >= 96) & (lane < 108)

    def level(ref):
        last = ref[pl.ds(HP - 1, queries, stride=HP), :]
        return jnp.where(stat, last + pltpu.roll(last, 128 - H, 1), 0.0)

    first, second = level(a_s), level(b_s)
    top = jnp.maximum(first, second)
    near, far = jnp.exp(first - top), jnp.exp(second - top)
    both = near + far
    share = jnp.where(stat, far / both, 0.0)
    hi, lo = split(top + jnp.log(both))
    pieces = [piece.astype(BF16) for piece in split(share)]
    mixed = []
    for r in range(4):
        columns = lane_columns(r)
        weight = sum(jnp.dot(piece, columns, preferred_element_type=F32) for piece in pieces)
        one = a_s[pl.ds(H + r, queries, stride=HP), :]
        two = b_s[pl.ds(H + r, queries, stride=HP), :]
        mixed.append(one + weight * (two - one))
    mixed[3] = jnp.where(
        stat, hi, jnp.where((lane >= 108) & (lane < 120), pltpu.roll(lo, H, 1), mixed[3])
    )
    own = (
        lax.broadcasted_iota(jnp.int32, (HP, 128), 0) + 96
        == lax.broadcasted_iota(jnp.int32, (HP, 128), 1)
    ).astype(F32)
    column = jnp.sum((share[:, None, :] * own[None]).reshape(rows, 128), 1, keepdims=True)
    one = a_s[...]
    a_s[...] = one + column * (b_s[...] - one)
    for r in range(4):
        a_s[pl.ds(H + r, queries, stride=HP), :] = mixed[r]
    out_ref[...] = a_s[...].astype(BF16)


def inside(x):
    return pltpu.with_memory_space_constraint(x, pltpu.VMEM)


def outside(x):
    return pltpu.with_memory_space_constraint(x, pltpu.HBM)


VMEM = pl.BlockSpec(memory_space=pltpu.VMEM)


HBM = pl.BlockSpec(memory_space=pltpu.HBM)


def shadow(qs, others, pair):
    queries, keys = pair.shape[:2]
    pair = pair.reshape(queries // SHARE // 2, 2, SHARE, keys, CZ)
    return pl.pallas_call(
        shadow_kernel,
        out_shape=(
            pltpu.VMEM((queries // SHARE, SHARE, KD), F32),
            pltpu.VMEM((HP, KD + GL + keys + 128), F32),
            pltpu.VMEM(others[10].shape, BF16),
            pltpu.VMEM((queries * HP, keys), F32),
        ),
        in_specs=[VMEM] + [HBM] * 12,
        out_specs=(VMEM,) * 4,
        scratch_shapes=[pltpu.VMEM(x.shape, x.dtype) for x in others[:10]]
        + [
            pltpu.VMEM((queries // 128, 384, 128), F32),
            pltpu.VMEM((HP, queries), F32),
            pltpu.VMEM((KD, queries), F32),
            pltpu.VMEM((HP, CZ), F32),
            pltpu.VMEM((queries, KD), F32),
            pltpu.VMEM((queries // SB, SB // SHARE, SHARE, keys, CZ), BF16),
            pltpu.SemaphoreType.DMA((11,)),
            pltpu.SemaphoreType.DMA((queries // SB,)),
        ],
        cost_estimate=pl.CostEstimate(
            flops=2 * queries * keys * CZ * HP, bytes_accessed=pair.size * 2, transcendentals=0
        ),
        compiler_params=pltpu.CompilerParams(vmem_limit_bytes=16 * 2**20),
    )(qs, *[outside(x) for x in (*others, pair)])


def attend(near, far, held, pair):
    queries, keys = pair.shape[:2]
    pair = pair.reshape(queries // SHARE // 2, 2, SHARE, keys, CZ)
    return pl.pallas_call(
        attend_kernel,
        out_shape=(jax.ShapeDtypeStruct((queries * HP // 2, CZ), BF16),) * 2,
        in_specs=[VMEM] * (len(held) + 2) + [HBM],
        out_specs=(VMEM,) * 2,
        scratch_shapes=[
            pltpu.VMEM((keys // 128, 896, 128), F32),
            pltpu.VMEM((HP, keys), F32),
            pltpu.VMEM((KD, keys), BF16),
            pltpu.VMEM((GL, keys), BF16),
            pltpu.VMEM((keys, GL), BF16),
            pltpu.VMEM((queries * HP, keys), BF16),
            pltpu.VMEM((queries, GL), F32),
            pltpu.VMEM((queries * HP, CZ), F32),
            pltpu.VMEM((384, keys), BF16),
            pltpu.VMEM((queries // QB, QB // SHARE, SHARE, keys, CZ), BF16),
            pltpu.SemaphoreType.DMA((queries // QB,)),
        ],
        cost_estimate=pl.CostEstimate(
            flops=2 * queries * HP * keys * (KD + GL + CZ),
            bytes_accessed=queries * keys * CZ * 2,
            transcendentals=queries * HP * keys,
        ),
        compiler_params=pltpu.CompilerParams(vmem_limit_bytes=20 * 2**20),
    )(near, far, *[inside(x) for x in held], outside(pair))


def join(own, come):
    return pl.pallas_call(
        pair_kernel,
        out_shape=jax.ShapeDtypeStruct(own.shape, BF16),
        in_specs=[VMEM, VMEM],
        out_specs=VMEM,
        scratch_shapes=[pltpu.VMEM(own.shape, F32)] * 2,
        compiler_params=pltpu.CompilerParams(vmem_limit_bytes=8 * 2**20),
    )(own, come)


def fetch_kernel(after, qf_hbm, em_hbm, ob_hbm, ow_hbm, fr_ref, em_ref, ob_ref, ow_ref, qf_v, sem):
    moves = [(qf_hbm, qf_v), (em_hbm, em_ref), (ob_hbm, ob_ref), (ow_hbm, ow_ref)]
    copies = [pltpu.make_async_copy(*move, sem.at[i]) for i, move in enumerate(moves)]
    for copy in copies:
        copy.start()
    copies[0].wait()
    first = lax.axis_index("col") * SHARE
    shape = (fr_ref.shape[0], 128)
    lane = lax.broadcasted_iota(jnp.int32, shape, 1)
    slot = lane == first + lax.broadcasted_iota(jnp.int32, shape, 0)
    frame = jnp.zeros(shape, F32)
    for j in range(12):
        value = jnp.sum(jnp.where(slot, qf_v[j : j + 1, :], 0.0), 1, keepdims=True)
        frame = jnp.where(lane == j, value, frame)
    fr_ref[...] = frame
    for copy in copies[1:]:
        copy.wait()


def finish_kernel(x_ref, fr_ref, em_ref, ob_ref, ow_ref, out_ref, x_s, p_s, g_s, w_s, f_s):
    share = out_ref.shape[0]
    sources = x_ref.shape[0]
    lane = lax.broadcasted_iota(jnp.int32, (sources, 128), 1)
    stat = (lane >= 96) & (lane < 108)
    for q in range(share):
        block = x_ref[:, HP * q : HP * q + HP, :].reshape(sources * HP, 128)
        x_s[...] = block.astype(F32)
        rows = [x_s[pl.ds(H + r, sources, stride=HP), :] for r in range(4)]
        level = jnp.where(stat, rows[3] + pltpu.roll(rows[3], 128 - H, 1), 0.0)
        part = jnp.exp(level - jnp.max(level, 0, keepdims=True))
        part = jnp.where(stat, part / jnp.sum(part, 0, keepdims=True), 0.0)
        hi, lo = split(part)
        spread = jnp.dot(hi.astype(BF16), em_ref[...], preferred_element_type=F32) + jnp.dot(
            lo.astype(BF16), em_ref[...], preferred_element_type=F32
        )
        for r in range(4):
            g_s[pl.ds(8 * r + q, 1), :] = jnp.sum(
                spread[:, 128 * r : 128 * r + 128] * rows[r], 0, keepdims=True
            )
        w_s[...] = jnp.zeros_like(w_s)
        w_s[0:sources] = part
        turned = w_s[...].T[96:112]
        source = lax.broadcasted_iota(jnp.int32, (128, sources * HP), 0)
        column = lax.broadcasted_iota(jnp.int32, (128, sources * HP), 1)
        repeat = (lax.shift_right_logical(column, 4) == source).astype(BF16)
        own = lax.broadcasted_iota(jnp.int32, (HP, sources * HP), 0) == jnp.bitwise_and(
            lax.broadcasted_iota(jnp.int32, (HP, sources * HP), 1), HP - 1
        )
        paired = jnp.zeros((HP, 128), F32)
        for piece in split(turned):
            wide = jnp.dot(piece.astype(BF16), repeat, preferred_element_type=F32)
            wide = jnp.where(own, wide, 0.0).astype(BF16)
            paired += jnp.dot(wide, block, preferred_element_type=F32)
        p_s[HP * q : HP * q + HP] = paired

    frame = [fr_ref[0:share, j : j + 1] for j in range(12)]
    g = [g_s[8 * r : 8 * r + share, :] for r in range(4)]
    moved = [g[x] - frame[9 + x] for x in range(3)]
    local = [
        frame[x] * moved[0] + frame[3 + x] * moved[1] + frame[6 + x] * moved[2] for x in range(3)
    ]
    lengths = jnp.sqrt(local[0] * local[0] + local[1] * local[1] + local[2] * local[2] + 1.0)
    spot = lax.broadcasted_iota(jnp.int32, (128, 384), 0)
    column = lax.broadcasted_iota(jnp.int32, (128, 384), 1)
    woven = sum(
        jnp.dot(
            local[x].astype(BF16),
            ((column == 3 * spot + x) & (spot < 96)).astype(BF16),
            preferred_element_type=F32,
        )
        for x in range(3)
    )
    f_s[:, 0:384] = woven
    f_s[:, 384:512] = lengths
    for r in range(3):
        f_s[:, 512 + 128 * r : 640 + 128 * r] = pltpu.roll(g[r], 32, 1)
    total = ob_ref[...] + jnp.zeros((share, ob_ref.shape[1]), F32)

    def add(value, low, high):
        return jnp.dot(value.astype(BF16), ow_ref[low:high, :], preferred_element_type=F32)

    total += add(f_s[:, 0:288], 192, 480)
    total += add(f_s[:, 384:480], 480, 576)
    for r in range(3):
        total += add(f_s[:, 512 + 128 * r : 544 + 128 * r], 32 * r, 32 * r + 32)
    total += add(g[3][:, 0:96], 96, 192)
    for h in range(H):
        value = p_s[pl.ds(h, share, stride=HP), :]
        total += add(value, 576 + CZ * h, 576 + CZ * h + CZ)
    out_ref[...] = total.astype(BF16)


def fetch(after, qf, out_weight, out_bias):
    expand = np.zeros((128, GL), np.float32)
    for index, head in enumerate(lane_heads()[0]):
        if head >= 0:
            expand[96 + head, index] = 1.0
    others = [qf, jnp.asarray(expand, BF16), out_bias.reshape(1, -1), out_weight]
    return pl.pallas_call(
        fetch_kernel,
        out_shape=(
            pltpu.VMEM((8, 128), F32),
            *[pltpu.VMEM(x.shape, x.dtype) for x in others[1:]],
        ),
        in_specs=[pl.BlockSpec(memory_space=pl.ANY)] + [HBM] * 4,
        out_specs=(VMEM,) * 4,
        scratch_shapes=[pltpu.VMEM(qf.shape, F32), pltpu.SemaphoreType.DMA((4,))],
        cost_estimate=pl.CostEstimate(flops=0, bytes_accessed=4 * 2**20, transcendentals=0),
        compiler_params=pltpu.CompilerParams(vmem_limit_bytes=4 * 2**20),
    )(after, *[outside(x) for x in others])


def finish(parts, others, columns):
    share = parts.shape[1] // HP
    sources = parts.shape[0]
    return pl.pallas_call(
        finish_kernel,
        out_shape=jax.ShapeDtypeStruct((share, columns), BF16),
        in_specs=[VMEM] * 5,
        out_specs=VMEM,
        scratch_shapes=[
            pltpu.VMEM((sources * HP, 128), F32),
            pltpu.VMEM((share * HP, 128), F32),
            pltpu.VMEM((32, 128), F32),
            pltpu.VMEM((128, 128), F32),
            pltpu.VMEM((share, 896), F32),
        ],
        compiler_params=pltpu.CompilerParams(vmem_limit_bytes=4 * 2**20),
    )(parts, *[inside(x) for x in others])


def body(
    query_single,
    query_frames,
    query_chain,
    key_single,
    key_frames,
    key_chain,
    key_mask,
    pair,
    w_query,
    w_key,
    pair_weight,
    point_raw,
    chain_bias,
    out_weight,
    out_bias,
):
    rows, cols = lax.axis_size("row"), lax.axis_size("col")
    turned = key_single.T
    chips = rows // 2
    near = jnp.stack(
        [turned]
        + [
            lax.ppermute(
                turned, "row", [((i + 2 * k) % rows, i) for i in range(rows)]
            )
            for k in range(1, chips)
        ]
    )
    far = lax.ppermute(near, "row", [(i, i ^ 1) for i in range(rows)])
    queries = lax.all_to_all(
        jnp.broadcast_to(query_single[None], (cols, *query_single.shape)), "col", 0, 0, tiled=True
    ).reshape(-1, query_single.shape[1])
    heads = (lane_heads()[1][None, :] == np.arange(HP)[:, None]).astype(np.float32)
    feats, mask, wk, *held = shadow(
        queries,
        [
            w_query.T, query_frames, query_chain.reshape(1, -1), point_raw.reshape(1, -1),
            chain_bias.reshape(1, -1), jnp.asarray(np.concatenate([depth_mask(), heads], 1)),
            key_frames, key_chain.reshape(1, -1), key_mask.reshape(1, -1), pair_weight.T, w_key.T,
        ],
        pair,
    )
    send, own = attend(near, far, [wk, feats, mask, *held], pair)
    come = lax.ppermute(send, "col", [(i, i ^ 1) for i in range(cols)])
    sums = join(own, come).reshape(cols // 2, -1, CZ)
    groups = [list(range(core, cols, 2)) for core in range(2)]
    parts = lax.all_to_all(sums, "col", 0, 0, axis_index_groups=groups, tiled=True)
    others = fetch(sums, query_frames, out_weight, out_bias)
    return finish(parts, others, out_weight.shape[1])


def solution(mesh):
    return jax.shard_map(
        body,
        mesh=mesh,
        in_specs=(
            P(("row", "col"), None),
            P(None, "row"),
            P("row"),
            P("col", "row"),
            P(None, "col"),
            P("col"),
            P("col"),
            P("row", "col", None),
            P(),
            P(),
            P(),
            P(),
            P(),
            P(),
            P(),
        ),
        out_specs=P(("row", "col"), None),
        check_vma=False,
    )
```

```python
import functools
import math

import jax
import jax.numpy as jnp
import numpy as np
from jax import lax
from jax.experimental import pallas as pl
from jax.experimental.pallas import tpu as pltpu
from jax.sharding import PartitionSpec as P

H = 12
C = 16
PQ = 4
PV = 8
CZ = 128
HP = 16
KD = 768
GL = 512
QB = 32
SB = 16
SHARE = 4
FAR = -1e30
F32 = jnp.float32
BF16 = jnp.bfloat16
NT = (((1,), (1,)), ((), ()))
NN = (((1,), (0,)), ((), ()))


def lane_heads():
    head = np.full((GL,), -1)
    for row in range(3):
        head[128 * row : 128 * row + 96] = np.arange(96) // PV
        head[128 * row + 96 : 128 * row + 128] = (np.arange(32) + 32 * row) // C
    head[384:480] = (np.arange(96) + 96) // C
    plain = head.copy()
    head[480:492] = np.arange(H)
    head[492:504] = np.arange(H)
    return plain, head


def depth_mask():
    column = np.arange(KD)
    head = np.full((KD,), -1)
    head[:192] = column[:192] // C
    head[192:624] = ((column[192:624] - 192) % 48) // PQ
    head[624:720] = (column[624:720] - 624) % HP
    mask = (head[None, :] == np.arange(HP)[:, None]).astype(np.float32)
    mask[:, 744] = 1.0
    mask[H:] = 0.0
    return mask


def split(x):
    hi = x.astype(BF16).astype(F32)
    return hi, x - hi


def split3(x):
    hi, rest = split(x)
    mid, rest = split(rest)
    return hi, mid, rest.astype(BF16).astype(F32)


def column_of(row, rows, per):
    shape = (rows, H)
    index = lax.broadcasted_iota(jnp.int32, shape, 0)
    lane = lax.broadcasted_iota(jnp.int32, shape, 1)
    hit = (index >= lane * per) & (index < lane * per + per)
    return jnp.sum(jnp.where(hit, row, 0.0), 1, keepdims=True)


def rotate(points, frames):
    return [
        frames[3 * x : 3 * x + 1] * points[0]
        + frames[3 * x + 1 : 3 * x + 2] * points[1]
        + frames[3 * x + 2 : 3 * x + 3] * points[2]
        + frames[9 + x : 10 + x]
        for x in range(3)
    ]


def take(ref, start, count, stride):
    return jnp.concatenate(
        [ref.at[tile][pl.ds(start, count, stride=stride), :] for tile in range(ref.shape[0])], 1
    )


def put(ref, start, value):
    for tile in range(ref.shape[0]):
        ref[tile, start : start + value.shape[0], :] = value[:, 128 * tile : 128 * tile + 128]


def gamma_of(raw):
    soft = jnp.maximum(raw, 0.0) + jnp.log1p(jnp.exp(-jnp.abs(raw)))
    return (0.5 * math.sqrt(2.0 / (9.0 * PQ))) * soft


def shadow_kernel(
    raw_hbm, cb_hbm, dm_hbm, kf_hbm, kc_hbm, km_hbm, qf_hbm, qc_hbm, pw_hbm, wk_hbm, wq_hbm,
    pair_ref, mask_ref, wk_ref, wq_ref, bias_ref,
    raw_v, cb_v, dm_v, kf_v, kc_v, km_v, qf_v, qc_v, pw_v, pw_s, pair_v, sem, pair_sem,
):
    moves = [
        (pw_hbm, pw_v), (raw_hbm, raw_v), (cb_hbm, cb_v), (dm_hbm, dm_v), (kf_hbm, kf_v),
        (kc_hbm, kc_v), (km_hbm, km_v), (qf_hbm, qf_v), (qc_hbm, qc_v), (wk_hbm, wk_ref),
        (wq_hbm, wq_ref),
    ]
    small = [pltpu.make_async_copy(*move, sem.at[i]) for i, move in enumerate(moves)]
    core = lax.rem(lax.axis_index("col"), 2)
    groups = SB // SHARE
    steps = pair_ref.shape[0] // groups
    copies = [
        pltpu.make_async_copy(
            pair_ref.at[pl.ds(groups * step, groups), 1 - core if half == 0 else core],
            pair_v.at[half * steps + step],
            pair_sem.at[half * steps + step],
        )
        for half in range(2)
        for step in range(steps)
    ]
    for copy in small[:1] + copies[:4] + small[1:] + copies[4:]:
        copy.start()
    small[0].wait()
    pw_s[...] = jnp.zeros_like(pw_s)
    pw_s[0:H] = pw_v[...].astype(F32)
    weight = pw_s[...].astype(BF16)
    for i, copy in enumerate(copies):
        if i == len(copies) // 2:
            for other in small[1:]:
                other.wait()
            prepare_masks(raw_v, cb_v, dm_v, kf_v, kc_v, km_v, qf_v, qc_v, mask_ref)
        copy.wait()
        for q in range(SB):
            row = (SB * i + q) * HP
            bias_ref[row : row + HP] = lax.dot_general(
                weight,
                pair_v[i, q // SHARE, q % SHARE],
                NT,
                preferred_element_type=F32,
            )


def prepare_masks(raw_v, cb_v, dm_v, kf_v, kc_v, km_v, qf_v, qc_v, mask_ref):
    mask_ref[:, 0 : KD + GL] = dm_v[...]
    lane = lax.broadcasted_iota(jnp.int32, (HP, 128), 1)
    tail = dm_v[:, 640:768]
    for t, part in enumerate(split3(column_of(cb_v[...], HP, 1))):
        tail = jnp.where((lane >= 80 + 8 * t) & (lane < 88 + 8 * t), part, tail)
    mask_ref[:, 640:768] = tail
    at = KD + GL
    mask_ref[0:H, at : at + 256] = kf_v[...]
    mask_ref[H : H + 1, at : at + 256] = kc_v[...].astype(F32)
    mask_ref[H + 1 : H + 2, at : at + 256] = km_v[...].astype(F32)
    gamma = column_of(gamma_of(raw_v[...]), HP, 1)
    mask_ref[:, at + 256 : at + 384] = jnp.broadcast_to(gamma, (HP, 128))
    mask_ref[0:H, at + 384 : at + 512] = qf_v[...]
    mask_ref[H : H + 1, at + 384 : at + 512] = qc_v[...].astype(F32)
    mask_ref[H + 1 : H + 2, at + 384 : at + 384 + H] = raw_v[...]


def prepare_keys(info, gamma16, kt_ref, vt_ref, kpt_s, nk_s):
    frames, chain, kept = info[0:H], info[H : H + 1], info[H + 1 : H + 2]
    kt_ref[0:192] = take(kpt_s, 0, 192, 1).astype(BF16)
    points = rotate([take(kpt_s, 384 + x, 48, 3) for x in range(3)], frames)
    for x in range(3):
        hi, lo = split(points[x])
        kt_ref[192 + 48 * x : 240 + 48 * x] = hi.astype(BF16)
        kt_ref[336 + 48 * x : 384 + 48 * x] = lo.astype(BF16)
        kt_ref[480 + 48 * x : 528 + 48 * x] = hi.astype(BF16)
    put(kpt_s, 816, points[0] * points[0] + points[1] * points[1] + points[2] * points[2])
    nk_s[...] = jnp.zeros_like(nk_s)
    nk_s[0:H] = sum(take(kpt_s, 816 + p, H, PQ) for p in range(PQ))
    for t, part in enumerate(split3(-gamma16 * nk_s[...])):
        kt_ref[624 + HP * t : 640 + HP * t] = part.astype(BF16)
    kt_ref[672:720] = jnp.ones((48, kt_ref.shape[1]), BF16)
    shape = (48, kt_ref.shape[1])
    index = lax.broadcasted_iota(jnp.int32, shape, 0)
    same = (jnp.bitwise_and(index, 7).astype(F32) == chain) & (index < 24)
    away = jnp.where((index == 24) & (kept != 1.0), FAR, 0.0)
    kt_ref[720:768] = (same.astype(F32) + away).astype(BF16)
    points = rotate([take(kpt_s, 528 + x, 96, 3) for x in range(3)], frames)
    for x in range(3):
        vt_ref[128 * x : 128 * x + 96] = points[x].astype(BF16)
        vt_ref[128 * x + 96 : 128 * x + 128] = take(kpt_s, 192 + 32 * x, 32, 1).astype(BF16)
    vt_ref[384:480] = take(kpt_s, 288, 96, 1).astype(BF16)
    vt_ref[480:512] = jnp.zeros((32, vt_ref.shape[1]), BF16)


def prepare_queries(qs_ref, wq_ref, info, gamma16, qpt_s, nq_s, qft_s, qf_s):
    gamma48 = column_of(gamma_of(info[H + 1 : H + 2, 0:H]), H * PQ, PQ)
    put(qpt_s, 0, lax.dot_general(wq_ref[...], qs_ref[...], NT, preferred_element_type=F32))
    frames = info[0:H]
    qft_s[0:192] = take(qpt_s, 0, 192, 1).astype(BF16).astype(F32) * (1.0 / math.sqrt(C))
    points = rotate([take(qpt_s, 192 + x, 48, 3) for x in range(3)], frames)
    for x in range(3):
        hi, lo = split(2.0 * gamma48 * points[x])
        qft_s[192 + 48 * x : 240 + 48 * x] = hi
        qft_s[336 + 48 * x : 384 + 48 * x] = hi
        qft_s[480 + 48 * x : 528 + 48 * x] = lo
    put(qpt_s, 336, points[0] * points[0] + points[1] * points[1] + points[2] * points[2])
    nq_s[...] = jnp.zeros_like(nq_s)
    nq_s[0:H] = sum(take(qpt_s, 336 + p, H, PQ) for p in range(PQ))
    qft_s[624:672] = jnp.ones((48, qft_s.shape[1]), F32)
    for t, part in enumerate(split3(-gamma16 * nq_s[...])):
        qft_s[672 + HP * t : 688 + HP * t] = part
    shape = (48, qft_s.shape[1])
    index = lax.broadcasted_iota(jnp.int32, shape, 0)
    same = (jnp.bitwise_and(index, 7).astype(F32) == info[H : H + 1]) & (index < 24)
    qft_s[720:768] = (same | (index == 24)).astype(F32)
    qf_s[...] = qft_s[...].T


def attend_kernel(
    near_ref, far_ref, qs_ref, wk_ref, mask_ref, wq_ref, bias_ref, pair_ref,
    send_ref, own_ref, kpt_s, nk_s, kt_s, vt_s, v_s, w_s, z_s, o_s, ks_s,
    qpt_s, nq_s, qft_s, qf_s, feat_s, pair_v, pair_sem,
):
    core = lax.rem(lax.axis_index("col"), 2)
    groups = QB // SHARE
    steps = pair_ref.shape[0] // groups
    copies = {}
    for index in range(2 * steps):
        half, step = divmod(index, steps)
        copies[index] = pltpu.make_async_copy(
            pair_ref.at[pl.ds(groups * step, groups), 1 - core if half == 0 else core],
            pair_v.at[index],
            pair_sem.at[index],
        )
        copies[index].start()
    row = lax.axis_index("row")
    count, part = near_ref.shape[:2]
    for k in range(count):
        x = lax.rem(lax.div(row, 2) + k, count)
        for ref, z in ((near_ref, lax.rem(row, 2)), (far_ref, 1 - lax.rem(row, 2))):
            ks_s[pl.ds(pl.multiple_of((2 * x + z) * part, part), part), :] = ref[k]
    put(kpt_s, 0, jnp.dot(wk_ref[...], ks_s[...], preferred_element_type=F32))
    info = mask_ref[:, KD + GL : KD + GL + 256]
    gamma16 = mask_ref[:, KD + GL + 256 : KD + GL + 257]
    prepare_keys(info, gamma16, kt_s, vt_s, kpt_s, nk_s)
    info = mask_ref[:, KD + GL + 384 : KD + GL + 512]
    prepare_queries(qs_ref, wq_ref, info, gamma16, qpt_s, nq_s, qft_s, qf_s)
    half_groups = feat_s.shape[0] // 2
    for group in range(2 * half_groups):
        half = core if group % 2 == 0 else 1 - core
        feat_s[(1 - half) * half_groups + group // 2] = qf_s[SHARE * group : SHARE * group + SHARE]
    v_s[...] = vt_s[...].T
    rows = QB * HP
    lane = lax.broadcasted_iota(jnp.int32, (rows, 128), 1)
    gather = (
        lax.shift_right_logical(lax.broadcasted_iota(jnp.int32, (QB, rows), 1), 4)
        == lax.broadcasted_iota(jnp.int32, (QB, rows), 0)
    ).astype(BF16)

    for half in range(2):
        for step in range(steps):
            start = (half * steps + step) * rows
            group = start // (SHARE * HP)
            mine = feat_s[group : group + groups].reshape(QB, 1, KD)
            spread = (mine * mask_ref[:, 0:KD][None]).reshape(rows, KD).astype(BF16)
            logits = jnp.dot(spread, kt_s[...], preferred_element_type=F32)
            bias = bias_ref[start : start + rows, :]
            logits = math.sqrt(1.0 / 3.0) * (logits + bias)
            peak = jnp.maximum(jnp.max(logits, 1, keepdims=True), 0.1 * FAR)
            expd = jnp.exp(logits - peak)
            total = jnp.maximum(jnp.sum(expd, 1, keepdims=True), 1e-30)
            weights = (expd * (1.0 / total)).astype(BF16)
            hi, lo = split(peak + jnp.log(total))
            w_s[start : start + rows, :] = weights
            spots = jnp.dot(weights, v_s[...], preferred_element_type=F32)
            tail = jnp.where(lane < 96, spots[:, 384:512], jnp.where(lane < 108, hi, lo))
            own = [
                (
                    tile.reshape(QB, HP, 128)
                    * mask_ref[:, KD + 128 * row : KD + 128 * row + 128][None]
                )
                .reshape(rows, 128)
                .astype(BF16)
                for row, tile in enumerate(
                    [spots[:, 128 * r : 128 * r + 128] for r in range(3)] + [tail]
                )
            ]
            z_s[start // HP : start // HP + QB, :] = jnp.dot(
                gather, jnp.concatenate(own, 1), preferred_element_type=F32
            )

    for half in range(2):
        out_ref = (send_ref, own_ref)[half]
        for step in range(steps):
            index = half * steps + step
            start = index * rows
            copies[index].wait()
            block = pair_v.at[index]
            for i in range(QB):
                row = start + HP * i
                o_s[row : row + HP] = jnp.dot(
                    w_s[row : row + HP, :],
                    block[i // SHARE, i % SHARE],
                    preferred_element_type=F32,
                )
            for r in range(4):
                o_s[pl.ds(start + H + r, QB, stride=HP), :] = z_s[
                    start // HP : start // HP + QB, 128 * r : 128 * r + 128
                ]
            out_ref[step * rows : step * rows + rows, :] = o_s[start : start + rows, :].astype(BF16)


def lane_columns(row):
    head = lax.broadcasted_iota(jnp.int32, (128, 128), 0) - 96
    lane = lax.broadcasted_iota(jnp.int32, (128, 128), 1)
    value = lax.shift_right_logical(lane + (96 if row == 3 else 0), 4)
    if row < 3:
        value = jnp.where(
            lane < 96,
            lax.shift_right_logical(lane, 3),
            lax.shift_right_logical(jnp.maximum(lane - 96, 0) + 32 * row, 4),
        )
        return (head == value).astype(BF16)
    return ((head == value) & (lane < 96)).astype(BF16)


def merge(sources, held):
    rows = sources[0].shape[0]
    queries = rows // HP
    for source, ref in zip(sources, held, strict=True):
        ref[...] = source[...].astype(F32)
    lane = lax.broadcasted_iota(jnp.int32, (queries, 128), 1)
    stat = (lane >= 96) & (lane < 108)

    def level(ref):
        last = ref[pl.ds(HP - 1, queries, stride=HP), :]
        return jnp.where(stat, last + pltpu.roll(last, 128 - H, 1), 0.0)

    levels = [level(ref) for ref in held]
    top = functools.reduce(jnp.maximum, levels)
    shares = [jnp.exp(one - top) for one in levels]
    total = sum(shares)
    hi, lo = split(top + jnp.log(total))
    shares = [jnp.where(stat, one / total, 0.0) for one in shares]
    own = (
        lax.broadcasted_iota(jnp.int32, (HP, 128), 0) + 96
        == lax.broadcasted_iota(jnp.int32, (HP, 128), 1)
    ).astype(F32)
    mixed = [held[0][pl.ds(H + r, queries, stride=HP), :] for r in range(4)]
    base = held[0][...]
    result = base
    for share, ref in zip(shares[1:], held[1:], strict=True):
        pieces = [piece.astype(BF16) for piece in split(share)]
        for r in range(4):
            columns = lane_columns(r)
            weight = sum(jnp.dot(piece, columns, preferred_element_type=F32) for piece in pieces)
            near = held[0][pl.ds(H + r, queries, stride=HP), :]
            far = ref[pl.ds(H + r, queries, stride=HP), :]
            mixed[r] = mixed[r] + weight * (far - near)
        column = jnp.sum((share[:, None, :] * own[None]).reshape(rows, 128), 1, keepdims=True)
        result = result + column * (ref[...] - base)
    mixed[3] = jnp.where(
        stat, hi, jnp.where((lane >= 108) & (lane < 120), pltpu.roll(lo, H, 1), mixed[3])
    )
    held[0][...] = result
    for r in range(4):
        held[0][pl.ds(H + r, queries, stride=HP), :] = mixed[r]


def join_kernel(count, first, *refs):
    sources, parts, held = refs[:count], refs[count:-count], refs[-count:]
    rows = sources[0].shape[0]
    merge(sources, held)
    place = first(lax.axis_index("col"))
    size = rows // len(parts)
    for k, part in enumerate(parts):
        start = pl.multiple_of(lax.rem(place + k, len(parts)) * size, size)
        part[...] = held[0][pl.ds(start, size), :].astype(BF16)


def inside(x):
    return pltpu.with_memory_space_constraint(x, pltpu.VMEM)


def outside(x):
    return pltpu.with_memory_space_constraint(x, pltpu.HBM)


VMEM = pl.BlockSpec(memory_space=pltpu.VMEM)


HBM = pl.BlockSpec(memory_space=pltpu.HBM)


def shadow(others, pair):
    queries, keys = pair.shape[:2]
    pair = pair.reshape(queries // SHARE // 2, 2, SHARE, keys, CZ)
    return pl.pallas_call(
        shadow_kernel,
        out_shape=(
            pltpu.VMEM((HP, KD + GL + keys + 256), F32),
            pltpu.VMEM(others[9].shape, BF16),
            pltpu.VMEM(others[10].shape, BF16),
            pltpu.VMEM((queries * HP, keys), F32),
        ),
        in_specs=[HBM] * 12,
        out_specs=(VMEM,) * 4,
        scratch_shapes=[pltpu.VMEM(x.shape, x.dtype) for x in others[:9]]
        + [
            pltpu.VMEM((HP, CZ), F32),
            pltpu.VMEM((queries // SB, SB // SHARE, SHARE, keys, CZ), BF16),
            pltpu.SemaphoreType.DMA((11,)),
            pltpu.SemaphoreType.DMA((queries // SB,)),
        ],
        cost_estimate=pl.CostEstimate(
            flops=2 * queries * keys * CZ * HP, bytes_accessed=pair.size * 2, transcendentals=0
        ),
        compiler_params=pltpu.CompilerParams(vmem_limit_bytes=16 * 2**20),
    )(*[outside(x) for x in (*others, pair)])


def attend(came, held, pair):
    queries, keys = pair.shape[:2]
    pair = pair.reshape(queries // SHARE // 2, 2, SHARE, keys, CZ)
    return pl.pallas_call(
        attend_kernel,
        out_shape=(jax.ShapeDtypeStruct((queries * HP // 2, CZ), BF16),) * 2,
        in_specs=[VMEM] * (len(held) + 3) + [HBM],
        out_specs=(VMEM,) * 2,
        scratch_shapes=[
            pltpu.VMEM((keys // 128, 896, 128), F32),
            pltpu.VMEM((HP, keys), F32),
            pltpu.VMEM((KD, keys), BF16),
            pltpu.VMEM((GL, keys), BF16),
            pltpu.VMEM((keys, GL), BF16),
            pltpu.VMEM((queries * HP, keys), BF16),
            pltpu.VMEM((queries, GL), F32),
            pltpu.VMEM((queries * HP, CZ), F32),
            pltpu.VMEM((384, keys), BF16),
            pltpu.VMEM((queries // 128, 384, 128), F32),
            pltpu.VMEM((HP, queries), F32),
            pltpu.VMEM((KD, queries), F32),
            pltpu.VMEM((queries, KD), F32),
            pltpu.VMEM((queries // SHARE, SHARE, KD), F32),
            pltpu.VMEM((queries // QB, QB // SHARE, SHARE, keys, CZ), BF16),
            pltpu.SemaphoreType.DMA((queries // QB,)),
        ],
        cost_estimate=pl.CostEstimate(
            flops=2 * queries * HP * keys * (KD + GL + CZ),
            bytes_accessed=queries * keys * CZ * 2,
            transcendentals=queries * HP * keys,
        ),
        compiler_params=pltpu.CompilerParams(vmem_limit_bytes=20 * 2**20),
    )(*came, *[inside(x) for x in held], outside(pair))


def join(sources, first, parts):
    rows, columns = sources[0].shape
    return pl.pallas_call(
        functools.partial(join_kernel, len(sources), first),
        out_shape=(jax.ShapeDtypeStruct((rows // parts, columns), BF16),) * parts,
        in_specs=[VMEM] * len(sources),
        out_specs=(VMEM,) * parts,
        scratch_shapes=[pltpu.VMEM((rows, columns), F32)] * len(sources),
        compiler_params=pltpu.CompilerParams(vmem_limit_bytes=8 * 2**20),
    )(*sources)


def exchange(parts, width, apart, count):
    def to(i, k):
        place = (i // apart) % width
        return i + ((place + k) % width - place) * apart

    return [parts[0]] + [
        lax.ppermute(parts[k], "col", [(i, to(i, k)) for i in range(count)])
        for k in range(1, width)
    ]


def fetch_kernel(after, qf_hbm, ob_hbm, ow_hbm, fr_ref, ob_ref, ow_ref, qf_v, sem):
    moves = [(qf_hbm, qf_v), (ob_hbm, ob_ref), (ow_hbm, ow_ref)]
    copies = [pltpu.make_async_copy(*move, sem.at[i]) for i, move in enumerate(moves)]
    for copy in copies:
        copy.start()
    copies[0].wait()
    first = lax.axis_index("col") * SHARE
    shape = (fr_ref.shape[0], 128)
    lane = lax.broadcasted_iota(jnp.int32, shape, 1)
    slot = lane == first + lax.broadcasted_iota(jnp.int32, shape, 0)
    frame = jnp.zeros(shape, F32)
    for j in range(12):
        value = jnp.sum(jnp.where(slot, qf_v[j : j + 1, :], 0.0), 1, keepdims=True)
        frame = jnp.where(lane == j, value, frame)
    fr_ref[...] = frame
    for copy in copies[1:]:
        copy.wait()


def finish_kernel(sources, *refs):
    parts, refs = refs[:sources], refs[sources:]
    fr_ref, ob_ref, ow_ref, out_ref, f_s, *held = refs
    share = out_ref.shape[0]
    merge(parts, held)
    sums = held[0]
    frame = [fr_ref[0:share, j : j + 1] for j in range(12)]
    g = [sums[pl.ds(H + r, share, stride=HP), :] for r in range(4)]
    moved = [g[x] - frame[9 + x] for x in range(3)]
    local = [
        frame[x] * moved[0] + frame[3 + x] * moved[1] + frame[6 + x] * moved[2] for x in range(3)
    ]
    lengths = jnp.sqrt(local[0] * local[0] + local[1] * local[1] + local[2] * local[2] + 1.0)
    spot = lax.broadcasted_iota(jnp.int32, (128, 384), 0)
    column = lax.broadcasted_iota(jnp.int32, (128, 384), 1)
    woven = sum(
        jnp.dot(
            local[x].astype(BF16),
            ((column == 3 * spot + x) & (spot < 96)).astype(BF16),
            preferred_element_type=F32,
        )
        for x in range(3)
    )
    f_s[:, 0:384] = woven
    f_s[:, 384:512] = lengths
    for r in range(3):
        f_s[:, 512 + 128 * r : 640 + 128 * r] = pltpu.roll(g[r], 32, 1)
    total = ob_ref[...] + jnp.zeros((share, ob_ref.shape[1]), F32)

    def add(value, low, high):
        return jnp.dot(value.astype(BF16), ow_ref[low:high, :], preferred_element_type=F32)

    total += add(f_s[:, 0:288], 192, 480)
    total += add(f_s[:, 384:480], 480, 576)
    for r in range(3):
        total += add(f_s[:, 512 + 128 * r : 544 + 128 * r], 32 * r, 32 * r + 32)
    total += add(g[3][:, 0:96], 96, 192)
    for h in range(H):
        value = sums[pl.ds(h, share, stride=HP), :]
        total += add(value, 576 + CZ * h, 576 + CZ * h + CZ)
    out_ref[...] = total.astype(BF16)


def fetch(after, qf, out_weight, out_bias):
    others = [qf, out_bias.reshape(1, -1), out_weight]
    return pl.pallas_call(
        fetch_kernel,
        out_shape=(
            pltpu.VMEM((8, 128), F32),
            *[pltpu.VMEM(x.shape, x.dtype) for x in others[1:]],
        ),
        in_specs=[pl.BlockSpec(memory_space=pl.ANY)] + [HBM] * 3,
        out_specs=(VMEM,) * 3,
        scratch_shapes=[pltpu.VMEM(qf.shape, F32), pltpu.SemaphoreType.DMA((3,))],
        cost_estimate=pl.CostEstimate(flops=0, bytes_accessed=4 * 2**20, transcendentals=0),
        compiler_params=pltpu.CompilerParams(vmem_limit_bytes=4 * 2**20),
    )(after, *[outside(x) for x in others])


def finish(parts, others, columns):
    share = parts[0].shape[0] // HP
    sources = len(parts)
    return pl.pallas_call(
        functools.partial(finish_kernel, sources),
        out_shape=jax.ShapeDtypeStruct((share, columns), BF16),
        in_specs=[VMEM] * (sources + 3),
        out_specs=VMEM,
        scratch_shapes=[
            pltpu.VMEM((share, 896), F32),
            *[pltpu.VMEM(parts[0].shape, F32)] * sources,
        ],
        compiler_params=pltpu.CompilerParams(vmem_limit_bytes=4 * 2**20),
    )(*parts, *[inside(x) for x in others])


def body(
    query_single,
    query_frames,
    query_chain,
    key_single,
    key_frames,
    key_chain,
    key_mask,
    pair,
    w_query,
    w_key,
    pair_weight,
    point_raw,
    chain_bias,
    out_weight,
    out_bias,
):
    rows, cols = lax.axis_size("row"), lax.axis_size("col")
    turned = key_single.T
    chips = rows // 2
    near = jnp.stack(
        [turned]
        + [
            lax.ppermute(
                turned, "row", [((i + 2 * k) % rows, i) for i in range(rows)]
            )
            for k in range(1, chips)
        ]
    )
    far = lax.ppermute(near, "row", [(i, i ^ 1) for i in range(rows)])
    queries = lax.all_to_all(
        jnp.broadcast_to(query_single[None], (cols, *query_single.shape)), "col", 0, 0, tiled=True
    ).reshape(-1, query_single.shape[1])
    heads = (lane_heads()[1][None, :] == np.arange(HP)[:, None]).astype(np.float32)
    mask, wk, wq, bias = shadow(
        [
            point_raw.reshape(1, -1), chain_bias.reshape(1, -1),
            jnp.asarray(np.concatenate([depth_mask(), heads], 1)),
            key_frames, key_chain.reshape(1, -1), key_mask.reshape(1, -1), query_frames,
            query_chain.reshape(1, -1), pair_weight.T, w_key.T, w_query.T,
        ],
        pair,
    )
    send, own = attend([near, far, queries], [wk, mask, wq, bias], pair)
    come = lax.ppermute(send, "col", [(i, i ^ 1) for i in range(cols)])
    sums = join([own, come], lambda col: lax.div(col, 8), 4)
    sums = exchange(sums, 4, 8, cols)
    others = fetch(sums[0], query_frames, out_weight, out_bias)
    sums = join(sums, lambda col: lax.rem(lax.div(col, 2), 4), 4)
    parts = exchange(sums, 4, 2, cols)
    return finish(parts, others, out_weight.shape[1])


def solution(mesh):
    return jax.shard_map(
        body,
        mesh=mesh,
        in_specs=(
            P(("row", "col"), None),
            P(None, "row"),
            P("row"),
            P("col", "row"),
            P(None, "col"),
            P("col"),
            P("col"),
            P("row", "col", None),
            P(),
            P(),
            P(),
            P(),
            P(),
            P(),
            P(),
        ),
        out_specs=P(("row", "col"), None),
        check_vma=False,
    )
```

```python
import functools
import math

import jax
import jax.numpy as jnp
import numpy as np
from jax import lax
from jax.experimental import pallas as pl
from jax.experimental.pallas import tpu as pltpu
from jax.sharding import PartitionSpec as P

H = 12
C = 16
PQ = 4
PV = 8
CZ = 128
HP = 16
KD = 768
GL = 512
QB = 32
SB = 16
SHARE = 4
FAR = -1e30
F32 = jnp.float32
BF16 = jnp.bfloat16
NT = (((1,), (1,)), ((), ()))
NN = (((1,), (0,)), ((), ()))


def lane_heads():
    head = np.full((GL,), -1)
    for row in range(3):
        head[128 * row : 128 * row + 96] = np.arange(96) // PV
        head[128 * row + 96 : 128 * row + 128] = (np.arange(32) + 32 * row) // C
    head[384:480] = (np.arange(96) + 96) // C
    plain = head.copy()
    head[480:492] = np.arange(H)
    head[492:504] = np.arange(H)
    return plain, head


def depth_mask():
    column = np.arange(KD)
    head = np.full((KD,), -1)
    head[:192] = column[:192] // C
    head[192:624] = ((column[192:624] - 192) % 48) // PQ
    head[624:720] = (column[624:720] - 624) % HP
    mask = (head[None, :] == np.arange(HP)[:, None]).astype(np.float32)
    mask[:, 744] = 1.0
    mask[H:] = 0.0
    return mask


def split(x):
    hi = x.astype(BF16).astype(F32)
    return hi, x - hi


def split3(x):
    hi, rest = split(x)
    mid, rest = split(rest)
    return hi, mid, rest.astype(BF16).astype(F32)


def column_of(row, rows, per):
    shape = (rows, H)
    index = lax.broadcasted_iota(jnp.int32, shape, 0)
    lane = lax.broadcasted_iota(jnp.int32, shape, 1)
    hit = (index >= lane * per) & (index < lane * per + per)
    return jnp.sum(jnp.where(hit, row, 0.0), 1, keepdims=True)


def rotate(points, frames):
    return [
        frames[3 * x : 3 * x + 1] * points[0]
        + frames[3 * x + 1 : 3 * x + 2] * points[1]
        + frames[3 * x + 2 : 3 * x + 3] * points[2]
        + frames[9 + x : 10 + x]
        for x in range(3)
    ]


def take(ref, start, count, stride):
    return jnp.concatenate(
        [ref.at[tile][pl.ds(start, count, stride=stride), :] for tile in range(ref.shape[0])], 1
    )


def put(ref, start, value):
    for tile in range(ref.shape[0]):
        ref[tile, start : start + value.shape[0], :] = value[:, 128 * tile : 128 * tile + 128]


def gamma_of(raw):
    soft = jnp.maximum(raw, 0.0) + jnp.log1p(jnp.exp(-jnp.abs(raw)))
    return (0.5 * math.sqrt(2.0 / (9.0 * PQ))) * soft


def shadow_kernel(
    raw_hbm, cb_hbm, dm_hbm, kf_hbm, kc_hbm, km_hbm, qf_hbm, qc_hbm, pw_hbm, wk_hbm, wq_hbm,
    pair_ref, mask_ref, wk_ref, wq_ref, bias_ref,
    raw_v, cb_v, dm_v, kf_v, kc_v, km_v, qf_v, qc_v, pw_v, pw_s, pair_v, sem, pair_sem,
):
    moves = [
        (pw_hbm, pw_v), (raw_hbm, raw_v), (cb_hbm, cb_v), (dm_hbm, dm_v), (kf_hbm, kf_v),
        (kc_hbm, kc_v), (km_hbm, km_v), (qf_hbm, qf_v), (qc_hbm, qc_v), (wk_hbm, wk_ref),
        (wq_hbm, wq_ref),
    ]
    small = [pltpu.make_async_copy(*move, sem.at[i]) for i, move in enumerate(moves)]
    core = lax.rem(lax.axis_index("col"), 2)
    groups = SB // SHARE
    steps = pair_ref.shape[0] // groups
    copies = [
        pltpu.make_async_copy(
            pair_ref.at[pl.ds(groups * step, groups), 1 - core], pair_v.at[step], pair_sem.at[step]
        )
        for step in range(steps)
    ]
    for copy in small[:1] + copies[:2] + small[1:] + copies[2:]:
        copy.start()
    small[0].wait()
    pw_s[...] = jnp.zeros_like(pw_s)
    pw_s[0:H] = pw_v[...].astype(F32)
    weight = pw_s[...].astype(BF16)
    for i, copy in enumerate(copies):
        if i == len(copies) // 2:
            for other in small[1:]:
                other.wait()
            prepare_masks(raw_v, cb_v, dm_v, kf_v, kc_v, km_v, qf_v, qc_v, pw_s[...], mask_ref)
        copy.wait()
        for q in range(SB):
            row = (SB * i + q) * HP
            bias_ref[row : row + HP] = lax.dot_general(
                weight,
                pair_v[i, q // SHARE, q % SHARE],
                NT,
                preferred_element_type=F32,
            )


def prepare_masks(raw_v, cb_v, dm_v, kf_v, kc_v, km_v, qf_v, qc_v, pw, mask_ref):
    mask_ref[:, 0 : KD + GL] = dm_v[...]
    lane = lax.broadcasted_iota(jnp.int32, (HP, 128), 1)
    tail = dm_v[:, 640:768]
    for t, part in enumerate(split3(column_of(cb_v[...], HP, 1))):
        tail = jnp.where((lane >= 80 + 8 * t) & (lane < 88 + 8 * t), part, tail)
    mask_ref[:, 640:768] = tail
    at = KD + GL
    mask_ref[0:H, at : at + 256] = kf_v[...]
    mask_ref[H : H + 1, at : at + 256] = kc_v[...].astype(F32)
    mask_ref[H + 1 : H + 2, at : at + 256] = km_v[...].astype(F32)
    gamma = column_of(gamma_of(raw_v[...]), HP, 1)
    mask_ref[:, at + 256 : at + 384] = jnp.broadcast_to(gamma, (HP, 128))
    mask_ref[0:H, at + 384 : at + 512] = qf_v[...]
    mask_ref[H : H + 1, at + 384 : at + 512] = qc_v[...].astype(F32)
    mask_ref[H + 1 : H + 2, at + 384 : at + 384 + H] = raw_v[...]
    mask_ref[:, at + 512 :] = pw


def prepare_keys(info, gamma16, kt_ref, vt_ref, kpt_s, nk_s):
    frames, chain, kept = info[0:H], info[H : H + 1], info[H + 1 : H + 2]
    kt_ref[0:192] = take(kpt_s, 0, 192, 1).astype(BF16)
    points = rotate([take(kpt_s, 384 + x, 48, 3) for x in range(3)], frames)
    for x in range(3):
        hi, lo = split(points[x])
        kt_ref[192 + 48 * x : 240 + 48 * x] = hi.astype(BF16)
        kt_ref[336 + 48 * x : 384 + 48 * x] = lo.astype(BF16)
        kt_ref[480 + 48 * x : 528 + 48 * x] = hi.astype(BF16)
    put(kpt_s, 816, points[0] * points[0] + points[1] * points[1] + points[2] * points[2])
    nk_s[...] = jnp.zeros_like(nk_s)
    nk_s[0:H] = sum(take(kpt_s, 816 + p, H, PQ) for p in range(PQ))
    for t, part in enumerate(split3(-gamma16 * nk_s[...])):
        kt_ref[624 + HP * t : 640 + HP * t] = part.astype(BF16)
    kt_ref[672:720] = jnp.ones((48, kt_ref.shape[1]), BF16)
    shape = (48, kt_ref.shape[1])
    index = lax.broadcasted_iota(jnp.int32, shape, 0)
    same = (jnp.bitwise_and(index, 7).astype(F32) == chain) & (index < 24)
    away = jnp.where((index == 24) & (kept != 1.0), FAR, 0.0)
    kt_ref[720:768] = (same.astype(F32) + away).astype(BF16)
    points = rotate([take(kpt_s, 528 + x, 96, 3) for x in range(3)], frames)
    for x in range(3):
        vt_ref[128 * x : 128 * x + 96] = points[x].astype(BF16)
        vt_ref[128 * x + 96 : 128 * x + 128] = take(kpt_s, 192 + 32 * x, 32, 1).astype(BF16)
    vt_ref[384:480] = take(kpt_s, 288, 96, 1).astype(BF16)
    vt_ref[480:512] = jnp.zeros((32, vt_ref.shape[1]), BF16)


def prepare_queries(qs_ref, wq_ref, info, gamma16, qpt_s, nq_s, qft_s, qf_s):
    gamma48 = column_of(gamma_of(info[H + 1 : H + 2, 0:H]), H * PQ, PQ)
    put(qpt_s, 0, lax.dot_general(wq_ref[...], qs_ref[...], NT, preferred_element_type=F32))
    frames = info[0:H]
    qft_s[0:192] = take(qpt_s, 0, 192, 1).astype(BF16).astype(F32) * (1.0 / math.sqrt(C))
    points = rotate([take(qpt_s, 192 + x, 48, 3) for x in range(3)], frames)
    for x in range(3):
        hi, lo = split(2.0 * gamma48 * points[x])
        qft_s[192 + 48 * x : 240 + 48 * x] = hi
        qft_s[336 + 48 * x : 384 + 48 * x] = hi
        qft_s[480 + 48 * x : 528 + 48 * x] = lo
    put(qpt_s, 336, points[0] * points[0] + points[1] * points[1] + points[2] * points[2])
    nq_s[...] = jnp.zeros_like(nq_s)
    nq_s[0:H] = sum(take(qpt_s, 336 + p, H, PQ) for p in range(PQ))
    qft_s[624:672] = jnp.ones((48, qft_s.shape[1]), F32)
    for t, part in enumerate(split3(-gamma16 * nq_s[...])):
        qft_s[672 + HP * t : 688 + HP * t] = part
    shape = (48, qft_s.shape[1])
    index = lax.broadcasted_iota(jnp.int32, shape, 0)
    same = (jnp.bitwise_and(index, 7).astype(F32) == info[H : H + 1]) & (index < 24)
    qft_s[720:768] = (same | (index == 24)).astype(F32)
    qf_s[...] = qft_s[...].T


def attend_kernel(
    both_ref, next_ref, over_ref, last_ref, qs_ref, wk_ref, mask_ref, wq_ref, bias_ref, pair_ref,
    send_ref, own_ref, kpt_s, nk_s, kt_s, vt_s, v_s, w_s, z_s, o_s, ks_s,
    qpt_s, nq_s, qft_s, qf_s, feat_s, pair_v, pair_sem,
):
    core = lax.rem(lax.axis_index("col"), 2)
    groups = QB // SHARE
    steps = pair_ref.shape[0] // groups
    copies = {}
    order = [*range(steps, 2 * steps), *range(steps)]
    for index in order:
        half, step = divmod(index, steps)
        copies[index] = pltpu.make_async_copy(
            pair_ref.at[pl.ds(groups * step, groups), 1 - core if half == 0 else core],
            pair_v.at[index],
            pair_sem.at[index],
        )
        copies[index].start()
    row = lax.axis_index("row")
    pieces = (both_ref, next_ref, over_ref, last_ref)
    part = both_ref.shape[1]
    for k, ref in enumerate(pieces):
        x = lax.rem(lax.div(row, 2) + k, len(pieces))
        for z in range(2):
            own = jnp.bitwise_xor(lax.rem(row, 2), z)
            ks_s[pl.ds(pl.multiple_of((2 * x + own) * part, part), part), :] = ref[z]
    put(kpt_s, 0, jnp.dot(wk_ref[...], ks_s[...], preferred_element_type=F32))
    info = mask_ref[:, KD + GL : KD + GL + 256]
    gamma16 = mask_ref[:, KD + GL + 256 : KD + GL + 257]
    prepare_keys(info, gamma16, kt_s, vt_s, kpt_s, nk_s)
    info = mask_ref[:, KD + GL + 384 : KD + GL + 512]
    prepare_queries(qs_ref, wq_ref, info, gamma16, qpt_s, nq_s, qft_s, qf_s)
    half_groups = feat_s.shape[0] // 2
    for group in range(2 * half_groups):
        half = core if group % 2 == 0 else 1 - core
        feat_s[(1 - half) * half_groups + group // 2] = qf_s[SHARE * group : SHARE * group + SHARE]
    v_s[...] = vt_s[...].T
    rows = QB * HP
    lane = lax.broadcasted_iota(jnp.int32, (rows, 128), 1)
    gather = (
        lax.shift_right_logical(lax.broadcasted_iota(jnp.int32, (QB, rows), 1), 4)
        == lax.broadcasted_iota(jnp.int32, (QB, rows), 0)
    ).astype(BF16)

    weight = mask_ref[:, KD + GL + 512 :].astype(BF16)
    for half in range(2):
        for step in range(steps):
            start = (half * steps + step) * rows
            group = start // (SHARE * HP)
            mine = feat_s[group : group + groups].reshape(QB, 1, KD)
            spread = (mine * mask_ref[:, 0:KD][None]).reshape(rows, KD).astype(BF16)
            logits = jnp.dot(spread, kt_s[...], preferred_element_type=F32)
            if half == 0:
                bias = bias_ref[start : start + rows, :]
            else:
                index = steps + step
                copies[index].wait()
                bias = jnp.concatenate(
                    [
                        lax.dot_general(
                            weight,
                            pair_v[index, q // SHARE, q % SHARE],
                            NT,
                            preferred_element_type=F32,
                        )
                        for q in range(QB)
                    ],
                    0,
                )
            logits = math.sqrt(1.0 / 3.0) * (logits + bias)
            peak = jnp.maximum(jnp.max(logits, 1, keepdims=True), 0.1 * FAR)
            expd = jnp.exp(logits - peak)
            total = jnp.maximum(jnp.sum(expd, 1, keepdims=True), 1e-30)
            weights = (expd * (1.0 / total)).astype(BF16)
            hi, lo = split(peak + jnp.log(total))
            w_s[start : start + rows, :] = weights
            spots = jnp.dot(weights, v_s[...], preferred_element_type=F32)
            tail = jnp.where(lane < 96, spots[:, 384:512], jnp.where(lane < 108, hi, lo))
            own = [
                (
                    tile.reshape(QB, HP, 128)
                    * mask_ref[:, KD + 128 * row : KD + 128 * row + 128][None]
                )
                .reshape(rows, 128)
                .astype(BF16)
                for row, tile in enumerate(
                    [spots[:, 128 * r : 128 * r + 128] for r in range(3)] + [tail]
                )
            ]
            z_s[start // HP : start // HP + QB, :] = jnp.dot(
                gather, jnp.concatenate(own, 1), preferred_element_type=F32
            )

    for half in (1, 0):
        out_ref = (send_ref, own_ref)[half]
        for step in range(steps):
            index = half * steps + step
            start = index * rows
            if half == 0:
                copies[index].wait()
            block = pair_v.at[index]
            for i in range(QB):
                row = start + HP * i
                o_s[row : row + HP] = jnp.dot(
                    w_s[row : row + HP, :],
                    block[i // SHARE, i % SHARE],
                    preferred_element_type=F32,
                )
            for r in range(4):
                o_s[pl.ds(start + H + r, QB, stride=HP), :] = z_s[
                    start // HP : start // HP + QB, 128 * r : 128 * r + 128
                ]
            out_ref[step * rows : step * rows + rows, :] = o_s[start : start + rows, :].astype(BF16)


def lane_columns(row):
    head = lax.broadcasted_iota(jnp.int32, (128, 128), 0) - 96
    lane = lax.broadcasted_iota(jnp.int32, (128, 128), 1)
    value = lax.shift_right_logical(lane + (96 if row == 3 else 0), 4)
    if row < 3:
        value = jnp.where(
            lane < 96,
            lax.shift_right_logical(lane, 3),
            lax.shift_right_logical(jnp.maximum(lane - 96, 0) + 32 * row, 4),
        )
        return (head == value).astype(BF16)
    return ((head == value) & (lane < 96)).astype(BF16)


def merge(sources, held):
    rows = sources[0].shape[0]
    queries = rows // HP
    for source, ref in zip(sources, held, strict=True):
        ref[...] = source[...].astype(F32)
    lane = lax.broadcasted_iota(jnp.int32, (queries, 128), 1)
    stat = (lane >= 96) & (lane < 108)

    def level(ref):
        last = ref[pl.ds(HP - 1, queries, stride=HP), :]
        return jnp.where(stat, last + pltpu.roll(last, 128 - H, 1), 0.0)

    levels = [level(ref) for ref in held]
    top = functools.reduce(jnp.maximum, levels)
    shares = [jnp.exp(one - top) for one in levels]
    total = sum(shares)
    hi, lo = split(top + jnp.log(total))
    shares = [jnp.where(stat, one / total, 0.0) for one in shares]
    own = (
        lax.broadcasted_iota(jnp.int32, (HP, 128), 0) + 96
        == lax.broadcasted_iota(jnp.int32, (HP, 128), 1)
    ).astype(F32)
    mixed = [held[0][pl.ds(H + r, queries, stride=HP), :] for r in range(4)]
    base = held[0][...]
    result = base
    for share, ref in zip(shares[1:], held[1:], strict=True):
        pieces = [piece.astype(BF16) for piece in split(share)]
        for r in range(4):
            columns = lane_columns(r)
            weight = sum(jnp.dot(piece, columns, preferred_element_type=F32) for piece in pieces)
            near = held[0][pl.ds(H + r, queries, stride=HP), :]
            far = ref[pl.ds(H + r, queries, stride=HP), :]
            mixed[r] = mixed[r] + weight * (far - near)
        column = jnp.sum((share[:, None, :] * own[None]).reshape(rows, 128), 1, keepdims=True)
        result = result + column * (ref[...] - base)
    mixed[3] = jnp.where(
        stat, hi, jnp.where((lane >= 108) & (lane < 120), pltpu.roll(lo, H, 1), mixed[3])
    )
    held[0][...] = result
    for r in range(4):
        held[0][pl.ds(H + r, queries, stride=HP), :] = mixed[r]


def join_kernel(count, first, skip, *refs):
    sources, parts, held = refs[:count], refs[count + skip : -count], refs[-count:]
    rows = sources[0].shape[0]
    merge(sources, held)
    place = first(lax.axis_index("col"))
    size = rows // len(parts)
    for k, part in enumerate(parts):
        start = pl.multiple_of(lax.rem(place + k, len(parts)) * size, size)
        part[...] = held[0][pl.ds(start, size), :].astype(BF16)


def inside(x):
    return pltpu.with_memory_space_constraint(x, pltpu.VMEM)


def outside(x):
    return pltpu.with_memory_space_constraint(x, pltpu.HBM)


VMEM = pl.BlockSpec(memory_space=pltpu.VMEM)


HBM = pl.BlockSpec(memory_space=pltpu.HBM)


def shadow(others, pair):
    queries, keys = pair.shape[:2]
    pair = pair.reshape(queries // SHARE // 2, 2, SHARE, keys, CZ)
    return pl.pallas_call(
        shadow_kernel,
        out_shape=(
            pltpu.VMEM((HP, KD + GL + keys + 384), F32),
            pltpu.VMEM(others[9].shape, BF16),
            pltpu.VMEM(others[10].shape, BF16),
            pltpu.VMEM((queries * HP // 2, keys), F32),
        ),
        in_specs=[HBM] * 12,
        out_specs=(VMEM,) * 4,
        scratch_shapes=[pltpu.VMEM(x.shape, x.dtype) for x in others[:9]]
        + [
            pltpu.VMEM((HP, CZ), F32),
            pltpu.VMEM((queries // SB // 2, SB // SHARE, SHARE, keys, CZ), BF16),
            pltpu.SemaphoreType.DMA((11,)),
            pltpu.SemaphoreType.DMA((queries // SB // 2,)),
        ],
        cost_estimate=pl.CostEstimate(
            flops=queries * keys * CZ * HP, bytes_accessed=pair.size, transcendentals=0
        ),
        compiler_params=pltpu.CompilerParams(vmem_limit_bytes=16 * 2**20),
    )(*[outside(x) for x in (*others, pair)])


def attend(came, held, pair):
    queries, keys = pair.shape[:2]
    pair = pair.reshape(queries // SHARE // 2, 2, SHARE, keys, CZ)
    return pl.pallas_call(
        attend_kernel,
        out_shape=(jax.ShapeDtypeStruct((queries * HP // 2, CZ), BF16),) * 2,
        in_specs=[VMEM] * (len(held) + 5) + [HBM],
        out_specs=(VMEM,) * 2,
        scratch_shapes=[
            pltpu.VMEM((keys // 128, 896, 128), F32),
            pltpu.VMEM((HP, keys), F32),
            pltpu.VMEM((KD, keys), BF16),
            pltpu.VMEM((GL, keys), BF16),
            pltpu.VMEM((keys, GL), BF16),
            pltpu.VMEM((queries * HP, keys), BF16),
            pltpu.VMEM((queries, GL), F32),
            pltpu.VMEM((queries * HP, CZ), F32),
            pltpu.VMEM((384, keys), BF16),
            pltpu.VMEM((queries // 128, 448, 128), F32),
            pltpu.VMEM((HP, queries), F32),
            pltpu.VMEM((KD, queries), F32),
            pltpu.VMEM((queries, KD), F32),
            pltpu.VMEM((queries // SHARE, SHARE, KD), F32),
            pltpu.VMEM((queries // QB, QB // SHARE, SHARE, keys, CZ), BF16),
            pltpu.SemaphoreType.DMA((queries // QB,)),
        ],
        cost_estimate=pl.CostEstimate(
            flops=2 * queries * HP * keys * (KD + GL + CZ),
            bytes_accessed=queries * keys * CZ * 2,
            transcendentals=queries * HP * keys,
        ),
        compiler_params=pltpu.CompilerParams(vmem_limit_bytes=20 * 2**20),
    )(*came, *[inside(x) for x in held], outside(pair))


def join(sources, first, parts, after=()):
    rows, columns = sources[0].shape
    return pl.pallas_call(
        functools.partial(join_kernel, len(sources), first, len(after)),
        out_shape=(jax.ShapeDtypeStruct((rows // parts, columns), BF16),) * parts,
        in_specs=[VMEM] * (len(sources) + len(after)),
        out_specs=(VMEM,) * parts,
        scratch_shapes=[pltpu.VMEM((rows, columns), F32)] * len(sources),
        compiler_params=pltpu.CompilerParams(vmem_limit_bytes=8 * 2**20),
    )(*sources, *[inside(x) for x in after])


def exchange(parts, width, apart, count):
    def to(i, k):
        place = (i // apart) % width
        return i + ((place + k) % width - place) * apart

    return [parts[0]] + [
        lax.ppermute(parts[k], "col", [(i, to(i, k)) for i in range(count)])
        for k in range(1, width)
    ]


def fetch_kernel(after, qf_hbm, ob_hbm, ow_hbm, fr_ref, ob_ref, ow_ref, qf_v, sem):
    moves = [(qf_hbm, qf_v), (ob_hbm, ob_ref), (ow_hbm, ow_ref)]
    copies = [pltpu.make_async_copy(*move, sem.at[i]) for i, move in enumerate(moves)]
    for copy in copies:
        copy.start()
    copies[0].wait()
    first = lax.axis_index("col") * SHARE
    shape = (fr_ref.shape[0], 128)
    lane = lax.broadcasted_iota(jnp.int32, shape, 1)
    slot = lane == first + lax.broadcasted_iota(jnp.int32, shape, 0)
    frame = jnp.zeros(shape, F32)
    for j in range(12):
        value = jnp.sum(jnp.where(slot, qf_v[j : j + 1, :], 0.0), 1, keepdims=True)
        frame = jnp.where(lane == j, value, frame)
    fr_ref[...] = frame
    for copy in copies[1:]:
        copy.wait()


def finish_kernel(sources, *refs):
    parts, refs = refs[:sources], refs[sources:]
    fr_ref, ob_ref, ow_ref, out_ref, f_s, *held = refs
    share = out_ref.shape[0]
    held = [ref.at[pl.ds(0, share * HP)] for ref in held]
    merge(parts, held)
    sums = held[0]
    frame = [fr_ref[0:share, j : j + 1] for j in range(12)]
    g = [sums[pl.ds(H + r, share, stride=HP), :] for r in range(4)]
    moved = [g[x] - frame[9 + x] for x in range(3)]
    local = [
        frame[x] * moved[0] + frame[3 + x] * moved[1] + frame[6 + x] * moved[2] for x in range(3)
    ]
    lengths = jnp.sqrt(local[0] * local[0] + local[1] * local[1] + local[2] * local[2] + 1.0)
    spot = lax.broadcasted_iota(jnp.int32, (128, 384), 0)
    column = lax.broadcasted_iota(jnp.int32, (128, 384), 1)
    woven = sum(
        jnp.dot(
            local[x].astype(BF16),
            ((column == 3 * spot + x) & (spot < 96)).astype(BF16),
            preferred_element_type=F32,
        )
        for x in range(3)
    )
    f_s[:, 0:384] = woven
    f_s[:, 384:512] = lengths
    for r in range(3):
        f_s[:, 512 + 128 * r : 640 + 128 * r] = pltpu.roll(g[r], 32, 1)
    total = ob_ref[...] + jnp.zeros((share, ob_ref.shape[1]), F32)

    def add(value, low, high):
        return jnp.dot(value.astype(BF16), ow_ref[low:high, :], preferred_element_type=F32)

    total += add(f_s[:, 0:288], 192, 480)
    total += add(f_s[:, 384:480], 480, 576)
    for r in range(3):
        total += add(f_s[:, 512 + 128 * r : 544 + 128 * r], 32 * r, 32 * r + 32)
    total += add(g[3][:, 0:96], 96, 192)
    for h in range(H):
        value = sums[pl.ds(h, share, stride=HP), :]
        total += add(value, 576 + CZ * h, 576 + CZ * h + CZ)
    out_ref[...] = total.astype(BF16)


def fetch(after, qf, out_weight, out_bias):
    others = [qf, out_bias.reshape(1, -1), out_weight]
    return pl.pallas_call(
        fetch_kernel,
        out_shape=(
            pltpu.VMEM((8, 128), F32),
            *[pltpu.VMEM(x.shape, x.dtype) for x in others[1:]],
        ),
        in_specs=[pl.BlockSpec(memory_space=pl.ANY)] + [HBM] * 3,
        out_specs=(VMEM,) * 3,
        scratch_shapes=[pltpu.VMEM(qf.shape, F32), pltpu.SemaphoreType.DMA((3,))],
        cost_estimate=pl.CostEstimate(flops=0, bytes_accessed=4 * 2**20, transcendentals=0),
        compiler_params=pltpu.CompilerParams(vmem_limit_bytes=4 * 2**20),
    )(after, *[outside(x) for x in others])


def finish(parts, others, columns):
    share = parts[0].shape[0] // HP
    sources = len(parts)
    return pl.pallas_call(
        functools.partial(finish_kernel, sources),
        out_shape=jax.ShapeDtypeStruct((share, columns), BF16),
        in_specs=[VMEM] * (sources + 3),
        out_specs=VMEM,
        scratch_shapes=[
            pltpu.VMEM((share, 896), F32),
            *[pltpu.VMEM((8 * HP + HP, CZ), F32)] * sources,
        ],
        compiler_params=pltpu.CompilerParams(vmem_limit_bytes=4 * 2**20),
    )(*parts, *[inside(x) for x in others])


def body(
    query_single,
    query_frames,
    query_chain,
    key_single,
    key_frames,
    key_chain,
    key_mask,
    pair,
    w_query,
    w_key,
    pair_weight,
    point_raw,
    chain_bias,
    out_weight,
    out_bias,
):
    rows, cols = lax.axis_size("row"), lax.axis_size("col")
    turned = key_single.T
    chips = rows // 2
    both = jnp.stack([turned, lax.ppermute(turned, "row", [(i, i ^ 1) for i in range(rows)])])
    rest = [
        lax.ppermute(both, "row", [((i + 2 * k) % rows, i) for i in range(rows)])
        for k in range(1, chips)
    ]
    other = lax.ppermute(query_single, "col", [(i, i ^ 1) for i in range(cols)])
    even = lax.rem(lax.axis_index("col"), 2) == 0
    chip = jnp.concatenate(
        [jnp.where(even, query_single, other), jnp.where(even, other, query_single)], 0
    )
    queries = lax.all_to_all(
        jnp.broadcast_to(chip[None], (cols // 2, *chip.shape)),
        "col",
        0,
        0,
        axis_index_groups=[list(range(core, cols, 2)) for core in range(2)],
        tiled=True,
    ).reshape(-1, chip.shape[1])
    heads = (lane_heads()[1][None, :] == np.arange(HP)[:, None]).astype(np.float32)
    mask, wk, wq, bias = shadow(
        [
            point_raw.reshape(1, -1), chain_bias.reshape(1, -1),
            jnp.asarray(np.concatenate([depth_mask(), heads], 1)),
            key_frames, key_chain.reshape(1, -1), key_mask.reshape(1, -1), query_frames,
            query_chain.reshape(1, -1), pair_weight.T, w_key.T, w_query.T,
        ],
        pair,
    )
    send, own = attend([both, *rest, queries], [wk, mask, wq, bias], pair)
    come = lax.ppermute(send, "col", [(i, i ^ 1) for i in range(cols)])
    sums = join([own, come], lambda col: lax.div(col, 8), 4)
    sums = exchange(sums, 4, 8, cols)
    others = fetch(sums[0], query_frames, out_weight, out_bias)
    keep, send = join(sums, lambda col: lax.rem(lax.div(col, 4), 2), 2, others[:1])
    come = lax.ppermute(send, "col", [(i, i ^ 4) for i in range(cols)])
    keep, send = join([keep, come], lambda col: lax.rem(lax.div(col, 2), 2), 2)
    come = lax.ppermute(send, "col", [(i, i ^ 2) for i in range(cols)])
    parts = [keep, come]
    return finish(parts, others, out_weight.shape[1])


def solution(mesh):
    return jax.shard_map(
        body,
        mesh=mesh,
        in_specs=(
            P(("row", "col"), None),
            P(None, "row"),
            P("row"),
            P("col", "row"),
            P(None, "col"),
            P("col"),
            P("col"),
            P("row", "col", None),
            P(),
            P(),
            P(),
            P(),
            P(),
            P(),
            P(),
        ),
        out_specs=P(("row", "col"), None),
        check_vma=False,
    )
```

```python
import functools
import math

import jax
import jax.numpy as jnp
import numpy as np
from jax import lax
from jax.experimental import pallas as pl
from jax.experimental.pallas import tpu as pltpu
from jax.sharding import PartitionSpec as P

H = 12
C = 16
PQ = 4
PV = 8
CZ = 128
HP = 16
KD = 768
GL = 512
QB = 32
SB = 16
SHARE = 4
FAR = -1e30
F32 = jnp.float32
BF16 = jnp.bfloat16
NT = (((1,), (1,)), ((), ()))
NN = (((1,), (0,)), ((), ()))


def lane_heads():
    head = np.full((GL,), -1)
    for row in range(3):
        head[128 * row : 128 * row + 96] = np.arange(96) // PV
        head[128 * row + 96 : 128 * row + 128] = (np.arange(32) + 32 * row) // C
    head[384:480] = (np.arange(96) + 96) // C
    plain = head.copy()
    head[480:492] = np.arange(H)
    head[492:504] = np.arange(H)
    return plain, head


def depth_mask():
    column = np.arange(KD)
    head = np.full((KD,), -1)
    head[:192] = column[:192] // C
    head[192:624] = ((column[192:624] - 192) % 48) // PQ
    head[624:720] = (column[624:720] - 624) % HP
    mask = (head[None, :] == np.arange(HP)[:, None]).astype(np.float32)
    mask[:, 744] = 1.0
    mask[H:] = 0.0
    return mask


def split(x):
    hi = x.astype(BF16).astype(F32)
    return hi, x - hi


def split3(x):
    hi, rest = split(x)
    mid, rest = split(rest)
    return hi, mid, rest.astype(BF16).astype(F32)


def column_of(row, rows, per):
    shape = (rows, H)
    index = lax.broadcasted_iota(jnp.int32, shape, 0)
    lane = lax.broadcasted_iota(jnp.int32, shape, 1)
    hit = (index >= lane * per) & (index < lane * per + per)
    return jnp.sum(jnp.where(hit, row, 0.0), 1, keepdims=True)


def rotate(points, frames):
    return [
        frames[3 * x : 3 * x + 1] * points[0]
        + frames[3 * x + 1 : 3 * x + 2] * points[1]
        + frames[3 * x + 2 : 3 * x + 3] * points[2]
        + frames[9 + x : 10 + x]
        for x in range(3)
    ]


def take(ref, start, count, stride):
    return jnp.concatenate(
        [ref.at[tile][pl.ds(start, count, stride=stride), :] for tile in range(ref.shape[0])], 1
    )


def put(ref, start, value):
    for tile in range(ref.shape[0]):
        ref[tile, start : start + value.shape[0], :] = value[:, 128 * tile : 128 * tile + 128]


def gamma_of(raw):
    soft = jnp.maximum(raw, 0.0) + jnp.log1p(jnp.exp(-jnp.abs(raw)))
    return (0.5 * math.sqrt(2.0 / (9.0 * PQ))) * soft


def shadow_kernel(
    raw_hbm, cb_hbm, dm_hbm, kf_hbm, kc_hbm, km_hbm, qf_hbm, qc_hbm, pw_hbm, wk_hbm, wq_hbm,
    pair_ref, mask_ref, wk_ref, wq_ref, bias_ref, kept_ref,
    raw_v, cb_v, dm_v, kf_v, kc_v, km_v, qf_v, qc_v, pw_v, pw_s, pair_v, sem, pair_sem,
):
    moves = [
        (pw_hbm, pw_v), (raw_hbm, raw_v), (cb_hbm, cb_v), (dm_hbm, dm_v), (kf_hbm, kf_v),
        (kc_hbm, kc_v), (km_hbm, km_v), (qf_hbm, qf_v), (qc_hbm, qc_v), (wk_hbm, wk_ref),
        (wq_hbm, wq_ref),
    ]
    small = [pltpu.make_async_copy(*move, sem.at[i]) for i, move in enumerate(moves)]
    core = lax.rem(lax.axis_index("col"), 2)
    groups = SB // SHARE
    steps = pair_ref.shape[0] // groups
    blocks = [kept_ref] + [pair_v.at[i] for i in range(steps - 1)]
    copies = [
        pltpu.make_async_copy(
            pair_ref.at[pl.ds(groups * step, groups), 1 - core], blocks[step], pair_sem.at[step]
        )
        for step in range(steps)
    ]
    for copy in small[:1] + copies[:2] + small[1:] + copies[2:]:
        copy.start()
    small[0].wait()
    pw_s[...] = jnp.zeros_like(pw_s)
    pw_s[0:H] = pw_v[...].astype(F32)
    weight = pw_s[...].astype(BF16)
    for i, copy in enumerate(copies):
        if i == len(copies) // 2:
            for other in small[1:]:
                other.wait()
            prepare_masks(raw_v, cb_v, dm_v, kf_v, kc_v, km_v, qf_v, qc_v, pw_s[...], mask_ref)
        copy.wait()
        for q in range(SB):
            row = (SB * i + q) * HP
            bias_ref[row : row + HP] = lax.dot_general(
                weight,
                blocks[i][q // SHARE, q % SHARE],
                NT,
                preferred_element_type=F32,
            )


def prepare_masks(raw_v, cb_v, dm_v, kf_v, kc_v, km_v, qf_v, qc_v, pw, mask_ref):
    mask_ref[:, 0 : KD + GL] = dm_v[...]
    lane = lax.broadcasted_iota(jnp.int32, (HP, 128), 1)
    tail = dm_v[:, 640:768]
    for t, part in enumerate(split3(column_of(cb_v[...], HP, 1))):
        tail = jnp.where((lane >= 80 + 8 * t) & (lane < 88 + 8 * t), part, tail)
    mask_ref[:, 640:768] = tail
    at = KD + GL
    mask_ref[0:H, at : at + 256] = kf_v[...]
    mask_ref[H : H + 1, at : at + 256] = kc_v[...].astype(F32)
    mask_ref[H + 1 : H + 2, at : at + 256] = km_v[...].astype(F32)
    gamma = column_of(gamma_of(raw_v[...]), HP, 1)
    mask_ref[:, at + 256 : at + 384] = jnp.broadcast_to(gamma, (HP, 128))
    mask_ref[0:H, at + 384 : at + 512] = qf_v[...]
    mask_ref[H : H + 1, at + 384 : at + 512] = qc_v[...].astype(F32)
    mask_ref[H + 1 : H + 2, at + 384 : at + 384 + H] = raw_v[...]
    mask_ref[:, at + 512 :] = pw


def prepare_keys(info, gamma16, kt_ref, vt_ref, kpt_s, nk_s):
    frames, chain, kept = info[0:H], info[H : H + 1], info[H + 1 : H + 2]
    kt_ref[0:192] = take(kpt_s, 0, 192, 1).astype(BF16)
    points = rotate([take(kpt_s, 384 + x, 48, 3) for x in range(3)], frames)
    for x in range(3):
        hi, lo = split(points[x])
        kt_ref[192 + 48 * x : 240 + 48 * x] = hi.astype(BF16)
        kt_ref[336 + 48 * x : 384 + 48 * x] = lo.astype(BF16)
        kt_ref[480 + 48 * x : 528 + 48 * x] = hi.astype(BF16)
    put(kpt_s, 816, points[0] * points[0] + points[1] * points[1] + points[2] * points[2])
    nk_s[...] = jnp.zeros_like(nk_s)
    nk_s[0:H] = sum(take(kpt_s, 816 + p, H, PQ) for p in range(PQ))
    for t, part in enumerate(split3(-gamma16 * nk_s[...])):
        kt_ref[624 + HP * t : 640 + HP * t] = part.astype(BF16)
    kt_ref[672:720] = jnp.ones((48, kt_ref.shape[1]), BF16)
    shape = (48, kt_ref.shape[1])
    index = lax.broadcasted_iota(jnp.int32, shape, 0)
    same = (jnp.bitwise_and(index, 7).astype(F32) == chain) & (index < 24)
    away = jnp.where((index == 24) & (kept != 1.0), FAR, 0.0)
    kt_ref[720:768] = (same.astype(F32) + away).astype(BF16)
    points = rotate([take(kpt_s, 528 + x, 96, 3) for x in range(3)], frames)
    for x in range(3):
        vt_ref[128 * x : 128 * x + 96] = points[x].astype(BF16)
        vt_ref[128 * x + 96 : 128 * x + 128] = take(kpt_s, 192 + 32 * x, 32, 1).astype(BF16)
    vt_ref[384:480] = take(kpt_s, 288, 96, 1).astype(BF16)
    vt_ref[480:512] = jnp.zeros((32, vt_ref.shape[1]), BF16)


def prepare_queries(qs_ref, wq_ref, info, gamma16, qpt_s, nq_s, qft_s, qf_s):
    gamma48 = column_of(gamma_of(info[H + 1 : H + 2, 0:H]), H * PQ, PQ)
    put(qpt_s, 0, lax.dot_general(wq_ref[...], qs_ref[...], NT, preferred_element_type=F32))
    frames = info[0:H]
    qft_s[0:192] = take(qpt_s, 0, 192, 1).astype(BF16).astype(F32) * (1.0 / math.sqrt(C))
    points = rotate([take(qpt_s, 192 + x, 48, 3) for x in range(3)], frames)
    for x in range(3):
        hi, lo = split(2.0 * gamma48 * points[x])
        qft_s[192 + 48 * x : 240 + 48 * x] = hi
        qft_s[336 + 48 * x : 384 + 48 * x] = hi
        qft_s[480 + 48 * x : 528 + 48 * x] = lo
    put(qpt_s, 336, points[0] * points[0] + points[1] * points[1] + points[2] * points[2])
    nq_s[...] = jnp.zeros_like(nq_s)
    nq_s[0:H] = sum(take(qpt_s, 336 + p, H, PQ) for p in range(PQ))
    qft_s[624:672] = jnp.ones((48, qft_s.shape[1]), F32)
    for t, part in enumerate(split3(-gamma16 * nq_s[...])):
        qft_s[672 + HP * t : 688 + HP * t] = part
    shape = (48, qft_s.shape[1])
    index = lax.broadcasted_iota(jnp.int32, shape, 0)
    same = (jnp.bitwise_and(index, 7).astype(F32) == info[H : H + 1]) & (index < 24)
    qft_s[720:768] = (same | (index == 24)).astype(F32)
    qf_s[...] = qft_s[...].T


def attend_kernel(
    both_ref, next_ref, over_ref, last_ref, qs_ref, wk_ref, mask_ref, wq_ref, bias_ref, kept_ref, pair_ref,
    send_ref, own_ref, kpt_s, nk_s, kt_s, vt_s, v_s, w_s, z_s, o_s, ks_s,
    qpt_s, nq_s, qft_s, qf_s, feat_s, pair_v, pair_sem,
):
    core = lax.rem(lax.axis_index("col"), 2)
    groups = QB // SHARE
    steps = pair_ref.shape[0] // groups
    copies = {}
    order = [*range(steps, 2 * steps), *range(steps)]
    for index in order:
        half, step = divmod(index, steps)
        skip = kept_ref.shape[0] if index == 0 else 0
        copies[index] = pltpu.make_async_copy(
            pair_ref.at[
                pl.ds(groups * step + skip, groups - skip), 1 - core if half == 0 else core
            ],
            pair_v.at[index, pl.ds(skip, groups - skip)],
            pair_sem.at[index],
        )
        copies[index].start()
    row = lax.axis_index("row")
    pieces = (both_ref, next_ref, over_ref, last_ref)
    part = both_ref.shape[1]
    for k, ref in enumerate(pieces):
        x = lax.rem(lax.div(row, 2) + k, len(pieces))
        for z in range(2):
            own = jnp.bitwise_xor(lax.rem(row, 2), z)
            ks_s[pl.ds(pl.multiple_of((2 * x + own) * part, part), part), :] = ref[z]
    put(kpt_s, 0, jnp.dot(wk_ref[...], ks_s[...], preferred_element_type=F32))
    info = mask_ref[:, KD + GL : KD + GL + 256]
    gamma16 = mask_ref[:, KD + GL + 256 : KD + GL + 257]
    prepare_keys(info, gamma16, kt_s, vt_s, kpt_s, nk_s)
    info = mask_ref[:, KD + GL + 384 : KD + GL + 512]
    prepare_queries(qs_ref, wq_ref, info, gamma16, qpt_s, nq_s, qft_s, qf_s)
    half_groups = feat_s.shape[0] // 2
    for group in range(2 * half_groups):
        half = core if group % 2 == 0 else 1 - core
        feat_s[(1 - half) * half_groups + group // 2] = qf_s[SHARE * group : SHARE * group + SHARE]
    v_s[...] = vt_s[...].T
    rows = QB * HP
    lane = lax.broadcasted_iota(jnp.int32, (rows, 128), 1)
    gather = (
        lax.shift_right_logical(lax.broadcasted_iota(jnp.int32, (QB, rows), 1), 4)
        == lax.broadcasted_iota(jnp.int32, (QB, rows), 0)
    ).astype(BF16)

    weight = mask_ref[:, KD + GL + 512 :].astype(BF16)
    for half in range(2):
        for step in range(steps):
            start = (half * steps + step) * rows
            group = start // (SHARE * HP)
            mine = feat_s[group : group + groups].reshape(QB, 1, KD)
            spread = (mine * mask_ref[:, 0:KD][None]).reshape(rows, KD).astype(BF16)
            logits = jnp.dot(spread, kt_s[...], preferred_element_type=F32)
            if half == 0:
                bias = bias_ref[start : start + rows, :]
            else:
                index = steps + step
                copies[index].wait()
                bias = jnp.concatenate(
                    [
                        lax.dot_general(
                            weight,
                            pair_v[index, q // SHARE, q % SHARE],
                            NT,
                            preferred_element_type=F32,
                        )
                        for q in range(QB)
                    ],
                    0,
                )
            logits = math.sqrt(1.0 / 3.0) * (logits + bias)
            peak = jnp.maximum(jnp.max(logits, 1, keepdims=True), 0.1 * FAR)
            expd = jnp.exp(logits - peak)
            total = jnp.maximum(jnp.sum(expd, 1, keepdims=True), 1e-30)
            weights = (expd * (1.0 / total)).astype(BF16)
            hi, lo = split(peak + jnp.log(total))
            w_s[start : start + rows, :] = weights
            spots = jnp.dot(weights, v_s[...], preferred_element_type=F32)
            tail = jnp.where(lane < 96, spots[:, 384:512], jnp.where(lane < 108, hi, lo))
            own = [
                (
                    tile.reshape(QB, HP, 128)
                    * mask_ref[:, KD + 128 * row : KD + 128 * row + 128][None]
                )
                .reshape(rows, 128)
                .astype(BF16)
                for row, tile in enumerate(
                    [spots[:, 128 * r : 128 * r + 128] for r in range(3)] + [tail]
                )
            ]
            z_s[start // HP : start // HP + QB, :] = jnp.dot(
                gather, jnp.concatenate(own, 1), preferred_element_type=F32
            )

    for half in (1, 0):
        out_ref = (send_ref, own_ref)[half]
        for step in range(steps):
            index = half * steps + step
            start = index * rows
            if half == 0:
                copies[index].wait()
            block = pair_v.at[index]
            for i in range(QB):
                row = start + HP * i
                o_s[row : row + HP] = jnp.dot(
                    w_s[row : row + HP, :],
                    (kept_ref if index == 0 and i < SB else block)[i // SHARE, i % SHARE],
                    preferred_element_type=F32,
                )
            for r in range(4):
                o_s[pl.ds(start + H + r, QB, stride=HP), :] = z_s[
                    start // HP : start // HP + QB, 128 * r : 128 * r + 128
                ]
            out_ref[step * rows : step * rows + rows, :] = o_s[start : start + rows, :].astype(BF16)


def lane_columns(row):
    head = lax.broadcasted_iota(jnp.int32, (128, 128), 0) - 96
    lane = lax.broadcasted_iota(jnp.int32, (128, 128), 1)
    value = lax.shift_right_logical(lane + (96 if row == 3 else 0), 4)
    if row < 3:
        value = jnp.where(
            lane < 96,
            lax.shift_right_logical(lane, 3),
            lax.shift_right_logical(jnp.maximum(lane - 96, 0) + 32 * row, 4),
        )
        return (head == value).astype(BF16)
    return ((head == value) & (lane < 96)).astype(BF16)


def merge(sources, held):
    rows = sources[0].shape[0]
    queries = rows // HP
    for source, ref in zip(sources, held, strict=True):
        ref[...] = source[...].astype(F32)
    lane = lax.broadcasted_iota(jnp.int32, (queries, 128), 1)
    stat = (lane >= 96) & (lane < 108)

    def level(ref):
        last = ref[pl.ds(HP - 1, queries, stride=HP), :]
        return jnp.where(stat, last + pltpu.roll(last, 128 - H, 1), 0.0)

    levels = [level(ref) for ref in held]
    top = functools.reduce(jnp.maximum, levels)
    shares = [jnp.exp(one - top) for one in levels]
    total = sum(shares)
    hi, lo = split(top + jnp.log(total))
    shares = [jnp.where(stat, one / total, 0.0) for one in shares]
    own = (
        lax.broadcasted_iota(jnp.int32, (HP, 128), 0) + 96
        == lax.broadcasted_iota(jnp.int32, (HP, 128), 1)
    ).astype(F32)
    mixed = [held[0][pl.ds(H + r, queries, stride=HP), :] for r in range(4)]
    base = held[0][...]
    result = base
    for share, ref in zip(shares[1:], held[1:], strict=True):
        pieces = [piece.astype(BF16) for piece in split(share)]
        for r in range(4):
            columns = lane_columns(r)
            weight = sum(jnp.dot(piece, columns, preferred_element_type=F32) for piece in pieces)
            near = held[0][pl.ds(H + r, queries, stride=HP), :]
            far = ref[pl.ds(H + r, queries, stride=HP), :]
            mixed[r] = mixed[r] + weight * (far - near)
        column = jnp.sum((share[:, None, :] * own[None]).reshape(rows, 128), 1, keepdims=True)
        result = result + column * (ref[...] - base)
    mixed[3] = jnp.where(
        stat, hi, jnp.where((lane >= 108) & (lane < 120), pltpu.roll(lo, H, 1), mixed[3])
    )
    held[0][...] = result
    for r in range(4):
        held[0][pl.ds(H + r, queries, stride=HP), :] = mixed[r]


def join_kernel(count, first, skip, *refs):
    sources, parts, held = refs[:count], refs[count + skip : -count], refs[-count:]
    rows = sources[0].shape[0]
    merge(sources, held)
    place = first(lax.axis_index("col"))
    size = rows // len(parts)
    for k, part in enumerate(parts):
        start = pl.multiple_of(lax.rem(place + k, len(parts)) * size, size)
        part[...] = held[0][pl.ds(start, size), :].astype(BF16)


def inside(x):
    return pltpu.with_memory_space_constraint(x, pltpu.VMEM)


def outside(x):
    return pltpu.with_memory_space_constraint(x, pltpu.HBM)


VMEM = pl.BlockSpec(memory_space=pltpu.VMEM)


HBM = pl.BlockSpec(memory_space=pltpu.HBM)


def shadow(others, pair):
    queries, keys = pair.shape[:2]
    pair = pair.reshape(queries // SHARE // 2, 2, SHARE, keys, CZ)
    return pl.pallas_call(
        shadow_kernel,
        out_shape=(
            pltpu.VMEM((HP, KD + GL + keys + 384), F32),
            pltpu.VMEM(others[9].shape, BF16),
            pltpu.VMEM(others[10].shape, BF16),
            pltpu.VMEM((queries * HP // 2, keys), F32),
            pltpu.VMEM((SB // SHARE, SHARE, keys, CZ), BF16),
        ),
        in_specs=[HBM] * 12,
        out_specs=(VMEM,) * 5,
        scratch_shapes=[pltpu.VMEM(x.shape, x.dtype) for x in others[:9]]
        + [
            pltpu.VMEM((HP, CZ), F32),
            pltpu.VMEM((queries // SB // 2 - 1, SB // SHARE, SHARE, keys, CZ), BF16),
            pltpu.SemaphoreType.DMA((11,)),
            pltpu.SemaphoreType.DMA((queries // SB // 2,)),
        ],
        cost_estimate=pl.CostEstimate(
            flops=queries * keys * CZ * HP, bytes_accessed=pair.size, transcendentals=0
        ),
        compiler_params=pltpu.CompilerParams(vmem_limit_bytes=16 * 2**20),
    )(*[outside(x) for x in (*others, pair)])


def attend(came, held, pair):
    queries, keys = pair.shape[:2]
    pair = pair.reshape(queries // SHARE // 2, 2, SHARE, keys, CZ)
    return pl.pallas_call(
        attend_kernel,
        out_shape=(jax.ShapeDtypeStruct((queries * HP // 2, CZ), BF16),) * 2,
        in_specs=[VMEM] * (len(held) + 5) + [HBM],
        out_specs=(VMEM,) * 2,
        scratch_shapes=[
            pltpu.VMEM((keys // 128, 896, 128), F32),
            pltpu.VMEM((HP, keys), F32),
            pltpu.VMEM((KD, keys), BF16),
            pltpu.VMEM((GL, keys), BF16),
            pltpu.VMEM((keys, GL), BF16),
            pltpu.VMEM((queries * HP, keys), BF16),
            pltpu.VMEM((queries, GL), F32),
            pltpu.VMEM((queries * HP, CZ), F32),
            pltpu.VMEM((384, keys), BF16),
            pltpu.VMEM((queries // 128, 448, 128), F32),
            pltpu.VMEM((HP, queries), F32),
            pltpu.VMEM((KD, queries), F32),
            pltpu.VMEM((queries, KD), F32),
            pltpu.VMEM((queries // SHARE, SHARE, KD), F32),
            pltpu.VMEM((queries // QB, QB // SHARE, SHARE, keys, CZ), BF16),
            pltpu.SemaphoreType.DMA((queries // QB,)),
        ],
        cost_estimate=pl.CostEstimate(
            flops=2 * queries * HP * keys * (KD + GL + CZ),
            bytes_accessed=queries * keys * CZ * 2,
            transcendentals=queries * HP * keys,
        ),
        compiler_params=pltpu.CompilerParams(vmem_limit_bytes=20 * 2**20),
    )(*came, *[inside(x) for x in held], outside(pair))


def join(sources, first, parts, after=()):
    rows, columns = sources[0].shape
    return pl.pallas_call(
        functools.partial(join_kernel, len(sources), first, len(after)),
        out_shape=(jax.ShapeDtypeStruct((rows // parts, columns), BF16),) * parts,
        in_specs=[VMEM] * (len(sources) + len(after)),
        out_specs=(VMEM,) * parts,
        scratch_shapes=[pltpu.VMEM((rows, columns), F32)] * len(sources),
        compiler_params=pltpu.CompilerParams(vmem_limit_bytes=8 * 2**20),
    )(*sources, *[inside(x) for x in after])


def exchange(parts, width, apart, count):
    def to(i, k):
        place = (i // apart) % width
        return i + ((place + k) % width - place) * apart

    return [parts[0]] + [
        lax.ppermute(parts[k], "col", [(i, to(i, k)) for i in range(count)])
        for k in range(1, width)
    ]


def fetch_kernel(after, qf_hbm, ob_hbm, ow_hbm, fr_ref, ob_ref, ow_ref, qf_v, sem):
    moves = [(qf_hbm, qf_v), (ob_hbm, ob_ref), (ow_hbm, ow_ref)]
    copies = [pltpu.make_async_copy(*move, sem.at[i]) for i, move in enumerate(moves)]
    for copy in copies:
        copy.start()
    copies[0].wait()
    first = lax.axis_index("col") * SHARE
    shape = (fr_ref.shape[0], 128)
    lane = lax.broadcasted_iota(jnp.int32, shape, 1)
    slot = lane == first + lax.broadcasted_iota(jnp.int32, shape, 0)
    frame = jnp.zeros(shape, F32)
    for j in range(12):
        value = jnp.sum(jnp.where(slot, qf_v[j : j + 1, :], 0.0), 1, keepdims=True)
        frame = jnp.where(lane == j, value, frame)
    fr_ref[...] = frame
    for copy in copies[1:]:
        copy.wait()


def finish_kernel(sources, *refs):
    parts, refs = refs[:sources], refs[sources:]
    fr_ref, ob_ref, ow_ref, out_ref, f_s, *held = refs
    share = out_ref.shape[0]
    held = [ref.at[pl.ds(0, share * HP)] for ref in held]
    merge(parts, held)
    sums = held[0]
    frame = [fr_ref[0:share, j : j + 1] for j in range(12)]
    g = [sums[pl.ds(H + r, share, stride=HP), :] for r in range(4)]
    moved = [g[x] - frame[9 + x] for x in range(3)]
    local = [
        frame[x] * moved[0] + frame[3 + x] * moved[1] + frame[6 + x] * moved[2] for x in range(3)
    ]
    lengths = jnp.sqrt(local[0] * local[0] + local[1] * local[1] + local[2] * local[2] + 1.0)
    spot = lax.broadcasted_iota(jnp.int32, (128, 384), 0)
    column = lax.broadcasted_iota(jnp.int32, (128, 384), 1)
    woven = sum(
        jnp.dot(
            local[x].astype(BF16),
            ((column == 3 * spot + x) & (spot < 96)).astype(BF16),
            preferred_element_type=F32,
        )
        for x in range(3)
    )
    f_s[:, 0:384] = woven
    f_s[:, 384:512] = lengths
    for r in range(3):
        f_s[:, 512 + 128 * r : 640 + 128 * r] = pltpu.roll(g[r], 32, 1)
    total = ob_ref[...] + jnp.zeros((share, ob_ref.shape[1]), F32)

    def add(value, low, high):
        return jnp.dot(value.astype(BF16), ow_ref[low:high, :], preferred_element_type=F32)

    total += add(f_s[:, 0:288], 192, 480)
    total += add(f_s[:, 384:480], 480, 576)
    for r in range(3):
        total += add(f_s[:, 512 + 128 * r : 544 + 128 * r], 32 * r, 32 * r + 32)
    total += add(g[3][:, 0:96], 96, 192)
    for h in range(H):
        value = sums[pl.ds(h, share, stride=HP), :]
        total += add(value, 576 + CZ * h, 576 + CZ * h + CZ)
    out_ref[...] = total.astype(BF16)


def fetch(after, qf, out_weight, out_bias):
    others = [qf, out_bias.reshape(1, -1), out_weight]
    return pl.pallas_call(
        fetch_kernel,
        out_shape=(
            pltpu.VMEM((8, 128), F32),
            *[pltpu.VMEM(x.shape, x.dtype) for x in others[1:]],
        ),
        in_specs=[pl.BlockSpec(memory_space=pl.ANY)] + [HBM] * 3,
        out_specs=(VMEM,) * 3,
        scratch_shapes=[pltpu.VMEM(qf.shape, F32), pltpu.SemaphoreType.DMA((3,))],
        cost_estimate=pl.CostEstimate(flops=0, bytes_accessed=4 * 2**20, transcendentals=0),
        compiler_params=pltpu.CompilerParams(vmem_limit_bytes=4 * 2**20),
    )(after, *[outside(x) for x in others])


def finish(parts, others, columns):
    share = parts[0].shape[0] // HP
    sources = len(parts)
    return pl.pallas_call(
        functools.partial(finish_kernel, sources),
        out_shape=jax.ShapeDtypeStruct((share, columns), BF16),
        in_specs=[VMEM] * (sources + 3),
        out_specs=VMEM,
        scratch_shapes=[
            pltpu.VMEM((share, 896), F32),
            *[pltpu.VMEM((8 * HP + HP, CZ), F32)] * sources,
        ],
        compiler_params=pltpu.CompilerParams(vmem_limit_bytes=4 * 2**20),
    )(*parts, *[inside(x) for x in others])


def body(
    query_single,
    query_frames,
    query_chain,
    key_single,
    key_frames,
    key_chain,
    key_mask,
    pair,
    w_query,
    w_key,
    pair_weight,
    point_raw,
    chain_bias,
    out_weight,
    out_bias,
):
    rows, cols = lax.axis_size("row"), lax.axis_size("col")
    turned = key_single.T
    chips = rows // 2
    both = jnp.stack([turned, lax.ppermute(turned, "row", [(i, i ^ 1) for i in range(rows)])])
    rest = [
        lax.ppermute(both, "row", [((i + 2 * k) % rows, i) for i in range(rows)])
        for k in range(1, chips)
    ]
    other = lax.ppermute(query_single, "col", [(i, i ^ 1) for i in range(cols)])
    even = lax.rem(lax.axis_index("col"), 2) == 0
    chip = jnp.concatenate(
        [jnp.where(even, query_single, other), jnp.where(even, other, query_single)], 0
    )
    queries = lax.all_to_all(
        jnp.broadcast_to(chip[None], (cols // 2, *chip.shape)),
        "col",
        0,
        0,
        axis_index_groups=[list(range(core, cols, 2)) for core in range(2)],
        tiled=True,
    ).reshape(-1, chip.shape[1])
    heads = (lane_heads()[1][None, :] == np.arange(HP)[:, None]).astype(np.float32)
    mask, wk, wq, *held = shadow(
        [
            point_raw.reshape(1, -1), chain_bias.reshape(1, -1),
            jnp.asarray(np.concatenate([depth_mask(), heads], 1)),
            key_frames, key_chain.reshape(1, -1), key_mask.reshape(1, -1), query_frames,
            query_chain.reshape(1, -1), pair_weight.T, w_key.T, w_query.T,
        ],
        pair,
    )
    send, own = attend([both, *rest, queries], [wk, mask, wq, *held], pair)
    come = lax.ppermute(send, "col", [(i, i ^ 1) for i in range(cols)])
    sums = join([own, come], lambda col: lax.div(col, 8), 4)
    sums = exchange(sums, 4, 8, cols)
    others = fetch(sums[0], query_frames, out_weight, out_bias)
    keep, send = join(sums, lambda col: lax.rem(lax.div(col, 4), 2), 2, others[:1])
    come = lax.ppermute(send, "col", [(i, i ^ 4) for i in range(cols)])
    keep, send = join([keep, come], lambda col: lax.rem(lax.div(col, 2), 2), 2)
    come = lax.ppermute(send, "col", [(i, i ^ 2) for i in range(cols)])
    parts = [keep, come]
    return finish(parts, others, out_weight.shape[1])


def solution(mesh):
    return jax.shard_map(
        body,
        mesh=mesh,
        in_specs=(
            P(("row", "col"), None),
            P(None, "row"),
            P("row"),
            P("col", "row"),
            P(None, "col"),
            P("col"),
            P("col"),
            P("row", "col", None),
            P(),
            P(),
            P(),
            P(),
            P(),
            P(),
            P(),
        ),
        out_specs=P(("row", "col"), None),
        check_vma=False,
    )
```
